32 devices in a mesh: dp: 16 (over z, y, x), tp: 2 (over core).
Axes of the slice: x: 2, y: 2, z: 4, core: 2. Of those that a mesh axis runs over, the one named last changes fastest.
Arguments:
- block_input: bfloat16 [128, 197, 768], P('dp'), may hold values from -6 to 6
- cotangent: float32 [128, 197, 768], P('dp'), may hold values from -6 to 6
- mask_patches: int32 [128, 75], P('dp'), may hold values from 0 to 195, as said below
- owners: int32 [48], replicated, may hold values from 0 to 15, as said below
- master_slots: float32 [48, 2, 384, 384], P('dp', 'tp'), may hold values from -0.21875 to 0.21875
- left_bases: float32 [48, 2, 384, 384], P('dp', 'tp'), as said below
- right_bases: float32 [48, 2, 384, 384], P('dp', 'tp'), as said below
- first_moment: float32 [48, 2, 384, 384], P('dp', 'tp'), may hold values from -0.00390625 to 0.00390625
- second_moment: float32 [48, 2, 384, 384], P('dp', 'tp'), may hold values from 7.064254e-08 to 2.8257017e-07
- shared_vectors: float32 [2, 6, 768], replicated
- shared_first: float32 [2, 6, 768], replicated, may hold values from -0.00390625 to 0.00390625
- shared_second: float32 [2, 6, 768], replicated, may hold values from 7.064254e-08 to 2.8257017e-07
- split_vectors: float32 [2, 6, 768], P(None, None, 'tp'), may hold values from -2 to 2
- split_first: float32 [2, 6, 768], P(None, None, 'tp'), may hold values from -0.00390625 to 0.00390625
- split_second: float32 [2, 6, 768], P(None, None, 'tp'), may hold values from 7.064254e-08 to 2.8257017e-07
Outputs:
- block_output: float32 [128, 197, 768], P('dp')
- input_grad: float32 [128, 197, 768], P('dp')
- new_master: float32 [48, 2, 384, 384], P('dp', 'tp')
- new_first: float32 [48, 2, 384, 384], P('dp', 'tp')
- new_second: float32 [48, 2, 384, 384], P('dp', 'tp')
- new_shared: float32 [2, 6, 768], replicated
- new_shared_first: float32 [2, 6, 768], replicated
- new_shared_second: float32 [2, 6, 768], replicated
- new_split: float32 [2, 6, 768], P(None, None, 'tp')
- new_split_first: float32 [2, 6, 768], P(None, None, 'tp')
- new_split_second: float32 [2, 6, 768], P(None, None, 'tp')
- layer_norms: float32 [2], replicated
- global_norm: float32 [], replicated
The draws below stay inside these ranges and needn't reach their ends.
Inputs may be any that keep to these rules, and one draw needn't show every extreme that they name: `owners`: no index of dp owns more than 3 of the 48 blocks, and some index owns exactly 3. `mask_patches`: each row names 75 distinct patches. `left_bases`: each block's basis is orthogonal. `right_bases`: each block's basis is orthogonal.
All inputs are finite; a program needn't handle non-finite values.
Results may differ from the reference program's by a relative error of at most 0.022.
Values may be sent and summed in bfloat16 or wider, within the bound.
A program may use at most 320 MiB of HBM per device.

```python
import math
from functools import partial
import jax
import jax.numpy as jnp
from jax import lax

D = 768
HEADS = 12
DH = 64
FF = 3072
GRID = 14
PATCHES = 196
MASKED = 75
LAYERS = 2
IMG_DEV = 8
SEQ = 197
IMAGES = 128
BLK = 384
NBLK = 48
SLOTS = 3
N_DP = 16
N_TP = 2


def draw_mask_patches(key, part):

    def one_image(image_key):
        centers = jax.random.randint(jax.random.fold_in(image_key, 1), (3, 2), 0, GRID)
        ranking = jax.random.permutation(jax.random.fold_in(image_key, 2), PATCHES).astype(jnp.int32)
        patch_ids = jnp.arange(PATCHES, dtype=jnp.int32)
        row_pos = patch_ids // GRID
        col_pos = patch_ids % GRID
        distance = jnp.maximum(jnp.abs(row_pos[None, :] - centers[:, 0:1]), jnp.abs(col_pos[None, :] - centers[:, 1:2]))
        nearest = jnp.min(distance, axis=0)
        scores = -(nearest * PATCHES + ranking)
        chosen = lax.top_k(scores, MASKED)[1]
        return chosen.astype(jnp.int32)
    image_keys = jax.random.split(jax.random.fold_in(key, 101), IMAGES)
    return jax.vmap(one_image)(image_keys)


def draw_owners(key, part):
    shuffle = jax.random.permutation(jax.random.fold_in(key, 211), NBLK).astype(jnp.int32)
    devices = jax.random.permutation(jax.random.fold_in(key, 212), N_DP).astype(jnp.int32)
    return devices[shuffle % N_DP].astype(jnp.int32)


def orthogonal(sub_key, size_value):
    rows_key = jax.random.fold_in(sub_key, 1)
    cols_key = jax.random.fold_in(sub_key, 2)
    flips_key = jax.random.fold_in(sub_key, 3)
    row_order = jax.random.permutation(rows_key, size_value)
    col_order = jax.random.permutation(cols_key, size_value)
    sign_flips = (2 * jax.random.randint(flips_key, (2, size_value), 0, 2) - 1).astype(jnp.float32)
    frequency = jnp.arange(size_value, dtype=jnp.int32)
    phase_step = (2 * frequency[None, :] + 1) * frequency[:, None] % (4 * size_value)
    angles = phase_step.astype(jnp.float32) * (math.pi / (2 * size_value))
    row_scale = jnp.where(frequency == 0, math.sqrt(1.0 / size_value), math.sqrt(2.0 / size_value)).astype(jnp.float32)
    cosine = jnp.cos(angles) * row_scale[:, None]
    table = cosine[row_order][:, col_order]
    return sign_flips[0][:, None] * table * sign_flips[1][None, :]


def draw_bases(key, salt):
    matrix_count = N_DP * SLOTS * N_TP
    sub_keys = jax.random.split(jax.random.fold_in(key, salt), matrix_count)
    matrices = jax.vmap(partial(orthogonal, size_value=BLK))(sub_keys)
    return matrices.reshape(N_DP * SLOTS, N_TP, BLK, BLK)


def draw_left_bases(key, part):
    return draw_bases(key, 301)


def draw_right_bases(key, part):
    return draw_bases(key, 302)


def draw_shared_vectors(key, part):
    shape_all = (LAYERS, 6, D)
    normal_part = 0.3 * jax.random.normal(jax.random.fold_in(key, 401), shape_all, jnp.float32)
    gain_part = jax.random.uniform(jax.random.fold_in(key, 402), shape_all, jnp.float32, 0.6, 1.4)
    entry_ids = jnp.arange(6, dtype=jnp.int32)
    is_gain = ((entry_ids == 0) | (entry_ids == 3))[None, :, None]
    return jnp.where(is_gain, gain_part, normal_part)


def level_of(key, extent, pieces, low, high):
    def one(axis_at, blocks):
        heights = jax.random.uniform(jax.random.fold_in(jax.random.fold_in(key, 6), axis_at), (blocks,), jnp.float32, low / len(pieces), high / len(pieces))
        return jnp.repeat(jnp.exp(heights), extent[axis_at] // blocks).reshape((-1,) + (1,) * (len(extent) - axis_at - 1))

    level = one(*pieces[0])
    for cut in pieces[1:]:
        level = level * one(*cut)
    return level


def centred(own_key, extent, scale, most, shards=(), kind=jnp.bfloat16):
    values = jax.random.normal(own_key, extent, jnp.float32) * scale
    if len(shards) > 0:
        values = level_of(own_key, extent, shards, -0.22, 0.18) * values
    return jnp.clip(values, min=-most, max=most).astype(kind)


def setup_inputs(seed: int = 0) -> dict:
    streams_of = jax.random.split(jax.random.key(seed), 16)
    block_input = centred(streams_of[0], (IMAGES, SEQ, D), 1.0, 6.0, ((0, 16),))
    cotangent = centred(streams_of[1], (IMAGES, SEQ, D), 1.0, 6.0, ((0, 16),), jnp.float32)
    mask_patches = draw_mask_patches(jax.random.fold_in(streams_of[15], 71), 0)
    owners = draw_owners(jax.random.fold_in(streams_of[15], 71), 0)
    master_slots = centred(streams_of[4], (N_DP * SLOTS, N_TP, BLK, BLK), D ** -0.5, 0.21875, ((0, 16), (1, 2)), jnp.float32)
    left_bases = draw_left_bases(jax.random.fold_in(streams_of[15], 71), 0)
    right_bases = draw_right_bases(jax.random.fold_in(streams_of[15], 71), 0)
    first_moment = centred(streams_of[7], (N_DP * SLOTS, N_TP, BLK, BLK), ((LAYERS * (4 * D * D + 2 * D * FF)) ** -0.5), 0.00390625, ((0, 16), (1, 2)), jnp.float32)
    second_moment = jnp.clip(jnp.exp(math.log(2.825701699293859e-07) - 1.3862944 * jax.random.uniform(streams_of[8], (N_DP * SLOTS, N_TP, BLK, BLK), jnp.float32) ** level_of(streams_of[8], (N_DP * SLOTS, N_TP, BLK, BLK), ((0, 16), (1, 2)), -0.2, 0.2)), 7.064254248234647e-08, 2.825701699293859e-07)
    shared_vectors = draw_shared_vectors(jax.random.fold_in(streams_of[15], 71), 0)
    shared_first = centred(streams_of[10], (LAYERS, 6, D), ((LAYERS * (4 * D * D + 2 * D * FF)) ** -0.5), 0.00390625, (), jnp.float32)
    shared_second = jnp.clip(jnp.exp(jax.random.uniform(streams_of[11], (LAYERS, 6, D), jnp.float32, math.log(7.064254248234647e-08), math.log(2.825701699293859e-07))), 7.064254248234647e-08, 2.825701699293859e-07)
    split_vectors = centred(streams_of[12], (LAYERS, 2 + FF // D, D), 0.3, 2.0, ((2, 2),), jnp.float32)
    split_first = centred(streams_of[13], (LAYERS, 2 + FF // D, D), ((LAYERS * (4 * D * D + 2 * D * FF)) ** -0.5), 0.00390625, ((2, 2),), jnp.float32)
    split_second = jnp.clip(jnp.exp(math.log(2.825701699293859e-07) - 1.3862944 * jax.random.uniform(streams_of[14], (LAYERS, 2 + FF // D, D), jnp.float32) ** level_of(streams_of[14], (LAYERS, 2 + FF // D, D), ((2, 2),), -0.2, 0.2)), 7.064254248234647e-08, 2.825701699293859e-07)
    return dict(block_input=block_input, cotangent=cotangent, mask_patches=mask_patches, owners=owners, master_slots=master_slots, left_bases=left_bases, right_bases=right_bases, first_moment=first_moment, second_moment=second_moment, shared_vectors=shared_vectors, shared_first=shared_first, shared_second=shared_second, split_vectors=split_vectors, split_first=split_first, split_second=split_second)


HIGHEST = lax.Precision.HIGHEST
CLIP_NORM = 1.0
MOMENT_DECAY = 0.5
CORRECTION = 0.9375
ADAM_EPSILON = 1e-08
WEIGHT_DECAY = 0.05
LAYER_EPSILON = 1e-06
VECTOR_RATE = 0.2

@jax.custom_vjp
def low(v):
    return lax.optimization_barrier(v.astype(jnp.bfloat16)).astype(jnp.float32)

@jax.custom_vjp
def low_back(v):
    return v

def low_keep(v):
    return (low(v), None)

def low_pass(kept, grad):
    return (grad,)

def back_keep(v):
    return (v, None)

def back_low(kept, grad):
    return (low(grad),)
low.defvjp(low_keep, low_pass)
low_back.defvjp(back_keep, back_low)

def layer_norm(stream, gain, bias):
    center = lax.optimization_barrier(jnp.mean(stream, axis=-1, keepdims=True))
    spread = stream - center
    second = lax.optimization_barrier(jnp.mean(spread * spread, axis=-1, keepdims=True))
    return spread * lax.rsqrt(second + LAYER_EPSILON) * gain + bias

def row_mask(mask_patches, seq_length):
    row_ids = jnp.arange(seq_length, dtype=jnp.int32)
    hits = mask_patches[:, :, None] + 1 == row_ids[None, None, :]
    return jnp.any(hits, axis=1).astype(jnp.float32)

def positions(owners, slot_count):
    block_ids = jnp.arange(owners.shape[0], dtype=jnp.int32)
    same_owner = owners[None, :] == owners[:, None]
    earlier = block_ids[None, :] < block_ids[:, None]
    ranking = lax.optimization_barrier(jnp.sum((same_owner & earlier).astype(jnp.int32), axis=1))
    return (owners * slot_count + ranking).astype(jnp.int32)

def to_blocks(w_project, w_output, w_upward, w_downward):
    layer_count = w_project.shape[0]
    model_width = w_project.shape[1]
    block_size = w_project.shape[3]
    piece_count = model_width // block_size
    mlp_ratio = w_upward.shape[2]
    first_part = w_project.reshape(layer_count, piece_count, block_size, 3, block_size).transpose(0, 1, 3, 2, 4).reshape(layer_count, piece_count * 3, block_size, block_size)
    second_part = w_output.reshape(layer_count, block_size, piece_count, block_size).transpose(0, 2, 1, 3)
    third_part = w_upward.reshape(layer_count, piece_count, block_size, mlp_ratio, block_size).transpose(0, 1, 3, 2, 4).reshape(layer_count, piece_count * mlp_ratio, block_size, block_size)
    fourth_part = w_downward.reshape(layer_count, mlp_ratio, block_size, piece_count, block_size).transpose(0, 1, 3, 2, 4).reshape(layer_count, mlp_ratio * piece_count, block_size, block_size)
    joined = jnp.concatenate([first_part, second_part, third_part, fourth_part], axis=1)
    return joined.reshape(-1, block_size, block_size)

def from_blocks(blocks, layer_count, piece_count, mlp_ratio):
    block_size = blocks.shape[-1]
    per_layer = piece_count * (4 + 2 * mlp_ratio)
    grouped = blocks.reshape(layer_count, per_layer, block_size, block_size)
    start_out = 3 * piece_count
    start_up = 4 * piece_count
    start_down = start_up + piece_count * mlp_ratio
    w_project = grouped[:, :start_out].reshape(layer_count, piece_count, 3, block_size, block_size).transpose(0, 1, 3, 2, 4).reshape(layer_count, piece_count * block_size, 3, block_size)
    w_output = grouped[:, start_out:start_up].transpose(0, 2, 1, 3).reshape(layer_count, block_size, piece_count * block_size)
    w_upward = grouped[:, start_up:start_down].reshape(layer_count, piece_count, mlp_ratio, block_size, block_size).transpose(0, 1, 3, 2, 4).reshape(layer_count, piece_count * block_size, mlp_ratio, block_size)
    w_downward = grouped[:, start_down:].reshape(layer_count, mlp_ratio, piece_count, block_size, block_size).transpose(0, 1, 3, 2, 4).reshape(layer_count, mlp_ratio, block_size, piece_count * block_size)
    return (w_project, w_output, w_upward, w_downward)

def rotated_update(gradient, weight, first_state, second_state, left_basis, right_basis, step_rate):
    half_turn = jnp.einsum('nki,nkl->nil', left_basis, gradient, precision=HIGHEST)
    turned = jnp.einsum('nil,nlj->nij', half_turn, right_basis, precision=HIGHEST)
    first_new = MOMENT_DECAY * first_state + (1.0 - MOMENT_DECAY) * turned
    second_new = MOMENT_DECAY * second_state + (1.0 - MOMENT_DECAY) * turned * turned
    stepped = first_new / CORRECTION / (jnp.sqrt(second_new / CORRECTION) + ADAM_EPSILON)
    half_back = jnp.einsum('nik,nkl->nil', left_basis, stepped, precision=HIGHEST)
    rotated_back = jnp.einsum('nil,njl->nij', half_back, right_basis, precision=HIGHEST)
    return (weight - step_rate * (rotated_back + WEIGHT_DECAY * weight), first_new, second_new)

def plain_update(gradient, weight, first_state, second_state, step_rate):
    first_new = MOMENT_DECAY * first_state + (1.0 - MOMENT_DECAY) * gradient
    second_new = MOMENT_DECAY * second_state + (1.0 - MOMENT_DECAY) * gradient * gradient
    stepped = first_new / CORRECTION / (jnp.sqrt(second_new / CORRECTION) + ADAM_EPSILON)
    return (weight - step_rate * stepped, first_new, second_new)

def forward(stream, w_project, w_output, w_upward, w_downward, shared, splitted):
    image_count = stream.shape[0]
    seq_length = stream.shape[1]
    model_width = stream.shape[2]
    scale = 1.0 / math.sqrt(DH)
    for layer_index in range(LAYERS):
        gain_one = shared[layer_index, 0]
        bias_one = shared[layer_index, 1]
        out_bias = shared[layer_index, 2]
        gain_two = shared[layer_index, 3]
        bias_two = shared[layer_index, 4]
        down_bias = shared[layer_index, 5]
        query_bias = splitted[layer_index, 0]
        value_bias = splitted[layer_index, 1]
        up_bias = splitted[layer_index, 2:]
        normed = low(layer_norm(stream, gain_one, bias_one))
        project = jnp.einsum('gsd,dje->gsje', normed, w_project[layer_index], precision=HIGHEST)
        query = low(low_back((project[:, :, 0] + query_bias) * scale)).reshape(image_count, seq_length, HEADS, DH)
        keyset = low(low_back(project[:, :, 1])).reshape(image_count, seq_length, HEADS, DH)
        valueset = low(low_back(project[:, :, 2] + value_bias)).reshape(image_count, seq_length, HEADS, DH)
        scores = low_back(jnp.einsum('gqhe,gkhe->ghqk', query, keyset, precision=HIGHEST))
        highest = lax.optimization_barrier(jnp.max(scores, axis=-1, keepdims=True))
        powered = jnp.exp(scores - highest)
        weights = low(powered / lax.optimization_barrier(jnp.sum(powered, axis=-1, keepdims=True)))
        mixed = jnp.einsum('ghqk,gkhe->gqhe', weights, valueset, precision=HIGHEST)
        mixed = low(low_back(mixed)).reshape(image_count, seq_length, model_width)
        branch = low_back(jnp.einsum('gse,ed->gsd', mixed, w_output[layer_index], precision=HIGHEST))
        middle = stream + branch + out_bias
        normed_two = low(layer_norm(middle, gain_two, bias_two))
        hidden = low_back(jnp.einsum('gsd,dje->gsje', normed_two, w_upward[layer_index], precision=HIGHEST) + up_bias)
        active = low(jax.nn.gelu(hidden, approximate=False))
        branch_two = low_back(jnp.einsum('gsje,jed->gsd', active, w_downward[layer_index], precision=HIGHEST))
        stream = middle + branch_two + down_bias
    return stream

def reference(block_input, cotangent, mask_patches, owners, master_slots, left_bases, right_bases, first_moment, second_moment, shared_vectors, shared_first, shared_second, split_vectors, split_first, split_second):
    slot_index = positions(owners, SLOTS)
    piece_count = D // BLK
    mlp_ratio = FF // D
    rounded = lax.optimization_barrier(master_slots.astype(jnp.bfloat16)).astype(jnp.float32)
    local_sets = [from_blocks(rounded[slot_index, tp_rank], LAYERS, piece_count, mlp_ratio) for tp_rank in range(N_TP)]
    w_project = jnp.concatenate([entry[0] for entry in local_sets], axis=3)
    w_output = jnp.concatenate([entry[1] for entry in local_sets], axis=1)
    w_upward = jnp.concatenate([entry[2] for entry in local_sets], axis=3)
    w_downward = jnp.concatenate([entry[3] for entry in local_sets], axis=2)
    weights = (w_project, w_output, w_upward, w_downward, shared_vectors, split_vectors)
    inputs = (block_input.astype(jnp.float32).reshape(N_DP, IMG_DEV, SEQ, D), cotangent.reshape(N_DP, IMG_DEV, SEQ, D), mask_patches.reshape(N_DP, IMG_DEV, MASKED))

    def group_step(totals, group_data):
        images, back_seed, marked = group_data
        output, pullback = jax.vjp(forward, images, *weights)
        grads = pullback(back_seed * row_mask(marked, SEQ)[:, :, None])
        totals = jax.tree.map(jnp.add, totals, tuple(grads[1:]))
        return (totals, (output, grads[0]))
    zeros = tuple((jnp.zeros_like(member) for member in weights))
    totals, (outputs, input_grads) = lax.scan(group_step, zeros, inputs)
    grad_project, grad_output, grad_upward, grad_downward, grad_shared, grad_split = totals
    squares = lax.optimization_barrier(jnp.sum(grad_project * grad_project, axis=(1, 2, 3))) + lax.optimization_barrier(jnp.sum(grad_output * grad_output, axis=(1, 2))) + lax.optimization_barrier(jnp.sum(grad_upward * grad_upward, axis=(1, 2, 3))) + lax.optimization_barrier(jnp.sum(grad_downward * grad_downward, axis=(1, 2, 3))) + lax.optimization_barrier(jnp.sum(grad_shared * grad_shared, axis=(1, 2))) + lax.optimization_barrier(jnp.sum(grad_split * grad_split, axis=(1, 2)))
    layer_norms = jnp.sqrt(squares)
    global_norm = jnp.sqrt(jnp.sum(squares))
    factor = CLIP_NORM / jnp.maximum(global_norm, CLIP_NORM)
    step_rate = 0.5 / math.sqrt(D)
    new_master = master_slots
    new_first = first_moment
    new_second = second_moment
    for tp_rank in range(N_TP):
        low_edge = tp_rank * BLK
        high_edge = low_edge + BLK
        grad_blocks = to_blocks(grad_project[..., low_edge:high_edge], grad_output[:, low_edge:high_edge], grad_upward[..., low_edge:high_edge], grad_downward[:, :, low_edge:high_edge]) * factor
        weight, first_state, second_state = rotated_update(grad_blocks, master_slots[slot_index, tp_rank], first_moment[slot_index, tp_rank], second_moment[slot_index, tp_rank], left_bases[slot_index, tp_rank], right_bases[slot_index, tp_rank], step_rate)
        new_master = new_master.at[slot_index, tp_rank].set(weight)
        new_first = new_first.at[slot_index, tp_rank].set(first_state)
        new_second = new_second.at[slot_index, tp_rank].set(second_state)
    new_shared, new_shared_first, new_shared_second = plain_update(grad_shared * factor, shared_vectors, shared_first, shared_second, VECTOR_RATE)
    new_split, new_split_first, new_split_second = plain_update(grad_split * factor, split_vectors, split_first, split_second, VECTOR_RATE)
    return (outputs.reshape(IMAGES, SEQ, D), input_grads.reshape(IMAGES, SEQ, D), new_master, new_first, new_second, new_shared, new_shared_first, new_shared_second, new_split, new_split_first, new_split_second, layer_norms, global_norm)
```

```python
import functools
import math

import jax
import jax.numpy as jnp
from jax import lax
from jax.experimental import pallas as pl
from jax.experimental.pallas import tpu as pltpu
from jax.sharding import PartitionSpec as P

DH = 64
GROUP = 4
LANES = GROUP * DH
CLIP_NORM = 1.0
MOMENT_DECAY = 0.5
CORRECTION = 0.9375
ADAM_EPSILON = 1e-08
WEIGHT_DECAY = 0.05
LAYER_EPSILON = 1e-06
VECTOR_RATE = 0.2
VMEM_LIMIT = 60 * 1024 * 1024
F32 = jnp.float32
BF16 = jnp.bfloat16


def nn(a, b):
    return lax.dot_general(a, b, (((1,), (0,)), ((), ())), preferred_element_type=F32)


def nt(a, b):
    return lax.dot_general(a, b, (((1,), (1,)), ((), ())), preferred_element_type=F32)


def tn(a, b):
    return lax.dot_general(a, b, (((0,), (0,)), ((), ())), preferred_element_type=F32)


def round_up(number, step):
    return (number + step - 1) // step * step


def positions(owners, slot_count):
    block_ids = jnp.arange(owners.shape[0], dtype=jnp.int32)
    same_owner = owners[None, :] == owners[:, None]
    earlier = block_ids[None, :] < block_ids[:, None]
    ranking = jnp.sum((same_owner & earlier).astype(jnp.int32), axis=1)
    return owners * slot_count + ranking


def normalized(v):
    center = jnp.mean(v, axis=-1, keepdims=True)
    spread = v - center
    second = jnp.mean(spread * spread, axis=-1, keepdims=True)
    inverse = lax.rsqrt(second + LAYER_EPSILON)
    return spread * inverse, inverse


def norm_back(grad, unit, inverse, gain):
    scaled = grad * gain
    first = jnp.mean(scaled, axis=-1, keepdims=True)
    second = jnp.mean(scaled * unit, axis=-1, keepdims=True)
    return inverse * (scaled - first - unit * second)


def gelu_pair(u):
    bell = jnp.exp(u * u * -0.5)
    below = 1.0 + jnp.abs(u) * (0.3275911 * math.sqrt(0.5))
    t = pl.reciprocal(below, approx=True)
    t = t * (2.0 - below * t)
    poly = 0.5 * 1.061405429
    for factor in (-1.453152027, 1.421413741, -0.284496736, 0.254829592):
        poly = poly * t + 0.5 * factor
    tail = poly * t * bell
    mass = jnp.where(u >= 0, 1.0 - tail, tail)
    return u * mass, mass + u * bell * (1.0 / math.sqrt(2.0 * math.pi))


def weight_copies(meta, layer, blocks, wp, wo, wu, wd, sems):
    side = blocks.shape[-1]
    width = wo.shape[0]
    pieces = width // side
    ratio = wd.shape[0] // width
    per_layer = pieces * (4 + 2 * ratio)
    base = layer * per_layer
    jobs = [[], [], [], []]

    def add(kind, target, b, row, col):
        for t in range(blocks.shape[0]):
            r, c = row(t), col(t)
            jobs[kind].append(
                pltpu.make_async_copy(
                    blocks.at[t, meta[base + b]],
                    target.at[pl.ds(r, side), pl.ds(c, side)],
                    sems.at[kind],
                )
            )

    for r in range(pieces):
        for p in range(3):
            add(0, wp, r * 3 + p, lambda t: r * side, lambda t: p * width + t * side)
    for c in range(pieces):
        add(1, wo, 3 * pieces + c, lambda t: t * side, lambda t: c * side)
    for r in range(pieces):
        for j in range(ratio):
            add(
                2, wu, 4 * pieces + r * ratio + j, lambda t: r * side, lambda t: j * width + t * side
            )
    for j in range(ratio):
        for c in range(pieces):
            add(
                3,
                wd,
                (4 + ratio) * pieces + j * pieces + c,
                lambda t: j * width + t * side,
                lambda t: c * side,
            )
    return jobs


def start_weights(jobs, order):
    @pl.when(pl.program_id(0) == 0)
    def _():
        for kind in order:
            for job in jobs[kind]:
                job.start()


def wait_weights(target, sem):
    @pl.when(pl.program_id(0) == 0)
    def _():
        pltpu.make_async_copy(target, target, sem).wait()


def head_masks():
    lane = lax.broadcasted_iota(jnp.int32, (1, LANES), 1)
    return [(lane // DH) == h for h in range(GROUP)]


def spread_heads(masks, value):
    zero = jnp.zeros((), value.dtype)
    return jnp.concatenate([jnp.where(m, value, zero) for m in masks], axis=0)


def forward_kernel(
    layer, seq, rows, keys, meta, x_ref, shared_ref, split_ref, blocks,
    a_ref, q_ref, k_ref, v_ref, p_ref, mixed_ref, h_ref, c_ref, act_ref, slope_ref, y_ref,
    wp, wo, wu, wd, xs, sems,
):
    width = wo.shape[0]
    ratio = wd.shape[0] // width
    groups = width // LANES
    jobs = weight_copies(meta, layer, blocks, wp, wo, wu, wd, sems)
    start_weights(jobs, (0, 1, 2, 3))
    if x_ref.shape[1] == seq:
        tail = seq // 16 * 16
        xs[tail:rows, :] = jnp.zeros((rows - tail, width), F32)
        xs[0:seq, :] = x_ref[0].astype(F32)
        x = xs[...]
    else:
        x = x_ref[0]
    unit, _ = normalized(x)
    a = (unit * shared_ref[0:1, :] + shared_ref[1:2, :]).astype(BF16)
    a_ref[0] = a
    wait_weights(wp, sems.at[0])
    q = ((nn(a, wp[:, 0:width]) + split_ref[0:1, :]) * (1.0 / math.sqrt(DH))).astype(BF16)
    q_ref[0] = q
    k_ref[0, 0:rows, :] = nn(a, wp[:, width : 2 * width]).astype(BF16)
    v_ref[0, 0:rows, :] = (nn(a, wp[:, 2 * width :]) + split_ref[1:2, :]).astype(BF16)
    k_ref[0, rows:keys, :] = jnp.zeros((keys - rows, width), BF16)
    v_ref[0, rows:keys, :] = jnp.zeros((keys - rows, width), BF16)
    masks = head_masks()
    real = lax.broadcasted_iota(jnp.int32, (1, keys), 1) < seq
    for g in range(groups):
        cols = slice(g * LANES, (g + 1) * LANES)
        qs = spread_heads(masks, q[:, cols])
        scores = nt(qs, k_ref[0, :, cols])
        scores = jnp.where(real, scores, -1e30)
        top = jnp.max(scores, axis=-1, keepdims=True)
        power = jnp.exp(scores - top)
        total = jnp.sum(power, axis=-1, keepdims=True)
        probs = (power * (1.0 / total)).astype(BF16)
        p_ref[0, g * GROUP * rows : (g + 1) * GROUP * rows, :] = probs
        v4 = v_ref[0, :, cols]
        mix = None
        for h in range(GROUP):
            part = nn(
                probs[h * rows : (h + 1) * rows, :], jnp.where(masks[h], v4, jnp.zeros((), BF16))
            )
            mix = part if mix is None else mix + part
        mixed_ref[0, :, cols] = mix.astype(BF16)
    wait_weights(wo, sems.at[1])
    h = x + nn(mixed_ref[0], wo[...]) + shared_ref[2:3, :]
    h_ref[0] = h
    unit, _ = normalized(h)
    c = (unit * shared_ref[3:4, :] + shared_ref[4:5, :]).astype(BF16)
    c_ref[0] = c
    wait_weights(wu, sems.at[2])
    wait_weights(wd, sems.at[3])
    y = h + shared_ref[5:6, :]
    for j in range(ratio):
        cols = slice(j * width, (j + 1) * width)
        u = nn(c, wu[:, cols]) + split_ref[2 + j : 3 + j, :]
        act, slope = gelu_pair(u)
        act = act.astype(BF16)
        act_ref[0, :, cols] = act
        slope_ref[0, :, cols] = slope.astype(BF16)
        y = y + nn(act, wd[cols, :])
    y_ref[0] = y[0 : y_ref.shape[1], :]


def backward_kernel(
    layer, seq, rows, keys, last, meta, dy_ref, hits_ref, x_ref, h_ref, slope_ref, p_ref, q_ref,
    k_ref, v_ref, shared_ref, blocks,
    dyr_ref, du_ref, dhr_ref, dqkv_ref, vec_ref, dx_ref,
    wp, wo, wu, wd, xs, sems,
):
    width = wo.shape[0]
    ratio = wd.shape[0] // width
    groups = width // LANES
    jobs = weight_copies(meta, layer, blocks, wp, wo, wu, wd, sems)
    start_weights(jobs, (3, 2, 1, 0))

    @pl.when(pl.program_id(0) == 0)
    def _():
        vec_ref[...] = jnp.zeros_like(vec_ref)

    def collect(row, value):
        vec_ref[row : row + 1, :] += jnp.sum(value, axis=0, keepdims=True)

    tail = seq // 16 * 16
    if last:
        wanted = lax.broadcasted_iota(jnp.int32, (rows, 1), 0)
        hit = jnp.max(jnp.where(hits_ref[0] + 1 == wanted, 1.0, 0.0), axis=-1, keepdims=True)
        xs[tail:rows, :] = jnp.zeros((rows - tail, width), F32)
        xs[0:seq, :] = dy_ref[0]
        dy = xs[...] * hit
    else:
        dy = dy_ref[0]
    collect(5, dy)
    dyr = dy.astype(BF16)
    dyr_ref[0] = dyr
    wait_weights(wd, sems.at[3])
    wait_weights(wu, sems.at[2])
    dc = None
    for j in range(ratio):
        cols = slice(j * width, (j + 1) * width)
        du = (nt(dyr, wd[cols, :]) * slope_ref[0, :, cols].astype(F32)).astype(BF16)
        du_ref[0, :, cols] = du
        collect(8 + j, du.astype(F32))
        part = nt(du, wu[:, cols])
        dc = part if dc is None else dc + part
    unit, inverse = normalized(h_ref[0])
    collect(3, dc * unit)
    collect(4, dc)
    dh = dy + norm_back(dc, unit, inverse, shared_ref[3:4, :])
    collect(2, dh)
    dhr = dh.astype(BF16)
    dhr_ref[0] = dhr
    wait_weights(wo, sems.at[1])
    dmixed = nt(dhr, wo[...]).astype(BF16)
    masks = head_masks()
    zero = jnp.zeros((), BF16)
    for g in range(groups):
        cols = slice(g * LANES, (g + 1) * LANES)
        dm = spread_heads(masks, dmixed[:, cols])
        probs = p_ref[0, g * GROUP * rows : (g + 1) * GROUP * rows, :]
        k4 = k_ref[0, :, cols]
        dprobs = nt(dm, v_ref[0, :, cols])
        wide = probs.astype(F32)
        both = wide * dprobs
        ds = (both - wide * jnp.sum(both, axis=-1, keepdims=True)).astype(BF16)
        dv = tn(probs, dm)[0:rows, :].astype(BF16)
        dk = tn(ds, spread_heads(masks, q_ref[0, :, cols]))[0:rows, :].astype(BF16)
        dq = None
        for h in range(GROUP):
            part = nn(ds[h * rows : (h + 1) * rows, :], jnp.where(masks[h], k4, zero))
            dq = part if dq is None else dq + part
        dq = (dq.astype(BF16).astype(F32) * (1.0 / math.sqrt(DH))).astype(BF16)
        dqkv_ref[0, :, cols] = dq
        dqkv_ref[0, :, width + g * LANES : width + (g + 1) * LANES] = dk
        dqkv_ref[0, :, 2 * width + g * LANES : 2 * width + (g + 1) * LANES] = dv
    collect(6, dqkv_ref[0, :, 0:width].astype(F32))
    collect(7, dqkv_ref[0, :, 2 * width :].astype(F32))
    wait_weights(wp, sems.at[0])
    da = nt(dqkv_ref[0, :, 0:width], wp[:, 0:width])
    da = da + nt(dqkv_ref[0, :, width : 2 * width], wp[:, width : 2 * width])
    da = da + nt(dqkv_ref[0, :, 2 * width :], wp[:, 2 * width :])
    if x_ref.shape[1] == seq:
        xs[tail:rows, :] = jnp.zeros((rows - tail, width), F32)
        xs[0:seq, :] = x_ref[0].astype(F32)
        x = xs[...]
    else:
        x = x_ref[0]
    unit, inverse = normalized(x)
    collect(0, da * unit)
    collect(1, da)
    dx = dh + norm_back(da, unit, inverse, shared_ref[0:1, :])
    dx_ref[0] = dx[0 : dx_ref.shape[1], :]


def gradient_kernel(
    pieces, ratio, meta, a_ref, dqkv_ref, mixed_ref, dhr_ref, c_ref, du_ref, act_ref, dyr_ref,
    *rest,
):
    out_ref, turned, wide = rest[-3:]
    side = out_ref.shape[-1]
    step = pl.program_id(0)
    start_out = 3 * pieces
    start_up = 4 * pieces
    start_down = start_up + pieces * ratio

    def by_columns(lhs_ref, rhs_ref, first):
        @pl.when(first)
        def _():
            turned[...] = lhs_ref[...].T

        res = nn(turned[...], rhs_ref[...])
        for t in range(out_ref.shape[0]):
            out_ref[t, 0] = res[:, t * side : (t + 1) * side].astype(BF16)

    def by_rows(lhs_ref, rhs_ref, first):
        @pl.when(first)
        def _():
            wide[...] = lhs_ref[...].T

        res = nn(wide[...], rhs_ref[...])
        for t in range(out_ref.shape[0]):
            out_ref[t, 0] = res[t * side : (t + 1) * side, :].astype(BF16)

    @pl.when(step < start_out)
    def _():
        by_columns(a_ref, dqkv_ref, step % 3 == 0)

    @pl.when((step >= start_out) & (step < start_up))
    def _():
        by_rows(mixed_ref, dhr_ref, step == start_out)

    @pl.when((step >= start_up) & (step < start_down))
    def _():
        by_columns(c_ref, du_ref, (step - start_up) % ratio == 0)

    @pl.when(step >= start_down)
    def _():
        by_rows(act_ref, dyr_ref, (step - start_down) % pieces == 0)


def adam_kernel(live_ref, factor_ref, g_ref, w_ref, l_ref, r_ref, m_ref, s_ref, w_out, m_out, s_out):
    step_rate = factor_ref[1]
    high = lax.Precision.HIGHEST

    def dot(a, b, dims):
        return lax.dot_general(a, b, (dims, ((), ())), precision=high, preferred_element_type=F32)

    slot = pl.program_id(0)
    alive = live_ref[slot] > 0
    weight = w_ref[0, 0]
    left = l_ref[0, 0]
    right = r_ref[0, 0]
    gradient = g_ref[0].astype(F32) * factor_ref[0]
    turned = dot(dot(left, gradient, ((0,), (0,))), right, ((1,), (0,)))
    first = MOMENT_DECAY * m_ref[0, 0] + (1.0 - MOMENT_DECAY) * turned
    second = MOMENT_DECAY * s_ref[0, 0] + (1.0 - MOMENT_DECAY) * turned * turned
    stepped = first / CORRECTION / (jnp.sqrt(second / CORRECTION) + ADAM_EPSILON)
    back = dot(dot(left, stepped, ((1,), (0,))), right, ((1,), (1,)))
    w_out[0, 0] = jnp.where(alive, weight - step_rate * (back + WEIGHT_DECAY * weight), weight)
    m_out[0, 0] = jnp.where(alive, first, m_ref[0, 0])
    s_out[0, 0] = jnp.where(alive, second, s_ref[0, 0])


def plain_update(gradient, weight, first_state, second_state, step_rate):
    first_new = MOMENT_DECAY * first_state + (1.0 - MOMENT_DECAY) * gradient
    second_new = MOMENT_DECAY * second_state + (1.0 - MOMENT_DECAY) * gradient * gradient
    stepped = first_new / CORRECTION / (jnp.sqrt(second_new / CORRECTION) + ADAM_EPSILON)
    return (weight - step_rate * stepped, first_new, second_new)


def image_spec(shape):
    return pl.BlockSpec((1,) + tuple(shape[1:]), lambda i, meta: (i, 0, 0))


def shifted_spec(shape, count, place):
    return pl.BlockSpec((1,) + tuple(shape[1:]), lambda i, meta: (meta[place] * count + i, 0, 0))


def whole_spec(shape):
    return pl.BlockSpec(tuple(shape), lambda i, meta: (0,) * len(shape))


def params():
    return pltpu.CompilerParams(vmem_limit_bytes=VMEM_LIMIT, dimension_semantics=("arbitrary",))


def weight_scratch(width, ratio, rows):
    return [
        pltpu.VMEM((width, 3 * width), BF16),
        pltpu.VMEM((width, width), BF16),
        pltpu.VMEM((width, ratio * width), BF16),
        pltpu.VMEM((ratio * width, width), BF16),
        pltpu.VMEM((rows, width), F32),
        pltpu.SemaphoreType.DMA((4,)),
    ]


def forward_layer(layer, last, count, seq, rows, keys, meta, place, stream, shared, split, blocks):
    width = shared.shape[1]
    ratio = split.shape[0] - 2
    heads = width // DH
    sd = jax.ShapeDtypeStruct
    outs = [
        sd((count, rows, width), BF16),
        sd((count, rows, width), BF16),
        sd((count, keys, width), BF16),
        sd((count, keys, width), BF16),
        sd((count, heads * rows, keys), BF16),
        sd((count, rows, width), BF16),
        sd((count, rows, width), F32),
        sd((count, rows, width), BF16),
        sd((count, rows, ratio * width), BF16),
        sd((count, rows, ratio * width), BF16),
        sd((count, seq if last else rows, width), F32),
    ]
    x_spec = (
        shifted_spec(stream.shape, count, place) if stream.shape[0] != count else image_spec(stream.shape)
    )
    grid = pltpu.PrefetchScalarGridSpec(
        num_scalar_prefetch=1,
        grid=(count,),
        in_specs=[x_spec, whole_spec(shared.shape), whole_spec(split.shape), pl.BlockSpec(memory_space=pl.ANY)],
        out_specs=[image_spec(o.shape) for o in outs],
        scratch_shapes=weight_scratch(width, ratio, rows),
    )
    return pl.pallas_call(
        functools.partial(forward_kernel, layer, seq, rows, keys),
        grid_spec=grid,
        out_shape=outs,
        compiler_params=params(),
        name=f"forward{layer}",
    )(meta, stream, shared, split, blocks)


def backward_layer(
    layer, last, count, seq, rows, keys, meta, place, grad, hits, stream, kept, shared, blocks
):
    a, q, k, v, probs, mixed, h, c, act, slope, _ = kept
    width = shared.shape[1]
    ratio = act.shape[2] // width
    sd = jax.ShapeDtypeStruct
    first = stream.shape[0] != count
    outs = [
        sd((count, rows, width), BF16),
        sd((count, rows, ratio * width), BF16),
        sd((count, rows, width), BF16),
        sd((count, rows, 3 * width), BF16),
        sd((16, width), F32),
        sd((count, seq if first else rows, width), F32),
    ]
    out_specs = [image_spec(o.shape) if o.shape[0] == count else whole_spec(o.shape) for o in outs]
    x_spec = shifted_spec(stream.shape, count, place) if first else image_spec(stream.shape)
    dy_spec = shifted_spec(grad.shape, count, place) if last else image_spec(grad.shape)
    grid = pltpu.PrefetchScalarGridSpec(
        num_scalar_prefetch=1,
        grid=(count,),
        in_specs=[
            dy_spec,
            shifted_spec(hits.shape, count, place),
            x_spec,
            image_spec(h.shape),
            image_spec(slope.shape),
            image_spec(probs.shape),
            image_spec(q.shape),
            image_spec(k.shape),
            image_spec(v.shape),
            whole_spec(shared.shape),
            pl.BlockSpec(memory_space=pl.ANY),
        ],
        out_specs=out_specs,
        scratch_shapes=weight_scratch(width, ratio, rows),
    )
    return pl.pallas_call(
        functools.partial(backward_kernel, layer, seq, rows, keys, last),
        grid_spec=grid,
        out_shape=outs,
        compiler_params=params(),
        name=f"backward{layer}",
    )(meta, grad, hits, stream, h, slope, probs, q, k, v, shared, blocks)


def layer_gradients(layer, meta, kept, pieces_back, target, slot_total, side, share_count):
    a, q, k, v, probs, mixed, h, c, act, slope, _ = kept
    dyr, du, dhr, dqkv = pieces_back
    flat = lambda z: z.reshape(-1, z.shape[-1])
    ops = [flat(z) for z in (a, dqkv, mixed, dhr, c, du, act, dyr)]
    tokens, width = ops[0].shape
    ratio = ops[5].shape[1] // width
    pieces = width // side
    per_layer = pieces * (4 + 2 * ratio)
    start_out = 3 * pieces
    start_up = 4 * pieces
    start_down = start_up + pieces * ratio

    def clip(s, low, count):
        return jnp.minimum(jnp.maximum(s - low, 0), count - 1)

    maps = [
        ((tokens, side), lambda s, meta: (0, clip(s, 0, start_out) // 3)),
        ((tokens, width), lambda s, meta: (0, clip(s, 0, start_out) % 3)),
        ((tokens, width), lambda s, meta: (0, 0)),
        ((tokens, side), lambda s, meta: (0, clip(s, start_out, pieces))),
        ((tokens, side), lambda s, meta: (0, clip(s, start_up, pieces * ratio) // ratio)),
        ((tokens, width), lambda s, meta: (0, clip(s, start_up, pieces * ratio) % ratio)),
        ((tokens, width), lambda s, meta: (0, clip(s, start_down, pieces * ratio) // pieces)),
        ((tokens, side), lambda s, meta: (0, clip(s, start_down, pieces * ratio) % pieces)),
    ]
    in_specs = [pl.BlockSpec(shape, index) for shape, index in maps]
    alias = {}
    if target is not None:
        in_specs.append(pl.BlockSpec(memory_space=pl.ANY))
        ops.append(target)
        alias = {len(ops): 0}
    grid = pltpu.PrefetchScalarGridSpec(
        num_scalar_prefetch=1,
        grid=(per_layer,),
        in_specs=in_specs,
        out_specs=pl.BlockSpec(
            (share_count, 1, side, side), lambda s, meta: (0, meta[layer * per_layer + s], 0, 0)
        ),
        scratch_shapes=[pltpu.VMEM((side, tokens), BF16), pltpu.VMEM((width, tokens), BF16)],
    )
    return pl.pallas_call(
        functools.partial(gradient_kernel, pieces, ratio),
        grid_spec=grid,
        out_shape=jax.ShapeDtypeStruct((share_count, slot_total, side, side), BF16),
        input_output_aliases=alias,
        compiler_params=params(),
        name=f"gradients{layer}",
    )(meta, *ops)


def adam(live, scalars, gradient, weight, left, right, first, second):
    count, _, side, _ = weight.shape
    spec = pl.BlockSpec((1, 1, side, side), lambda i: (i, 0, 0, 0))
    smem = pl.BlockSpec(memory_space=pltpu.SMEM)
    out = jax.ShapeDtypeStruct(weight.shape, F32)
    return pl.pallas_call(
        adam_kernel,
        grid=(count,),
        in_specs=[smem, smem, pl.BlockSpec((1, side, side), lambda i: (i, 0, 0))] + [spec] * 5,
        out_specs=[spec] * 3,
        out_shape=[out] * 3,
        compiler_params=params(),
        name="adam",
    )(live, scalars, gradient, weight, left, right, first, second)


def shards(
    block_input,
    cotangent,
    mask_patches,
    owners,
    master_slots,
    left_bases,
    right_bases,
    first_moment,
    second_moment,
    shared_vectors,
    shared_first,
    shared_second,
    split_vectors,
    split_first,
    split_second,
):
    slot_count = master_slots.shape[0]
    side = master_slots.shape[-1]
    layer_count = shared_vectors.shape[0]
    width = shared_vectors.shape[2]
    half = split_vectors.shape[2]
    ratio = split_vectors.shape[1] - 2
    block_total = owners.shape[0]
    per_layer = block_total // layer_count
    image_total, seq = block_input.shape[:2]
    dp_count = lax.axis_size("dp")
    tp_count = lax.axis_size("tp")
    count = image_total // tp_count
    rows = round_up(seq, 16)
    keys = round_up(seq, 128)
    slot_total = dp_count * slot_count
    dp_rank = lax.axis_index("dp")
    tp_rank = lax.axis_index("tp")
    slot_index = positions(owners, slot_count)
    meta = jnp.concatenate([slot_index, tp_rank[None].astype(jnp.int32)])
    place = block_total

    blocks = lax.all_gather(master_slots[:, 0].astype(BF16), "dp", axis=0, tiled=True)
    blocks = lax.all_gather(blocks, "tp", axis=0)
    split_all = lax.all_gather(split_vectors, "tp", axis=2, tiled=True)
    hits = mask_patches[:, None, :]

    streams = [block_input]
    kept = []
    for layer in range(layer_count):
        last = layer == layer_count - 1
        saved = forward_layer(
            layer, last, count, seq, rows, keys, meta, place, streams[-1],
            shared_vectors[layer], split_all[layer], blocks,
        )
        kept.append(saved)
        streams.append(saved[-1])
    block_output = lax.all_gather(streams[-1], "tp", axis=0, tiled=True)
    grad = cotangent
    vectors = [None] * layer_count
    target = None
    for layer in reversed(range(layer_count)):
        last = layer == layer_count - 1
        dyr, du, dhr, dqkv, vectors[layer], grad = backward_layer(
            layer, last, count, seq, rows, keys, meta, place, grad, hits, streams[layer],
            kept[layer], shared_vectors[layer], blocks,
        )
        target = layer_gradients(
            layer, meta, kept[layer], (dyr, du, dhr, dqkv), target, slot_total, side, tp_count
        )
    input_grad = lax.all_gather(grad, "tp", axis=0, tiled=True)
    reduced = lax.psum_scatter(target, "tp", scatter_dimension=0, tiled=False)
    reduced = lax.psum_scatter(reduced, "dp", scatter_dimension=0, tiled=True).astype(F32)
    vector_sum = lax.psum(jnp.stack(vectors), ("dp", "tp"))
    shared_sum = vector_sum[:, :6]
    split_full = vector_sum[:, 6 : 8 + ratio]
    split_sum = lax.dynamic_slice_in_dim(split_full, tp_rank * half, half, axis=2)
    mine_ids = dp_rank * slot_count + jnp.arange(slot_count, dtype=jnp.int32)
    matches = slot_index[None, :] == mine_ids[:, None]
    live = jnp.any(matches, axis=1)
    block_layer = jnp.arange(block_total, dtype=jnp.int32) // per_layer
    owned_layer = jnp.sum(jnp.where(matches, block_layer[None, :], 0), axis=1)
    block_squares = jnp.where(live, jnp.sum(reduced * reduced, axis=(1, 2)), 0.0)
    layer_pick = (owned_layer[:, None] == jnp.arange(layer_count, dtype=jnp.int32)[None, :]) & live[
        :, None
    ]
    matrix_squares = jnp.sum(jnp.where(layer_pick, block_squares[:, None], 0.0), axis=0)
    vector_squares = jnp.sum(shared_sum * shared_sum, axis=(1, 2)) + jnp.sum(
        split_full * split_full, axis=(1, 2)
    )
    squares = lax.psum(matrix_squares, ("dp", "tp")) + vector_squares
    layer_norms = jnp.sqrt(squares)
    global_norm = jnp.sqrt(jnp.sum(squares))
    factor = CLIP_NORM / jnp.maximum(global_norm, CLIP_NORM)
    step_rate = 0.5 / math.sqrt(width)
    scalars = jnp.stack([factor, jnp.asarray(step_rate, F32)])
    new_master, new_first, new_second = adam(
        live.astype(jnp.int32), scalars, reduced, master_slots, left_bases, right_bases,
        first_moment, second_moment,
    )
    new_shared, new_shared_first, new_shared_second = plain_update(
        shared_sum * factor, shared_vectors, shared_first, shared_second, VECTOR_RATE
    )
    new_split, new_split_first, new_split_second = plain_update(
        split_sum * factor, split_vectors, split_first, split_second, VECTOR_RATE
    )
    return (
        block_output,
        input_grad,
        new_master,
        new_first,
        new_second,
        new_shared,
        new_shared_first,
        new_shared_second,
        new_split,
        new_split_first,
        new_split_second,
        layer_norms,
        global_norm,
    )


def solution(mesh):
    sharded = P("dp", None, None)
    slots = P("dp", "tp", None, None)
    split = P(None, None, "tp")
    return jax.shard_map(
        shards,
        mesh=mesh,
        in_specs=(sharded, sharded, P("dp", None), P())
        + (slots,) * 5
        + (P(),) * 3
        + (split,) * 3,
        out_specs=(sharded, sharded) + (slots,) * 3 + (P(),) * 3 + (split,) * 3 + (P(), P()),
        check_vma=False,
    )
```

```python
import functools
import math

import jax
import jax.numpy as jnp
from jax import lax
from jax.experimental import pallas as pl
from jax.experimental.pallas import tpu as pltpu
from jax.sharding import PartitionSpec as P

DH = 64
GROUP = 4
LANES = GROUP * DH
CLIP_NORM = 1.0
MOMENT_DECAY = 0.5
CORRECTION = 0.9375
ADAM_EPSILON = 1e-08
WEIGHT_DECAY = 0.05
LAYER_EPSILON = 1e-06
VECTOR_RATE = 0.2
VMEM_LIMIT = 60 * 1024 * 1024
F32 = jnp.float32
BF16 = jnp.bfloat16


def nn(a, b):
    return lax.dot_general(a, b, (((1,), (0,)), ((), ())), preferred_element_type=F32)


def nt(a, b):
    return lax.dot_general(a, b, (((1,), (1,)), ((), ())), preferred_element_type=F32)


def tn(a, b):
    return lax.dot_general(a, b, (((0,), (0,)), ((), ())), preferred_element_type=F32)


def round_up(number, step):
    return (number + step - 1) // step * step


def positions(owners, slot_count):
    block_ids = jnp.arange(owners.shape[0], dtype=jnp.int32)
    same_owner = owners[None, :] == owners[:, None]
    earlier = block_ids[None, :] < block_ids[:, None]
    ranking = jnp.sum((same_owner & earlier).astype(jnp.int32), axis=1)
    return owners * slot_count + ranking


def normalized(v):
    center = jnp.mean(v, axis=-1, keepdims=True)
    spread = v - center
    second = jnp.mean(spread * spread, axis=-1, keepdims=True)
    inverse = lax.rsqrt(second + LAYER_EPSILON)
    return spread * inverse, inverse


def norm_back(grad, unit, inverse, gain):
    scaled = grad * gain
    first = jnp.mean(scaled, axis=-1, keepdims=True)
    second = jnp.mean(scaled * unit, axis=-1, keepdims=True)
    return inverse * (scaled - first - unit * second)


def gelu_pair(u):
    bell = jnp.exp(u * u * -0.5)
    below = 1.0 + jnp.abs(u) * (0.3275911 * math.sqrt(0.5))
    t = pl.reciprocal(below, approx=True)
    t = t * (2.0 - below * t)
    poly = 0.5 * 1.061405429
    for factor in (-1.453152027, 1.421413741, -0.284496736, 0.254829592):
        poly = poly * t + 0.5 * factor
    tail = poly * t * bell
    mass = jnp.where(u >= 0, 1.0 - tail, tail)
    return u * mass, mass + u * bell * (1.0 / math.sqrt(2.0 * math.pi))


def weight_copies(meta, layer, blocks, wp, wo, wu, wd, sems):
    side = blocks.shape[-1]
    width = wo.shape[0]
    pieces = width // side
    ratio = wd.shape[0] // width
    per_layer = pieces * (4 + 2 * ratio)
    base = layer * per_layer
    jobs = [[], [], [], []]

    def add(kind, target, b, row, col):
        for t in range(blocks.shape[0]):
            r, c = row(t), col(t)
            jobs[kind].append(
                pltpu.make_async_copy(
                    blocks.at[t, meta[base + b]],
                    target.at[pl.ds(r, side), pl.ds(c, side)],
                    sems.at[kind],
                )
            )

    for r in range(pieces):
        for p in range(3):
            add(0, wp, r * 3 + p, lambda t: r * side, lambda t: p * width + t * side)
    for c in range(pieces):
        add(1, wo, 3 * pieces + c, lambda t: t * side, lambda t: c * side)
    for r in range(pieces):
        for j in range(ratio):
            add(
                2, wu, 4 * pieces + r * ratio + j, lambda t: r * side, lambda t: j * width + t * side
            )
    for j in range(ratio):
        for c in range(pieces):
            add(
                3,
                wd,
                (4 + ratio) * pieces + j * pieces + c,
                lambda t: j * width + t * side,
                lambda t: c * side,
            )
    return jobs


def start_weights(jobs, order):
    @pl.when(pl.program_id(0) == 0)
    def _():
        for kind in order:
            for job in jobs[kind]:
                job.start()


def wait_weights(target, sem):
    @pl.when(pl.program_id(0) == 0)
    def _():
        pltpu.make_async_copy(target, target, sem).wait()


def head_masks():
    lane = lax.broadcasted_iota(jnp.int32, (1, LANES), 1)
    return [(lane // DH) == h for h in range(GROUP)]


def spread_heads(masks, value):
    zero = jnp.zeros((), value.dtype)
    return jnp.concatenate([jnp.where(m, value, zero) for m in masks], axis=0)


def forward_kernel(
    layer, seq, rows, keys, meta, x_ref, shared_ref, split_ref, blocks,
    a_ref, q_ref, k_ref, v_ref, p_ref, mixed_ref, h_ref, c_ref, act_ref, slope_ref, y_ref,
    wp, wo, wu, wd, xs, sems,
):
    width = wo.shape[0]
    ratio = wd.shape[0] // width
    groups = width // LANES
    jobs = weight_copies(meta, layer, blocks, wp, wo, wu, wd, sems)
    start_weights(jobs, (0, 1, 2, 3))
    if x_ref.shape[1] == seq:
        tail = seq // 16 * 16
        xs[tail:rows, :] = jnp.zeros((rows - tail, width), F32)
        xs[0:seq, :] = x_ref[0].astype(F32)
        x = xs[...]
    else:
        x = x_ref[0]
    unit, _ = normalized(x)
    a = (unit * shared_ref[0:1, :] + shared_ref[1:2, :]).astype(BF16)
    a_ref[0] = a
    wait_weights(wp, sems.at[0])
    q = ((nn(a, wp[:, 0:width]) + split_ref[0:1, :]) * (1.0 / math.sqrt(DH))).astype(BF16)
    q_ref[0] = q
    k_ref[0, 0:rows, :] = nn(a, wp[:, width : 2 * width]).astype(BF16)
    v_ref[0, 0:rows, :] = (nn(a, wp[:, 2 * width :]) + split_ref[1:2, :]).astype(BF16)
    k_ref[0, rows:keys, :] = jnp.zeros((keys - rows, width), BF16)
    v_ref[0, rows:keys, :] = jnp.zeros((keys - rows, width), BF16)
    masks = head_masks()
    real = lax.broadcasted_iota(jnp.int32, (1, keys), 1) < seq
    for g in range(groups):
        cols = slice(g * LANES, (g + 1) * LANES)
        qs = spread_heads(masks, q[:, cols])
        scores = nt(qs, k_ref[0, :, cols])
        scores = jnp.where(real, scores, -1e30)
        top = jnp.max(scores, axis=-1, keepdims=True)
        power = jnp.exp(scores - top)
        total = jnp.sum(power, axis=-1, keepdims=True)
        probs = (power * (1.0 / total)).astype(BF16)
        p_ref[0, g * GROUP * rows : (g + 1) * GROUP * rows, :] = probs
        v4 = v_ref[0, :, cols]
        mix = None
        for h in range(GROUP):
            part = nn(
                probs[h * rows : (h + 1) * rows, :], jnp.where(masks[h], v4, jnp.zeros((), BF16))
            )
            mix = part if mix is None else mix + part
        mixed_ref[0, :, cols] = mix.astype(BF16)
    wait_weights(wo, sems.at[1])
    h = x + nn(mixed_ref[0], wo[...]) + shared_ref[2:3, :]
    h_ref[0] = h
    unit, _ = normalized(h)
    c = (unit * shared_ref[3:4, :] + shared_ref[4:5, :]).astype(BF16)
    c_ref[0] = c
    wait_weights(wu, sems.at[2])
    wait_weights(wd, sems.at[3])
    y = h + shared_ref[5:6, :]
    for j in range(ratio):
        cols = slice(j * width, (j + 1) * width)
        u = nn(c, wu[:, cols]) + split_ref[2 + j : 3 + j, :]
        act, slope = gelu_pair(u)
        act = act.astype(BF16)
        act_ref[0, :, cols] = act
        slope_ref[0, :, cols] = slope.astype(BF16)
        y = y + nn(act, wd[cols, :])
    y_ref[0] = y[0 : y_ref.shape[1], :]


def backward_kernel(
    layer, seq, rows, keys, last, meta, dy_ref, hits_ref, x_ref, h_ref, slope_ref, p_ref, q_ref,
    k_ref, v_ref, shared_ref, blocks,
    dyr_ref, du_ref, dhr_ref, dqkv_ref, vec_ref, dx_ref,
    wp, wo, wu, wd, xs, sems,
):
    width = wo.shape[0]
    ratio = wd.shape[0] // width
    groups = width // LANES
    jobs = weight_copies(meta, layer, blocks, wp, wo, wu, wd, sems)
    start_weights(jobs, (3, 2, 1, 0))

    @pl.when(pl.program_id(0) == 0)
    def _():
        vec_ref[...] = jnp.zeros_like(vec_ref)

    def collect(row, value):
        vec_ref[row : row + 1, :] += jnp.sum(value, axis=0, keepdims=True)

    tail = seq // 16 * 16
    if last:
        wanted = lax.broadcasted_iota(jnp.int32, (rows, 1), 0)
        hit = jnp.max(jnp.where(hits_ref[0] + 1 == wanted, 1.0, 0.0), axis=-1, keepdims=True)
        xs[tail:rows, :] = jnp.zeros((rows - tail, width), F32)
        xs[0:seq, :] = dy_ref[0]
        dy = xs[...] * hit
    else:
        dy = dy_ref[0]
    collect(5, dy)
    dyr = dy.astype(BF16)
    dyr_ref[0] = dyr
    wait_weights(wd, sems.at[3])
    wait_weights(wu, sems.at[2])
    dc = None
    for j in range(ratio):
        cols = slice(j * width, (j + 1) * width)
        du = (nt(dyr, wd[cols, :]) * slope_ref[0, :, cols].astype(F32)).astype(BF16)
        du_ref[0, :, cols] = du
        collect(8 + j, du.astype(F32))
        part = nt(du, wu[:, cols])
        dc = part if dc is None else dc + part
    unit, inverse = normalized(h_ref[0])
    collect(3, dc * unit)
    collect(4, dc)
    dh = dy + norm_back(dc, unit, inverse, shared_ref[3:4, :])
    collect(2, dh)
    dhr = dh.astype(BF16)
    dhr_ref[0] = dhr
    wait_weights(wo, sems.at[1])
    dmixed = nt(dhr, wo[...]).astype(BF16)
    masks = head_masks()
    zero = jnp.zeros((), BF16)
    for g in range(groups):
        cols = slice(g * LANES, (g + 1) * LANES)
        dm = spread_heads(masks, dmixed[:, cols])
        probs = p_ref[0, g * GROUP * rows : (g + 1) * GROUP * rows, :]
        k4 = k_ref[0, :, cols]
        dprobs = nt(dm, v_ref[0, :, cols])
        wide = probs.astype(F32)
        both = wide * dprobs
        ds = (both - wide * jnp.sum(both, axis=-1, keepdims=True)).astype(BF16)
        dv = tn(probs, dm)[0:rows, :].astype(BF16)
        dk = tn(ds, spread_heads(masks, q_ref[0, :, cols]))[0:rows, :].astype(BF16)
        dq = None
        for h in range(GROUP):
            part = nn(ds[h * rows : (h + 1) * rows, :], jnp.where(masks[h], k4, zero))
            dq = part if dq is None else dq + part
        dq = (dq.astype(BF16).astype(F32) * (1.0 / math.sqrt(DH))).astype(BF16)
        dqkv_ref[0, :, cols] = dq
        dqkv_ref[0, :, width + g * LANES : width + (g + 1) * LANES] = dk
        dqkv_ref[0, :, 2 * width + g * LANES : 2 * width + (g + 1) * LANES] = dv
    collect(6, dqkv_ref[0, :, 0:width].astype(F32))
    collect(7, dqkv_ref[0, :, 2 * width :].astype(F32))
    wait_weights(wp, sems.at[0])
    da = nt(dqkv_ref[0, :, 0:width], wp[:, 0:width])
    da = da + nt(dqkv_ref[0, :, width : 2 * width], wp[:, width : 2 * width])
    da = da + nt(dqkv_ref[0, :, 2 * width :], wp[:, 2 * width :])
    if x_ref.shape[1] == seq:
        xs[tail:rows, :] = jnp.zeros((rows - tail, width), F32)
        xs[0:seq, :] = x_ref[0].astype(F32)
        x = xs[...]
    else:
        x = x_ref[0]
    unit, inverse = normalized(x)
    collect(0, da * unit)
    collect(1, da)
    dx = dh + norm_back(da, unit, inverse, shared_ref[0:1, :])
    dx_ref[0] = dx[0 : dx_ref.shape[1], :]


def gradient_kernel(
    pieces, ratio, meta, a_ref, dqkv_ref, mixed_ref, dhr_ref, c_ref, du_ref, act_ref, dyr_ref,
    *rest,
):
    out_ref, turned, wide = rest[-3:]
    side = out_ref.shape[-1]
    step = pl.program_id(0)
    start_out = 3 * pieces
    start_up = 4 * pieces
    start_down = start_up + pieces * ratio

    def by_columns(lhs_ref, rhs_ref, first):
        @pl.when(first)
        def _():
            turned[...] = lhs_ref[...].T

        res = nn(turned[...], rhs_ref[...])
        for t in range(out_ref.shape[0]):
            out_ref[t, 0] = res[:, t * side : (t + 1) * side].astype(BF16)

    def by_rows(lhs_ref, rhs_ref, first):
        @pl.when(first)
        def _():
            wide[...] = lhs_ref[...].T

        res = nn(wide[...], rhs_ref[...])
        for t in range(out_ref.shape[0]):
            out_ref[t, 0] = res[t * side : (t + 1) * side, :].astype(BF16)

    @pl.when(step < start_out)
    def _():
        by_columns(a_ref, dqkv_ref, step % 3 == 0)

    @pl.when((step >= start_out) & (step < start_up))
    def _():
        by_rows(mixed_ref, dhr_ref, step == start_out)

    @pl.when((step >= start_up) & (step < start_down))
    def _():
        by_columns(c_ref, du_ref, (step - start_up) % ratio == 0)

    @pl.when(step >= start_down)
    def _():
        by_rows(act_ref, dyr_ref, (step - start_down) % pieces == 0)


def adam_kernel(live_ref, factor_ref, g_ref, w_ref, l_ref, r_ref, m_ref, s_ref, w_out, m_out, s_out):
    step_rate = factor_ref[1]
    high = lax.Precision.HIGHEST

    def dot(a, b, dims):
        return lax.dot_general(a, b, (dims, ((), ())), precision=high, preferred_element_type=F32)

    slot = pl.program_id(0)
    alive = live_ref[slot] > 0
    weight = w_ref[0, 0]
    left = l_ref[0, 0]
    right = r_ref[0, 0]
    gradient = g_ref[0].astype(F32) * factor_ref[0]
    turned = dot(dot(left, gradient, ((0,), (0,))), right, ((1,), (0,)))
    first = MOMENT_DECAY * m_ref[0, 0] + (1.0 - MOMENT_DECAY) * turned
    second = MOMENT_DECAY * s_ref[0, 0] + (1.0 - MOMENT_DECAY) * turned * turned
    stepped = first / CORRECTION / (jnp.sqrt(second / CORRECTION) + ADAM_EPSILON)
    back = dot(dot(left, stepped, ((1,), (0,))), right, ((1,), (1,)))
    w_out[0, 0] = jnp.where(alive, weight - step_rate * (back + WEIGHT_DECAY * weight), weight)
    m_out[0, 0] = jnp.where(alive, first, m_ref[0, 0])
    s_out[0, 0] = jnp.where(alive, second, s_ref[0, 0])


def line_sizes(dp_count):
    if dp_count == 16:
        return (4, 2, 2)
    if dp_count == 64:
        return (4, 4, 4)
    return (dp_count, 1, 1)


def part_table(sizes, total_rows):
    step = 16
    if sizes[0] > sizes[1]:
        large = int(total_rows * 0.39) // step * step
        lengths = (total_rows - 2 * large, large, large)
        orders = ((2, 1, 0), (0, 1, 2), (0, 2, 1))
    else:
        small = total_rows // 3 // step * step
        lengths = (total_rows - 2 * small, small, small)
        orders = ((2, 1, 0), (0, 2, 1), (1, 0, 2))
    offsets = (0, lengths[0], lengths[0] + lengths[1])
    return [(orders[i], offsets[i], lengths[i]) for i in range(3)]


def gather_plan(sizes, parts):
    ready, moves, plan = {}, [], []
    free = [0.0] * 3
    for p, (order, _, _) in enumerate(parts):
        n = [sizes[d] for d in order]
        ready[(p, (0, 0, 0))] = 0.0
        for a in range(n[0]):
            if a + 1 < n[0]:
                moves.append((p, 0, (a, 0, 0)))
            for b in range(n[1]):
                if b + 1 < n[1]:
                    moves.append((p, 1, (a, b, 0)))
                for c in range(n[2] - 1):
                    moves.append((p, 2, (a, b, c)))
    while moves:
        choices = []
        for move in moves:
            p, stage, unit = move
            if (p, unit) in ready:
                start = max(ready[(p, unit)], free[parts[p][0][stage]])
                choices.append((start, stage, p, unit))
        start, stage, p, unit = min(choices)
        end = start + parts[p][2]
        free[parts[p][0][stage]] = end
        ready[(p, one_on(unit, stage))] = end + 60.0
        plan.append((p, stage, unit))
        moves.remove((p, stage, unit))
    return plan


def one_on(unit, stage):
    return tuple(v + (1 if i == stage else 0) for i, v in enumerate(unit))


class Place:
    def __init__(self, sizes):
        self.sizes = sizes
        self.dp = lax.axis_index("dp")
        self.tp = lax.axis_index("tp")
        nz, ny, nx = sizes
        self.at = (self.dp // (ny * nx), self.dp // nx % ny, self.dp % nx)

    def shifted(self, offsets):
        nz, ny, nx = self.sizes
        z, y, x = [
            lax.rem(self.at[d] + (offsets[d] + self.sizes[d]) % self.sizes[d], self.sizes[d])
            for d in range(3)
        ]
        return (z * ny + y) * nx + x

    def along(self, dim, step):
        return self.shifted(tuple(step if d == dim else 0 for d in range(3)))

    def behind(self, order, unit, sign):
        offsets = [0, 0, 0]
        for d, v in zip(order, unit):
            offsets[d] = sign * v
        return self.shifted(tuple(offsets))


def greet(place):
    barrier = pltpu.get_barrier_semaphore()
    number = 1
    pl.semaphore_signal(
        barrier, inc=1, device_id=(place.dp, 1 - place.tp), device_id_type=pl.DeviceIdType.MESH
    )
    for d in range(3):
        for step in range(1, place.sizes[d]):
            number += 1
            pl.semaphore_signal(
                barrier,
                inc=1,
                device_id=(place.along(d, step), place.tp),
                device_id_type=pl.DeviceIdType.MESH,
            )
    pl.semaphore_wait(barrier, number)


def remote(src, dst, send, recv, dp, tp):
    return pltpu.make_async_remote_copy(
        src_ref=src,
        dst_ref=dst,
        send_sem=send,
        recv_sem=recv,
        device_id=(dp, tp),
        device_id_type=pl.DeviceIdType.MESH,
    )


def gather_kernel(
    sizes, parts, plan, master_ref, split_ref, out_ref, split_out,
    own_ref, send, recv, over_send, over_recv, here,
):
    place = Place(sizes)
    dp, tp = place.dp, place.tp
    rows = own_ref.shape[0]
    dims = [n for n in sizes]
    numbers = {}
    for p, (order, _, _) in enumerate(parts):
        for a in range(dims[order[0]]):
            for b in range(dims[order[1]]):
                for c in range(dims[order[2]]):
                    numbers[(p, (a, b, c))] = len(numbers)

    def region(p, unit, share):
        order, start, length = parts[p]
        owner = place.behind(order, unit, -1)
        return out_ref.at[share, pl.ds(pl.multiple_of(owner * rows + start, 16), length)]

    def source(p, unit):
        if unit == (0, 0, 0):
            return own_ref.at[pl.ds(parts[p][1], parts[p][2])]
        return region(p, unit, tp)

    def pass_over(p, unit):
        n = numbers[(p, unit)]
        return remote(
            source(p, unit), region(p, unit, tp), over_send.at[n], over_recv.at[n], dp, 1 - tp
        )

    def taken_over(p, unit):
        n = numbers[(p, unit)]
        piece = region(p, unit, 1 - tp)
        return remote(piece, piece, over_send.at[n], over_recv.at[n], dp, 1 - tp)

    def arriving(p, unit):
        n = numbers[(p, unit)]
        piece = region(p, unit, tp)
        return remote(piece, piece, send.at[n], recv.at[n], dp, 1 - tp)

    def sending(p, stage, unit):
        n = numbers[(p, one_on(unit, stage))]
        target = place.along(parts[p][0][stage], 1)
        return remote(source(p, unit), region(p, unit, tp), send.at[n], recv.at[n], target, tp)

    own_ref[...] = master_ref[...].astype(BF16)
    greet(place)
    started = []
    arrived = set()

    def need(p, unit):
        if (p, unit) in arrived:
            return
        arrived.add((p, unit))
        if unit != (0, 0, 0):
            arriving(p, unit).wait_recv()
        late.append((p, unit))

    late = []
    for p, stage, unit in plan:
        need(p, unit)
        move = sending(p, stage, unit)
        move.start()
        started.append(move)
        while late:
            item = late.pop()
            move = pass_over(*item)
            move.start()
            started.append(move)
    vector = remote(split_ref, split_out.at[tp], here.at[1], here.at[2], dp, 1 - tp)
    vector.start()
    mine = pltpu.make_async_copy(
        own_ref, out_ref.at[tp, pl.ds(pl.multiple_of(dp * rows, 16), rows)], here.at[0]
    )
    mine.start()
    split_out[tp] = split_ref[...]
    for p, unit in numbers:
        need(p, unit)
        while late:
            item = late.pop()
            move = pass_over(*item)
            move.start()
            started.append(move)
    for p, unit in numbers:
        taken_over(p, unit).wait_recv()
    for move in started:
        move.wait_send()
    remote(split_ref, split_out.at[1 - tp], here.at[1], here.at[2], dp, 1 - tp).wait()
    mine.wait()


def gather_weights(sizes, own, split):
    dp_count = sizes[0] * sizes[1] * sizes[2]
    rows, side = own.shape
    parts = part_table(sizes, rows)
    plan = gather_plan(sizes, parts)
    count = 3 * dp_count
    anyspace = pl.BlockSpec(memory_space=pl.ANY)
    vmem = pl.BlockSpec(memory_space=pltpu.VMEM)
    return pl.pallas_call(
        functools.partial(gather_kernel, sizes, parts, plan),
        in_specs=[vmem] * 2,
        out_specs=[anyspace, vmem],
        out_shape=[
            jax.ShapeDtypeStruct((2, dp_count * rows, side), BF16),
            jax.ShapeDtypeStruct((2,) + split.shape, split.dtype),
        ],
        scratch_shapes=[pltpu.VMEM((rows, side), BF16)]
        + [pltpu.SemaphoreType.DMA((count,))] * 4
        + [pltpu.SemaphoreType.DMA((3,))],
        compiler_params=pltpu.CompilerParams(
            collective_id=0, has_side_effects=True, vmem_limit_bytes=VMEM_LIMIT
        ),
        name="gather_weights",
    )(own, split)


def reduce_kernel(
    sizes, parts, plan, layer_count, target_ref, vec_ref, live_ref, block_ref, grad_ref,
    sum_ref, vec_out, square_out, block_out, grad_out,
    own, other, pieces, vec_acc, vec_got, sq_acc, sq_got,
    load, over_send, over_recv, send, recv, vec_send, vec_recv, sq_send, sq_recv, image_sems,
):
    place = Place(sizes)
    dp, tp = place.dp, place.tp
    rows, side = sum_ref.shape
    moves = [(p, stage, one_on(unit, stage), unit) for p, stage, unit in reversed(plan)]
    order_used = []
    for p, stage, unit, _ in moves:
        if (p, unit) not in order_used:
            order_used.append((p, unit))
    for p in range(len(parts)):
        order_used.append((p, (0, 0, 0)))
    numbers = {item: i for i, item in enumerate(order_used)}
    landing = {}
    offset = 0
    inbound = {item: [] for item in order_used}
    for i, (p, stage, unit, to) in enumerate(moves):
        landing[i] = (offset, parts[p][2])
        offset += parts[p][2]
        inbound[(p, to)].append(i)

    def row_range(p, unit):
        order, start, length = parts[p]
        owner = place.behind(order, unit, 1)
        return pl.ds(pl.multiple_of(owner * rows + start, 16), length)

    def loading(item):
        span = row_range(*item)
        n = numbers[item]
        return pltpu.make_async_copy(target_ref.at[tp, span], own.at[span], load.at[n])

    def passing(item):
        span = row_range(*item)
        n = numbers[item]
        return remote(
            target_ref.at[1 - tp, span], other.at[span], over_send.at[n], over_recv.at[n], dp, 1 - tp
        )

    def sending(i):
        p, stage, unit, _ = moves[i]
        start, length = landing[i]
        return remote(
            own.at[row_range(p, unit)],
            pieces.at[pl.ds(start, length)],
            send.at[i],
            recv.at[i],
            place.along(parts[p][0][stage], 1),
            tp,
        )

    def combine(item, final):
        p, unit = item
        order, start, length = parts[p]
        owner = place.behind(order, unit, 1)
        base = owner * rows + start
        froms = [landing[i][0] for i in inbound[item]]
        step = math.gcd(length, 64)

        def body(k, carry):
            at = pl.ds(pl.multiple_of(base + k * step, 16), step)
            total = own[at, :].astype(F32) + other[at, :].astype(F32)
            for place_from in froms:
                got = pieces[pl.ds(pl.multiple_of(place_from + k * step, 16), step), :]
                total = total + got.astype(F32)
            if final:
                sum_ref[pl.ds(pl.multiple_of(start + k * step, 16), step), :] = total
            else:
                own[at, :] = total.astype(BF16)
            return carry

        lax.fori_loop(0, length // step, body, 0)

    hops = [(place.dp, 1 - tp)]
    hop_dims = [None]
    for d in (2, 1, 0):
        reach = 1
        while reach < sizes[d]:
            there = place.at[d] + reach * (1 - 2 * (place.at[d] // reach % 2))
            full = [there if e == d else place.at[e] for e in range(3)]
            hops.append(((full[0] * sizes[1] + full[1]) * sizes[2] + full[2], tp))
            hop_dims.append(d)
            reach *= 2

    def vec_hop(k):
        return remote(
            vec_acc.at[k], vec_got.at[k], vec_send.at[k], vec_recv.at[k], hops[k][0], hops[k][1]
        )

    def sq_hop(k):
        return remote(
            sq_acc.at[k], sq_got.at[k], sq_send.at[k], sq_recv.at[k], hops[k][0], hops[k][1]
        )

    def vec_step(k):
        if k > 0:
            vec_hop(k - 1).wait_recv()
            vec_acc[k] = vec_acc[k - 1] + vec_got[k - 1]
        if k < len(hops):
            vec_hop(k).start()

    vec_acc[0] = vec_ref[...]
    greet(place)
    for item in order_used:
        loading(item).start()
        passing(item).start()
    vec_step(0)
    done = 0
    since = 0
    combined = set()
    for i, (p, stage, unit, to) in enumerate(moves):
        item = (p, unit)
        if item not in combined:
            combined.add(item)
            loading(item).wait()
            passing(item).wait_recv()
            for j in inbound[item]:
                sending(j).wait_recv()
            combine(item, False)
            dim = hop_dims[min(done, len(hops) - 1)]
            behind = [
                j
                for j in inbound[item]
                if j >= since and parts[moves[j][0]][0][moves[j][1]] == dim
            ]
            if done < len(hops) and (behind or dim is None):
                done += 1
                vec_step(done)
                since = i
        sending(i).start()
    while done < len(hops):
        done += 1
        vec_step(done)
    images = [
        remote(src, dst, image_sems.at[2 * n], image_sems.at[2 * n + 1], dp, 1 - tp)
        for n, (src, dst) in enumerate(((block_ref, block_out), (grad_ref, grad_out)))
    ]
    for image in images:
        image.start()
    vec_sum = vec_acc[len(hops)]
    vec_out[...] = vec_sum
    for p in range(len(parts)):
        item = (p, (0, 0, 0))
        loading(item).wait()
        passing(item).wait_recv()
        for j in inbound[item]:
            sending(j).wait_recv()
        combine(item, True)
    slot_count = live_ref.shape[0]
    tile = jnp.zeros(square_out.shape, F32)
    lane = lax.broadcasted_iota(jnp.int32, square_out.shape, 1)
    for s in range(slot_count):
        block = sum_ref[s * side : (s + 1) * side, :]
        square = jnp.sum(jnp.sum(block * block, axis=0, keepdims=True), axis=1, keepdims=True)
        tile = tile + jnp.where(live_ref[s] > 0, square, 0.0)
    sq_acc[0] = tile
    for k in range(len(hops)):
        sq_hop(k).start()
        sq_hop(k).wait_recv()
        sq_acc[k + 1] = sq_acc[k] + sq_got[k]
    tile = sq_acc[len(hops)]
    per_layer = vec_sum.shape[0] // layer_count
    for layer in range(layer_count):
        block = vec_sum[layer * per_layer : (layer + 1) * per_layer, :]
        square = jnp.sum(jnp.sum(block * block, axis=0, keepdims=True), axis=1, keepdims=True)
        tile = tile + jnp.where(lane == layer, square, 0.0)
    square_out[...] = tile
    for item in order_used:
        passing(item).wait_send()
    for i in range(len(moves)):
        sending(i).wait_send()
    for k in range(len(hops)):
        vec_hop(k).wait_send()
        sq_hop(k).wait_send()
    for image in images:
        image.wait()


def reduce_gradients(sizes, layer_count, slot_count, target, vectors, live_tile, block_own, grad_own):
    dp_count = sizes[0] * sizes[1] * sizes[2]
    side = target.shape[-1]
    rows = slot_count * side
    target = target.reshape(2, dp_count * rows, side)
    parts = part_table(sizes, rows)
    plan = gather_plan(sizes, parts)
    hops = 1 + sum(n.bit_length() - 1 for n in sizes)
    units = 3 * dp_count
    landing = sum(parts[p][2] for p, _, _ in plan)
    anyspace = pl.BlockSpec(memory_space=pl.ANY)
    vmem = pl.BlockSpec(memory_space=pltpu.VMEM)
    sd = jax.ShapeDtypeStruct
    dma = pltpu.SemaphoreType.DMA
    return pl.pallas_call(
        functools.partial(reduce_kernel, sizes, parts, plan, layer_count),
        in_specs=[anyspace, vmem, vmem, anyspace, anyspace],
        out_specs=[vmem, vmem, vmem, anyspace, anyspace],
        out_shape=[
            sd((rows, side), F32),
            sd(vectors.shape, F32),
            sd(live_tile.shape[1:], F32),
            sd(block_own.shape, F32),
            sd(block_own.shape, F32),
        ],
        scratch_shapes=[
            pltpu.VMEM((dp_count * rows, side), BF16),
            pltpu.VMEM((dp_count * rows, side), BF16),
            pltpu.VMEM((landing, side), BF16),
            pltpu.VMEM((hops + 1,) + vectors.shape, F32),
            pltpu.VMEM((hops,) + vectors.shape, F32),
            pltpu.VMEM((hops + 1,) + live_tile.shape[1:], F32),
            pltpu.VMEM((hops,) + live_tile.shape[1:], F32),
            dma((units,)),
            dma((units,)),
            dma((units,)),
            dma((len(plan),)),
            dma((len(plan),)),
            dma((hops,)),
            dma((hops,)),
            dma((hops,)),
            dma((hops,)),
            dma((4,)),
        ],
        compiler_params=pltpu.CompilerParams(
            collective_id=1, has_side_effects=True, vmem_limit_bytes=VMEM_LIMIT
        ),
        name="reduce_gradients",
    )(target, vectors, live_tile, block_own, grad_own)


def plain_update(gradient, weight, first_state, second_state, step_rate):
    first_new = MOMENT_DECAY * first_state + (1.0 - MOMENT_DECAY) * gradient
    second_new = MOMENT_DECAY * second_state + (1.0 - MOMENT_DECAY) * gradient * gradient
    stepped = first_new / CORRECTION / (jnp.sqrt(second_new / CORRECTION) + ADAM_EPSILON)
    return (weight - step_rate * stepped, first_new, second_new)


def image_spec(shape):
    return pl.BlockSpec((1,) + tuple(shape[1:]), lambda i, meta: (i, 0, 0))


def shifted_spec(shape, count, place):
    return pl.BlockSpec((1,) + tuple(shape[1:]), lambda i, meta: (meta[place] * count + i, 0, 0))


def whole_spec(shape):
    return pl.BlockSpec(tuple(shape), lambda i, meta: (0,) * len(shape))


def params():
    return pltpu.CompilerParams(vmem_limit_bytes=VMEM_LIMIT, dimension_semantics=("arbitrary",))


def weight_scratch(width, ratio, rows):
    return [
        pltpu.VMEM((width, 3 * width), BF16),
        pltpu.VMEM((width, width), BF16),
        pltpu.VMEM((width, ratio * width), BF16),
        pltpu.VMEM((ratio * width, width), BF16),
        pltpu.VMEM((rows, width), F32),
        pltpu.SemaphoreType.DMA((4,)),
    ]


def forward_layer(layer, last, count, seq, rows, keys, meta, place, stream, shared, split, blocks):
    width = shared.shape[1]
    ratio = split.shape[0] - 2
    heads = width // DH
    sd = jax.ShapeDtypeStruct
    outs = [
        sd((count, rows, width), BF16),
        sd((count, rows, width), BF16),
        sd((count, keys, width), BF16),
        sd((count, keys, width), BF16),
        sd((count, heads * rows, keys), BF16),
        sd((count, rows, width), BF16),
        sd((count, rows, width), F32),
        sd((count, rows, width), BF16),
        sd((count, rows, ratio * width), BF16),
        sd((count, rows, ratio * width), BF16),
        sd((count, seq if last else rows, width), F32),
    ]
    x_spec = (
        shifted_spec(stream.shape, count, place) if stream.shape[0] != count else image_spec(stream.shape)
    )
    grid = pltpu.PrefetchScalarGridSpec(
        num_scalar_prefetch=1,
        grid=(count,),
        in_specs=[x_spec, whole_spec(shared.shape), whole_spec(split.shape), pl.BlockSpec(memory_space=pl.ANY)],
        out_specs=[image_spec(o.shape) for o in outs],
        scratch_shapes=weight_scratch(width, ratio, rows),
    )
    return pl.pallas_call(
        functools.partial(forward_kernel, layer, seq, rows, keys),
        grid_spec=grid,
        out_shape=outs,
        compiler_params=params(),
        name=f"forward{layer}",
    )(meta, stream, shared, split, blocks)


def backward_layer(
    layer, last, count, seq, rows, keys, meta, place, grad, hits, stream, kept, shared, blocks
):
    a, q, k, v, probs, mixed, h, c, act, slope, _ = kept
    width = shared.shape[1]
    ratio = act.shape[2] // width
    sd = jax.ShapeDtypeStruct
    first = stream.shape[0] != count
    outs = [
        sd((count, rows, width), BF16),
        sd((count, rows, ratio * width), BF16),
        sd((count, rows, width), BF16),
        sd((count, rows, 3 * width), BF16),
        sd((16, width), F32),
        sd((count, seq if first else rows, width), F32),
    ]
    out_specs = [image_spec(o.shape) if o.shape[0] == count else whole_spec(o.shape) for o in outs]
    x_spec = shifted_spec(stream.shape, count, place) if first else image_spec(stream.shape)
    dy_spec = shifted_spec(grad.shape, count, place) if last else image_spec(grad.shape)
    grid = pltpu.PrefetchScalarGridSpec(
        num_scalar_prefetch=1,
        grid=(count,),
        in_specs=[
            dy_spec,
            shifted_spec(hits.shape, count, place),
            x_spec,
            image_spec(h.shape),
            image_spec(slope.shape),
            image_spec(probs.shape),
            image_spec(q.shape),
            image_spec(k.shape),
            image_spec(v.shape),
            whole_spec(shared.shape),
            pl.BlockSpec(memory_space=pl.ANY),
        ],
        out_specs=out_specs,
        scratch_shapes=weight_scratch(width, ratio, rows),
    )
    return pl.pallas_call(
        functools.partial(backward_kernel, layer, seq, rows, keys, last),
        grid_spec=grid,
        out_shape=outs,
        compiler_params=params(),
        name=f"backward{layer}",
    )(meta, grad, hits, stream, h, slope, probs, q, k, v, shared, blocks)


def layer_gradients(layer, meta, kept, pieces_back, target, slot_total, side, share_count):
    a, q, k, v, probs, mixed, h, c, act, slope, _ = kept
    dyr, du, dhr, dqkv = pieces_back
    flat = lambda z: z.reshape(-1, z.shape[-1])
    ops = [flat(z) for z in (a, dqkv, mixed, dhr, c, du, act, dyr)]
    tokens, width = ops[0].shape
    ratio = ops[5].shape[1] // width
    pieces = width // side
    per_layer = pieces * (4 + 2 * ratio)
    start_out = 3 * pieces
    start_up = 4 * pieces
    start_down = start_up + pieces * ratio

    def clip(s, low, count):
        return jnp.minimum(jnp.maximum(s - low, 0), count - 1)

    maps = [
        ((tokens, side), lambda s, meta: (0, clip(s, 0, start_out) // 3)),
        ((tokens, width), lambda s, meta: (0, clip(s, 0, start_out) % 3)),
        ((tokens, width), lambda s, meta: (0, 0)),
        ((tokens, side), lambda s, meta: (0, clip(s, start_out, pieces))),
        ((tokens, side), lambda s, meta: (0, clip(s, start_up, pieces * ratio) // ratio)),
        ((tokens, width), lambda s, meta: (0, clip(s, start_up, pieces * ratio) % ratio)),
        ((tokens, width), lambda s, meta: (0, clip(s, start_down, pieces * ratio) // pieces)),
        ((tokens, side), lambda s, meta: (0, clip(s, start_down, pieces * ratio) % pieces)),
    ]
    in_specs = [pl.BlockSpec(shape, index) for shape, index in maps]
    alias = {}
    if target is not None:
        in_specs.append(pl.BlockSpec(memory_space=pl.ANY))
        ops.append(target)
        alias = {len(ops): 0}
    grid = pltpu.PrefetchScalarGridSpec(
        num_scalar_prefetch=1,
        grid=(per_layer,),
        in_specs=in_specs,
        out_specs=pl.BlockSpec(
            (share_count, 1, side, side), lambda s, meta: (0, meta[layer * per_layer + s], 0, 0)
        ),
        scratch_shapes=[pltpu.VMEM((side, tokens), BF16), pltpu.VMEM((width, tokens), BF16)],
    )
    return pl.pallas_call(
        functools.partial(gradient_kernel, pieces, ratio),
        grid_spec=grid,
        out_shape=jax.ShapeDtypeStruct((share_count, slot_total, side, side), BF16),
        input_output_aliases=alias,
        compiler_params=params(),
        name=f"gradients{layer}",
    )(meta, *ops)


def adam(live, scalars, gradient, weight, left, right, first, second):
    count, _, side, _ = weight.shape
    spec = pl.BlockSpec((1, 1, side, side), lambda i: (i, 0, 0, 0))
    smem = pl.BlockSpec(memory_space=pltpu.SMEM)
    out = jax.ShapeDtypeStruct(weight.shape, F32)
    return pl.pallas_call(
        adam_kernel,
        grid=(count,),
        in_specs=[smem, smem, pl.BlockSpec((1, side, side), lambda i: (i, 0, 0))] + [spec] * 5,
        out_specs=[spec] * 3,
        out_shape=[out] * 3,
        compiler_params=params(),
        name="adam",
    )(live, scalars, gradient, weight, left, right, first, second)


def shards(
    block_input,
    cotangent,
    mask_patches,
    owners,
    master_slots,
    left_bases,
    right_bases,
    first_moment,
    second_moment,
    shared_vectors,
    shared_first,
    shared_second,
    split_vectors,
    split_first,
    split_second,
):
    slot_count = master_slots.shape[0]
    side = master_slots.shape[-1]
    layer_count = shared_vectors.shape[0]
    width = shared_vectors.shape[2]
    half = split_vectors.shape[2]
    ratio = split_vectors.shape[1] - 2
    block_total = owners.shape[0]
    per_layer = block_total // layer_count
    image_total, seq = block_input.shape[:2]
    dp_count = lax.axis_size("dp")
    tp_count = lax.axis_size("tp")
    count = image_total // tp_count
    rows = round_up(seq, 16)
    keys = round_up(seq, 128)
    slot_total = dp_count * slot_count
    dp_rank = lax.axis_index("dp")
    tp_rank = lax.axis_index("tp")
    slot_index = positions(owners, slot_count)
    meta = jnp.concatenate([slot_index, tp_rank[None].astype(jnp.int32)])
    place = block_total

    sizes = line_sizes(dp_count)
    own = master_slots.reshape(slot_count * side, side)
    blocks, split_pair = gather_weights(sizes, own, split_vectors)
    blocks = blocks.reshape(tp_count, slot_total, side, side)
    split_all = jnp.concatenate([split_pair[t] for t in range(tp_count)], axis=2)
    hits = mask_patches[:, None, :]

    streams = [block_input]
    kept = []
    for layer in range(layer_count):
        last = layer == layer_count - 1
        saved = forward_layer(
            layer, last, count, seq, rows, keys, meta, place, streams[-1],
            shared_vectors[layer], split_all[layer], blocks,
        )
        kept.append(saved)
        streams.append(saved[-1])
    grad = cotangent
    vectors = [None] * layer_count
    target = None
    for layer in reversed(range(layer_count)):
        last = layer == layer_count - 1
        dyr, du, dhr, dqkv, vectors[layer], grad = backward_layer(
            layer, last, count, seq, rows, keys, meta, place, grad, hits, streams[layer],
            kept[layer], shared_vectors[layer], blocks,
        )
        target = layer_gradients(
            layer, meta, kept[layer], (dyr, du, dhr, dqkv), target, slot_total, side, tp_count
        )
    mine_ids = dp_rank * slot_count + jnp.arange(slot_count, dtype=jnp.int32)
    matches = slot_index[None, :] == mine_ids[:, None]
    live = jnp.any(matches, axis=1)
    block_layer = jnp.arange(block_total, dtype=jnp.int32) // per_layer
    owned_layer = jnp.sum(jnp.where(matches, block_layer[None, :], 0), axis=1)
    lanes = lax.broadcasted_iota(jnp.int32, (slot_count, 8, 128), 2)
    live_tile = jnp.where((lanes == owned_layer[:, None, None]) & live[:, None, None], 1.0, 0.0)
    reduced, vector_sum, square_tile, block_far, grad_far = reduce_gradients(
        sizes, layer_count, slot_count, target, jnp.concatenate(vectors), live_tile, streams[-1], grad
    )

    def both(near, far):
        low = jnp.where(tp_rank == 0, near, far)
        high = jnp.where(tp_rank == 0, far, near)
        return jnp.concatenate([low, high], axis=0)

    block_output = both(streams[-1], block_far)
    input_grad = both(grad, grad_far)
    reduced = reduced.reshape(slot_count, side, side)
    vector_sum = vector_sum.reshape(layer_count, -1, width)
    shared_sum = vector_sum[:, :6]
    split_full = vector_sum[:, 6 : 8 + ratio]
    split_sum = lax.dynamic_slice_in_dim(split_full, tp_rank * half, half, axis=2)
    squares = square_tile[0, :layer_count]
    layer_norms = jnp.sqrt(squares)
    global_norm = jnp.sqrt(jnp.sum(squares))
    factor = CLIP_NORM / jnp.maximum(global_norm, CLIP_NORM)
    step_rate = 0.5 / math.sqrt(width)
    scalars = jnp.stack([factor, jnp.asarray(step_rate, F32)])
    new_master, new_first, new_second = adam(
        live.astype(jnp.int32), scalars, reduced, master_slots, left_bases, right_bases,
        first_moment, second_moment,
    )
    new_shared, new_shared_first, new_shared_second = plain_update(
        shared_sum * factor, shared_vectors, shared_first, shared_second, VECTOR_RATE
    )
    new_split, new_split_first, new_split_second = plain_update(
        split_sum * factor, split_vectors, split_first, split_second, VECTOR_RATE
    )
    return (
        block_output,
        input_grad,
        new_master,
        new_first,
        new_second,
        new_shared,
        new_shared_first,
        new_shared_second,
        new_split,
        new_split_first,
        new_split_second,
        layer_norms,
        global_norm,
    )


def solution(mesh):
    sharded = P("dp", None, None)
    slots = P("dp", "tp", None, None)
    split = P(None, None, "tp")
    return jax.shard_map(
        shards,
        mesh=mesh,
        in_specs=(sharded, sharded, P("dp", None), P())
        + (slots,) * 5
        + (P(),) * 3
        + (split,) * 3,
        out_specs=(sharded, sharded) + (slots,) * 3 + (P(),) * 3 + (split,) * 3 + (P(), P()),
        check_vma=False,
    )
```

```python
import functools
import math

import jax
import jax.numpy as jnp
from jax import lax
from jax.experimental import pallas as pl
from jax.experimental.pallas import tpu as pltpu
from jax.sharding import PartitionSpec as P

DH = 64
GROUP = 4
LANES = GROUP * DH
CLIP_NORM = 1.0
MOMENT_DECAY = 0.5
CORRECTION = 0.9375
ADAM_EPSILON = 1e-08
WEIGHT_DECAY = 0.05
LAYER_EPSILON = 1e-06
VECTOR_RATE = 0.2
VMEM_LIMIT = 60 * 1024 * 1024
F32 = jnp.float32
BF16 = jnp.bfloat16


def nn(a, b):
    return lax.dot_general(a, b, (((1,), (0,)), ((), ())), preferred_element_type=F32)


def nt(a, b):
    return lax.dot_general(a, b, (((1,), (1,)), ((), ())), preferred_element_type=F32)


def tn(a, b):
    return lax.dot_general(a, b, (((0,), (0,)), ((), ())), preferred_element_type=F32)


def round_up(number, step):
    return (number + step - 1) // step * step


def positions(owners, slot_count):
    block_ids = jnp.arange(owners.shape[0], dtype=jnp.int32)
    same_owner = owners[None, :] == owners[:, None]
    earlier = block_ids[None, :] < block_ids[:, None]
    ranking = jnp.sum((same_owner & earlier).astype(jnp.int32), axis=1)
    return owners * slot_count + ranking


def normalized(v):
    center = jnp.mean(v, axis=-1, keepdims=True)
    spread = v - center
    second = jnp.mean(spread * spread, axis=-1, keepdims=True)
    inverse = lax.rsqrt(second + LAYER_EPSILON)
    return spread * inverse, inverse


def norm_back(grad, unit, inverse, gain):
    scaled = grad * gain
    first = jnp.mean(scaled, axis=-1, keepdims=True)
    second = jnp.mean(scaled * unit, axis=-1, keepdims=True)
    return inverse * (scaled - first - unit * second)


def gelu_pair(u):
    bell = jnp.exp(u * u * -0.5)
    mass = 0.5 + 0.5 * lax.erf(u * math.sqrt(0.5))
    return u * mass, mass + u * bell * (1.0 / math.sqrt(2.0 * math.pi))


def weight_copies(meta, layer, blocks, wp, wo, wu, wd, sems):
    side = blocks.shape[-1]
    width = wo.shape[0]
    pieces = width // side
    ratio = wd.shape[0] // width
    per_layer = pieces * (4 + 2 * ratio)
    base = layer * per_layer
    jobs = [[], [], [], []]

    def add(kind, target, b, row, col):
        for t in range(blocks.shape[0]):
            r, c = row(t), col(t)
            jobs[kind].append(
                pltpu.make_async_copy(
                    blocks.at[t, meta[base + b]],
                    target.at[pl.ds(r, side), pl.ds(c, side)],
                    sems.at[kind],
                )
            )

    for r in range(pieces):
        for p in range(3):
            add(0, wp, r * 3 + p, lambda t: r * side, lambda t: p * width + t * side)
    for c in range(pieces):
        add(1, wo, 3 * pieces + c, lambda t: t * side, lambda t: c * side)
    for r in range(pieces):
        for j in range(ratio):
            add(
                2, wu, 4 * pieces + r * ratio + j, lambda t: r * side, lambda t: j * width + t * side
            )
    for j in range(ratio):
        for c in range(pieces):
            add(
                3,
                wd,
                (4 + ratio) * pieces + j * pieces + c,
                lambda t: j * width + t * side,
                lambda t: c * side,
            )
    return jobs


def head_masks():
    lane = lax.broadcasted_iota(jnp.int32, (1, LANES), 1)
    return [(lane // DH) == h for h in range(GROUP)]


def spread_heads(masks, value):
    zero = jnp.zeros((), value.dtype)
    return jnp.concatenate([jnp.where(m, value, zero) for m in masks], axis=0)


def padded_rows(ref, seq, rows, scratch):
    tail = seq // 16 * 16
    scratch[tail:rows, :] = jnp.zeros((rows - tail, ref.shape[2]), F32)
    scratch[0:seq, :] = ref[0].astype(F32)


SAVED = ("a", "mixed", "c", "act", "dyr", "du", "dhr", "dqkv")


def layers_kernel(layer_count, seq, rows, keys, meta, x_ref, dy_ref, hits_ref, shared_ref, split_ref, blocks, *rest):
    outs = rest[: 8 * layer_count]
    y_ref, dx_ref, vec_ref = rest[8 * layer_count : 8 * layer_count + 3]
    rest = rest[8 * layer_count + 3 :]
    saves = rest[: 8 * layer_count]
    rest = rest[8 * layer_count :]
    weights = [rest[4 * n : 4 * n + 4] for n in range(layer_count)]
    rest = rest[4 * layer_count :]
    holds = [rest[7 * n : 7 * n + 7] for n in range(layer_count)]
    seed_ref, save_sems, weight_sems = rest[7 * layer_count :]
    width = x_ref.shape[2]
    ratio = split_ref.shape[1] - 2
    groups = width // LANES
    scale = 1.0 / math.sqrt(DH)
    step = pl.program_id(0)
    zero = jnp.zeros((), BF16)
    masks = head_masks()

    class Kept:
        def __init__(self, layer, name):
            n = layer * 8 + SAVED.index(name)
            self.out, self.ref, self.sem = outs[n], saves[n], save_sems.at[n]

        def copy(self, i):
            return pltpu.make_async_copy(self.ref, self.out.at[i], self.sem)

        def free(self):
            @pl.when(step > 0)
            def _():
                self.copy(step - 1).wait()

        def send(self):
            self.copy(step).start()

    def keep(layer, name, value):
        kept = Kept(layer, name)
        kept.free()
        kept.ref[...] = value
        kept.send()

    jobs = [
        weight_copies(meta, n, blocks, *weights[n], weight_sems.at[n]) for n in range(layer_count)
    ]

    def start(pairs):
        @pl.when(step == 0)
        def _():
            for n, kind in pairs:
                for job in jobs[n][kind]:
                    job.start()

    def ready(layer, kind):
        @pl.when(step == 0)
        def _():
            target = weights[layer][kind]
            pltpu.make_async_copy(target, target, weight_sems.at[layer, kind]).wait()

    start([(0, 0), (0, 1)])

    @pl.when(step == 0)
    def _():
        vec_ref[...] = jnp.zeros_like(vec_ref)
        for hold in holds:
            for ref in (hold[3], hold[4]):
                ref[rows:keys, :] = jnp.zeros((keys - rows, width), BF16)

    padded_rows(x_ref, seq, rows, holds[0][0])
    real = lax.broadcasted_iota(jnp.int32, (1, keys), 1) < seq
    for n in range(layer_count):
        xs, hs, qs, ks, vs, ps, ss = holds[n]
        wp, wo, wu, wd = weights[n]
        unit, _ = normalized(xs[...])
        a = (unit * shared_ref[n, 0:1, :] + shared_ref[n, 1:2, :]).astype(BF16)
        keep(n, "a", a)
        ready(n, 0)
        if n == 0:
            start([(0, 2), (0, 3)])
        qs[...] = ((nn(a, wp[:, 0:width]) + split_ref[n, 0:1, :]) * scale).astype(BF16)
        ks[0:rows, :] = nn(a, wp[:, width : 2 * width]).astype(BF16)
        vs[0:rows, :] = (nn(a, wp[:, 2 * width :]) + split_ref[n, 1:2, :]).astype(BF16)
        mixed = Kept(n, "mixed")
        mixed.free()
        for g in range(groups):
            cols = slice(g * LANES, (g + 1) * LANES)
            scores = nt(spread_heads(masks, qs[:, cols]), ks[:, cols])
            scores = jnp.where(real, scores, -1e30)
            top = jnp.max(scores, axis=-1, keepdims=True)
            power = jnp.exp(scores - top)
            total = jnp.sum(power, axis=-1, keepdims=True)
            probs = (power * (1.0 / total)).astype(BF16)
            ps[g * GROUP * rows : (g + 1) * GROUP * rows, :] = probs
            v4 = vs[:, cols]
            mix = None
            for h in range(GROUP):
                part = nn(probs[h * rows : (h + 1) * rows, :], jnp.where(masks[h], v4, zero))
                mix = part if mix is None else mix + part
            mixed.ref[:, cols] = mix.astype(BF16)
        mixed.send()
        ready(n, 1)
        h = xs[...] + nn(mixed.ref[...], wo[...]) + shared_ref[n, 2:3, :]
        hs[...] = h
        unit, _ = normalized(h)
        c = (unit * shared_ref[n, 3:4, :] + shared_ref[n, 4:5, :]).astype(BF16)
        keep(n, "c", c)
        ready(n, 2)
        ready(n, 3)
        if n == 0:
            start([(m, kind) for m in range(1, layer_count) for kind in range(4)])
        y = h + shared_ref[n, 5:6, :]
        active = Kept(n, "act")
        active.free()
        for j in range(ratio):
            cols = slice(j * width, (j + 1) * width)
            u = nn(c, wu[:, cols]) + split_ref[n, 2 + j : 3 + j, :]
            act, slope = gelu_pair(u)
            act = act.astype(BF16)
            active.ref[:, cols] = act
            ss[:, cols] = slope.astype(BF16)
            y = y + nn(act, wd[cols, :])
        active.send()
        if n + 1 < layer_count:
            holds[n + 1][0][...] = y
        else:
            y_ref[0] = y[0:seq, :]

    wanted = lax.broadcasted_iota(jnp.int32, (rows, 1), 0)
    hit = jnp.max(jnp.where(hits_ref[0] + 1 == wanted, 1.0, 0.0), axis=-1, keepdims=True)
    padded_rows(dy_ref, seq, rows, seed_ref)
    dy = seed_ref[...] * hit
    for n in reversed(range(layer_count)):
        xs, hs, qs, ks, vs, ps, ss = holds[n]
        wp, wo, wu, wd = weights[n]

        def collect(row, value):
            vec_ref[n, row : row + 1, :] += jnp.sum(value, axis=0, keepdims=True)

        collect(5, dy)
        dyr = dy.astype(BF16)
        keep(n, "dyr", dyr)
        hidden = Kept(n, "du")
        hidden.free()
        dc = None
        for j in range(ratio):
            cols = slice(j * width, (j + 1) * width)
            du = (nt(dyr, wd[cols, :]) * ss[:, cols].astype(F32)).astype(BF16)
            hidden.ref[:, cols] = du
            collect(8 + j, du.astype(F32))
            part = nt(du, wu[:, cols])
            dc = part if dc is None else dc + part
        hidden.send()
        unit, inverse = normalized(hs[...])
        collect(3, dc * unit)
        collect(4, dc)
        dh = dy + norm_back(dc, unit, inverse, shared_ref[n, 3:4, :])
        collect(2, dh)
        dhr = dh.astype(BF16)
        keep(n, "dhr", dhr)
        dmixed = nt(dhr, wo[...]).astype(BF16)
        back = Kept(n, "dqkv")
        back.free()
        for g in range(groups):
            cols = slice(g * LANES, (g + 1) * LANES)
            dm = spread_heads(masks, dmixed[:, cols])
            probs = ps[g * GROUP * rows : (g + 1) * GROUP * rows, :]
            k4 = ks[:, cols]
            dprobs = nt(dm, vs[:, cols])
            wide = probs.astype(F32)
            both = wide * dprobs
            ds = (both - wide * jnp.sum(both, axis=-1, keepdims=True)).astype(BF16)
            dv = tn(probs, dm)[0:rows, :].astype(BF16)
            dk = tn(ds, spread_heads(masks, qs[:, cols]))[0:rows, :].astype(BF16)
            dq = None
            for h in range(GROUP):
                part = nn(ds[h * rows : (h + 1) * rows, :], jnp.where(masks[h], k4, zero))
                dq = part if dq is None else dq + part
            back.ref[:, cols] = (dq.astype(BF16).astype(F32) * scale).astype(BF16)
            back.ref[:, width + g * LANES : width + (g + 1) * LANES] = dk
            back.ref[:, 2 * width + g * LANES : 2 * width + (g + 1) * LANES] = dv
        back.send()
        dqkv = back.ref[...]
        collect(6, dqkv[:, 0:width].astype(F32))
        collect(7, dqkv[:, 2 * width :].astype(F32))
        da = nt(dqkv, wp[...])
        unit, inverse = normalized(xs[...])
        collect(0, da * unit)
        collect(1, da)
        dy = dh + norm_back(da, unit, inverse, shared_ref[n, 0:1, :])
    dx_ref[0] = dy[0:seq, :]

    @pl.when(step == pl.num_programs(0) - 1)
    def _():
        for n in range(layer_count):
            for name in SAVED:
                Kept(n, name).copy(step).wait()


def run_layers(count, seq, rows, keys, meta, place, stream, seed, hits, shared, split, blocks):
    layer_count, _, width = shared.shape
    ratio = split.shape[1] - 2
    heads = width // DH
    sd = jax.ShapeDtypeStruct
    widths = [width, width, width, ratio * width, width, ratio * width, width, 3 * width] * layer_count
    anyspace = pl.BlockSpec(memory_space=pl.ANY)
    outs = [sd((count, rows, w), BF16) for w in widths]
    outs += [sd((count, seq, width), F32)] * 2 + [sd((layer_count, 16, width), F32)]
    image = pl.BlockSpec((1, seq, width), lambda i, meta: (i, 0, 0))

    def shifted(shape):
        return pl.BlockSpec((1,) + tuple(shape[1:]), lambda i, meta: (meta[place] * count + i, 0, 0))

    def whole(shape):
        return pl.BlockSpec(tuple(shape), lambda i, meta: (0,) * len(shape))

    vmem = pltpu.VMEM
    scratch = [vmem((rows, w), BF16) for w in widths]
    scratch += [
        vmem((width, 3 * width), BF16),
        vmem((width, width), BF16),
        vmem((width, ratio * width), BF16),
        vmem((ratio * width, width), BF16),
    ] * layer_count
    scratch += [
        vmem((rows, width), F32),
        vmem((rows, width), F32),
        vmem((rows, width), BF16),
        vmem((keys, width), BF16),
        vmem((keys, width), BF16),
        vmem((heads * rows, keys), BF16),
        vmem((rows, ratio * width), BF16),
    ] * layer_count
    scratch += [
        vmem((rows, width), F32),
        pltpu.SemaphoreType.DMA((8 * layer_count,)),
        pltpu.SemaphoreType.DMA((layer_count, 4)),
    ]
    grid = pltpu.PrefetchScalarGridSpec(
        num_scalar_prefetch=1,
        grid=(count,),
        in_specs=[
            shifted(stream.shape),
            shifted(seed.shape),
            shifted(hits.shape),
            whole(shared.shape),
            whole(split.shape),
            anyspace,
        ],
        out_specs=[anyspace] * len(widths) + [image, image, whole((layer_count, 16, width))],
        scratch_shapes=scratch,
    )
    res = pl.pallas_call(
        functools.partial(layers_kernel, layer_count, seq, rows, keys),
        grid_spec=grid,
        out_shape=outs,
        compiler_params=params(),
        name="layers",
    )(meta, stream, seed, hits, shared, split, blocks)
    kept = [dict(zip(SAVED, res[8 * n : 8 * n + 8])) for n in range(layer_count)]
    return kept, res[8 * layer_count], res[8 * layer_count + 1], res[8 * layer_count + 2]


def gradient_kernel(
    layer, pieces, ratio, meta, a_ref, dqkv_ref, mixed_ref, dhr_ref, c_ref, du_ref, act_ref,
    dyr_ref, *rest,
):
    out_ref, turned, stage, sems = rest[-4:]
    side = out_ref.shape[-1]
    shares = out_ref.shape[0]
    step = pl.program_id(0)
    last = pl.num_programs(0) - 1
    start_up = 4
    start_down = 4 + ratio
    base = layer * pieces * (4 + 2 * ratio)
    slot = step % 2

    def saves(buffer, place):
        out = []
        for i in range(pieces):
            for j in range(pieces):
                block, share = place(i, j)
                out.append(
                    pltpu.make_async_copy(
                        stage.at[buffer, pl.ds(i * side, side), pl.ds(j * side, side)],
                        out_ref.at[share, meta[base + block]],
                        sems.at[buffer],
                    )
                )
        return out

    def drain(buffer):
        pltpu.make_async_copy(stage.at[buffer], stage.at[buffer], sems.at[buffer]).wait()

    @pl.when(step >= 2)
    def _():
        drain(slot)

    def work(lhs_ref, rhs_ref, first, place):
        if first is None:
            lhs = lhs_ref[...].T
        else:

            @pl.when(first)
            def _():
                turned[...] = lhs_ref[...].T

            lhs = turned[...]
        stage[slot] = nn(lhs, rhs_ref[...]).astype(BF16)
        for save in saves(slot, place):
            save.start()

    @pl.when(step < 3)
    def _():
        work(a_ref, dqkv_ref, step == 0, lambda i, j: (i * 3 + step, j))

    @pl.when(step == 3)
    def _():
        work(mixed_ref, dhr_ref, None, lambda i, j: (3 * pieces + j, i))

    @pl.when((step >= start_up) & (step < start_down))
    def _():
        work(
            c_ref, du_ref, step == start_up,
            lambda i, j: (4 * pieces + i * ratio + step - start_up, j),
        )

    @pl.when(step >= start_down)
    def _():
        work(
            act_ref, dyr_ref, None,
            lambda i, j: ((4 + ratio) * pieces + (step - start_down) * pieces + j, i),
        )

    @pl.when(step == last)
    def _():
        drain(1 - slot)
        drain(slot)


def adam_kernel(live_ref, factor_ref, g_ref, w_ref, l_ref, r_ref, m_ref, s_ref, w_out, m_out, s_out):
    step_rate = factor_ref[1]
    slot = pl.program_id(0)
    alive = live_ref[slot] > 0
    weight = w_ref[0, 0]
    left = l_ref[0, 0].astype(BF16)
    right = r_ref[0, 0].astype(BF16)
    turned = nn(tn(left, g_ref[0].astype(BF16)).astype(BF16), right) * factor_ref[0]
    first = MOMENT_DECAY * m_ref[0, 0] + (1.0 - MOMENT_DECAY) * turned
    second = MOMENT_DECAY * s_ref[0, 0] + (1.0 - MOMENT_DECAY) * turned * turned
    stepped = first / CORRECTION / (jnp.sqrt(second / CORRECTION) + ADAM_EPSILON)
    back = nt(nn(left, stepped.astype(BF16)).astype(BF16), right)
    w_out[0, 0] = jnp.where(alive, weight - step_rate * (back + WEIGHT_DECAY * weight), weight)
    m_out[0, 0] = jnp.where(alive, first, m_ref[0, 0])
    s_out[0, 0] = jnp.where(alive, second, s_ref[0, 0])


def line_sizes(dp_count):
    if dp_count == 16:
        return (4, 2, 2)
    if dp_count == 64:
        return (4, 4, 4)
    return (dp_count, 1, 1)


def part_table(sizes, total_rows):
    step = 16
    if sizes[0] > sizes[1]:
        large = int(total_rows * 0.39) // step * step
        lengths = (total_rows - 2 * large, large, large)
        orders = ((2, 1, 0), (0, 1, 2), (0, 2, 1))
    else:
        small = total_rows // 3 // step * step
        lengths = (total_rows - 2 * small, small, small)
        orders = ((2, 1, 0), (0, 2, 1), (1, 0, 2))
    offsets = (0, lengths[0], lengths[0] + lengths[1])
    return [(orders[i], offsets[i], lengths[i]) for i in range(3)]


def gather_plan(sizes, parts):
    ready, moves, plan = {}, [], []
    free = [0.0] * 3
    for p, (order, _, _) in enumerate(parts):
        n = [sizes[d] for d in order]
        ready[(p, (0, 0, 0))] = 0.0
        for a in range(n[0]):
            if a + 1 < n[0]:
                moves.append((p, 0, (a, 0, 0)))
            for b in range(n[1]):
                if b + 1 < n[1]:
                    moves.append((p, 1, (a, b, 0)))
                for c in range(n[2] - 1):
                    moves.append((p, 2, (a, b, c)))
    while moves:
        choices = []
        for move in moves:
            p, stage, unit = move
            if (p, unit) in ready:
                start = max(ready[(p, unit)], free[parts[p][0][stage]])
                choices.append((start, stage, p, unit))
        start, stage, p, unit = min(choices)
        end = start + parts[p][2]
        free[parts[p][0][stage]] = end
        ready[(p, one_on(unit, stage))] = end + 60.0
        plan.append((p, stage, unit))
        moves.remove((p, stage, unit))
    return plan


def one_on(unit, stage):
    return tuple(v + (1 if i == stage else 0) for i, v in enumerate(unit))


class Place:
    def __init__(self, sizes):
        self.sizes = sizes
        self.dp = lax.axis_index("dp")
        self.tp = lax.axis_index("tp")
        nz, ny, nx = sizes
        self.at = (self.dp // (ny * nx), self.dp // nx % ny, self.dp % nx)

    def shifted(self, offsets):
        nz, ny, nx = self.sizes
        z, y, x = [
            lax.rem(self.at[d] + (offsets[d] + self.sizes[d]) % self.sizes[d], self.sizes[d])
            for d in range(3)
        ]
        return (z * ny + y) * nx + x

    def along(self, dim, step):
        return self.shifted(tuple(step if d == dim else 0 for d in range(3)))

    def behind(self, order, unit, sign):
        offsets = [0, 0, 0]
        for d, v in zip(order, unit):
            offsets[d] = sign * v
        return self.shifted(tuple(offsets))


def greet(place):
    barrier = pltpu.get_barrier_semaphore()
    number = 1
    pl.semaphore_signal(
        barrier, inc=1, device_id=(place.dp, 1 - place.tp), device_id_type=pl.DeviceIdType.MESH
    )
    for d in range(3):
        for step in range(1, place.sizes[d]):
            number += 1
            pl.semaphore_signal(
                barrier,
                inc=1,
                device_id=(place.along(d, step), place.tp),
                device_id_type=pl.DeviceIdType.MESH,
            )
    pl.semaphore_wait(barrier, number)


def remote(src, dst, send, recv, dp, tp):
    return pltpu.make_async_remote_copy(
        src_ref=src,
        dst_ref=dst,
        send_sem=send,
        recv_sem=recv,
        device_id=(dp, tp),
        device_id_type=pl.DeviceIdType.MESH,
    )


def gather_kernel(
    sizes, parts, plan, master_ref, split_ref, out_ref, split_out,
    own_ref, send, recv, over_send, over_recv, here,
):
    place = Place(sizes)
    dp, tp = place.dp, place.tp
    rows = own_ref.shape[0]
    dims = [n for n in sizes]
    numbers = {}
    for p, (order, _, _) in enumerate(parts):
        for a in range(dims[order[0]]):
            for b in range(dims[order[1]]):
                for c in range(dims[order[2]]):
                    numbers[(p, (a, b, c))] = len(numbers)

    def region(p, unit, share):
        order, start, length = parts[p]
        owner = place.behind(order, unit, -1)
        return out_ref.at[share, pl.ds(pl.multiple_of(owner * rows + start, 16), length)]

    def source(p, unit):
        if unit == (0, 0, 0):
            return own_ref.at[pl.ds(parts[p][1], parts[p][2])]
        return region(p, unit, tp)

    def pass_over(p, unit):
        n = numbers[(p, unit)]
        return remote(
            source(p, unit), region(p, unit, tp), over_send.at[n], over_recv.at[n], dp, 1 - tp
        )

    def taken_over(p, unit):
        n = numbers[(p, unit)]
        piece = region(p, unit, 1 - tp)
        return remote(piece, piece, over_send.at[n], over_recv.at[n], dp, 1 - tp)

    def arriving(p, unit):
        n = numbers[(p, unit)]
        piece = region(p, unit, tp)
        return remote(piece, piece, send.at[n], recv.at[n], dp, 1 - tp)

    def sending(p, stage, unit):
        n = numbers[(p, one_on(unit, stage))]
        target = place.along(parts[p][0][stage], 1)
        return remote(source(p, unit), region(p, unit, tp), send.at[n], recv.at[n], target, tp)

    own_ref[...] = master_ref[...].astype(BF16)
    greet(place)
    started = []
    arrived = set()

    def need(p, unit):
        if (p, unit) in arrived:
            return
        arrived.add((p, unit))
        if unit != (0, 0, 0):
            arriving(p, unit).wait_recv()
        late.append((p, unit))

    late = []
    for p, stage, unit in plan:
        need(p, unit)
        move = sending(p, stage, unit)
        move.start()
        started.append(move)
        while late:
            item = late.pop()
            move = pass_over(*item)
            move.start()
            started.append(move)
    vector = remote(split_ref, split_out.at[tp], here.at[1], here.at[2], dp, 1 - tp)
    vector.start()
    mine = pltpu.make_async_copy(
        own_ref, out_ref.at[tp, pl.ds(pl.multiple_of(dp * rows, 16), rows)], here.at[0]
    )
    mine.start()
    split_out[tp] = split_ref[...]
    for p, unit in numbers:
        need(p, unit)
        while late:
            item = late.pop()
            move = pass_over(*item)
            move.start()
            started.append(move)
    for p, unit in numbers:
        taken_over(p, unit).wait_recv()
    for move in started:
        move.wait_send()
    remote(split_ref, split_out.at[1 - tp], here.at[1], here.at[2], dp, 1 - tp).wait()
    mine.wait()


def gather_weights(sizes, own, split):
    dp_count = sizes[0] * sizes[1] * sizes[2]
    rows, side = own.shape
    parts = part_table(sizes, rows)
    plan = gather_plan(sizes, parts)
    count = 3 * dp_count
    anyspace = pl.BlockSpec(memory_space=pl.ANY)
    vmem = pl.BlockSpec(memory_space=pltpu.VMEM)
    return pl.pallas_call(
        functools.partial(gather_kernel, sizes, parts, plan),
        in_specs=[vmem] * 2,
        out_specs=[anyspace, vmem],
        out_shape=[
            jax.ShapeDtypeStruct((2, dp_count * rows, side), BF16),
            jax.ShapeDtypeStruct((2,) + split.shape, split.dtype),
        ],
        scratch_shapes=[pltpu.VMEM((rows, side), BF16)]
        + [pltpu.SemaphoreType.DMA((count,))] * 4
        + [pltpu.SemaphoreType.DMA((3,))],
        compiler_params=pltpu.CompilerParams(
            collective_id=0, has_side_effects=True, vmem_limit_bytes=VMEM_LIMIT
        ),
        name="gather_weights",
    )(own, split)


def reduce_kernel(
    sizes, parts, plan, layer_count, target_ref, vec_ref, live_ref, block_ref, grad_ref,
    sum_ref, vec_out, square_out, block_out, grad_out,
    own, other, pieces, tiles, far_tiles, tile_pieces, full,
    load, over_send, over_recv, send, recv, tile_send, tile_recv, hop_send, hop_recv, image_sems,
):
    place = Place(sizes)
    dp, tp = place.dp, place.tp
    rows, side = sum_ref.shape
    moves = [(p, stage, one_on(unit, stage), unit) for p, stage, unit in reversed(plan)]
    order_used = []
    for p, stage, unit, _ in moves:
        if (p, unit) not in order_used:
            order_used.append((p, unit))
    for p in range(len(parts)):
        order_used.append((p, (0, 0, 0)))
    numbers = {item: i for i, item in enumerate(order_used)}
    landing = {}
    offset = 0
    inbound = {item: [] for item in order_used}
    for i, (p, stage, unit, to) in enumerate(moves):
        landing[i] = (offset, parts[p][2])
        offset += parts[p][2]
        inbound[(p, to)].append(i)

    def row_range(p, unit):
        order, start, length = parts[p]
        owner = place.behind(order, unit, 1)
        return pl.ds(pl.multiple_of(owner * rows + start, 16), length)

    def loading(item):
        span = row_range(*item)
        n = numbers[item]
        return pltpu.make_async_copy(target_ref.at[tp, span], own.at[span], load.at[n])

    def passing(item):
        span = row_range(*item)
        n = numbers[item]
        return remote(
            target_ref.at[1 - tp, span], other.at[span], over_send.at[n], over_recv.at[n], dp, 1 - tp
        )

    def sending(i):
        p, stage, unit, _ = moves[i]
        start, length = landing[i]
        return remote(
            own.at[row_range(p, unit)],
            pieces.at[pl.ds(start, length)],
            send.at[i],
            recv.at[i],
            place.along(parts[p][0][stage], 1),
            tp,
        )

    def combine(item, final):
        p, unit = item
        order, start, length = parts[p]
        owner = place.behind(order, unit, 1)
        base = owner * rows + start
        froms = [landing[i][0] for i in inbound[item]]
        step = math.gcd(length, 64)

        def body(k, carry):
            at = pl.ds(pl.multiple_of(base + k * step, 16), step)
            total = own[at, :].astype(F32) + other[at, :].astype(F32)
            for place_from in froms:
                got = pieces[pl.ds(pl.multiple_of(place_from + k * step, 16), step), :]
                total = total + got.astype(F32)
            if final:
                sum_ref[pl.ds(pl.multiple_of(start + k * step, 16), step), :] = total
            else:
                own[at, :] = total.astype(BF16)
            return carry

        lax.fori_loop(0, length // step, body, 0)

    dp_count = sizes[0] * sizes[1] * sizes[2]
    lanes = tiles.shape[2]
    chunks = vec_ref.shape[1] // lanes
    square_row = chunks
    riding = [i for i in range(len(moves)) if moves[i][0] == 1]

    def tile_of(p, unit):
        return tp * dp_count + place.behind(parts[p][0], unit, 1)

    def tile_over():
        return remote(
            tiles.at[pl.ds((1 - tp) * dp_count, dp_count)],
            far_tiles,
            tile_send.at[len(riding)],
            tile_recv.at[len(riding)],
            dp,
            1 - tp,
        )

    def tile_sending(i):
        p, stage, unit, _ = moves[i]
        n = riding.index(i)
        return remote(
            tiles.at[tile_of(p, unit)],
            tile_pieces.at[n],
            tile_send.at[n],
            tile_recv.at[n],
            place.along(parts[p][0][stage], 1),
            tp,
        )

    def tile_combine(item):
        at = tile_of(*item)
        total = tiles[at] + far_tiles[place.behind(parts[1][0], item[1], 1)]
        for j in inbound[item]:
            tile_sending(j).wait_recv()
            total = total + tile_pieces[riding.index(j)]
        tiles[at] = total

    hops = []
    for d in (2, 1, 0):
        reach = 1
        while reach < sizes[d]:
            bit = place.at[d] // reach % 2
            there = place.at[d] + reach * (1 - 2 * bit)
            coords = [there if e == d else place.at[e] for e in range(3)]
            stride = (sizes[1] * sizes[2], sizes[2], 1)[d]
            low = dp // (stride * reach) * (stride * reach)
            hops.append(((coords[0] * sizes[1] + coords[1]) * sizes[2] + coords[2], tp, stride * reach, low))
            reach *= 2

    def hop_copy(k):
        far_dp, far_tp, span, low = hops[k]
        region = full.at[:, pl.ds(low, span)]
        return remote(region, region, hop_send.at[k], hop_recv.at[k], far_dp, far_tp)

    def hop_arrival(k):
        far_dp, far_tp, span, low = hops[k]
        region = full.at[:, pl.ds(far_dp // span * span, span)]
        return remote(region, region, hop_send.at[k], hop_recv.at[k], far_dp, far_tp)

    def swap_copy(share):
        region = full.at[share, dp]
        return remote(region, region, hop_send.at[len(hops)], hop_recv.at[len(hops)], dp, 1 - tp)

    tiles[...] = jnp.zeros_like(tiles)
    for r in range(vec_ref.shape[0]):
        for i in range(chunks):
            tiles[r, i : i + 1, :] = vec_ref[r : r + 1, i * lanes : (i + 1) * lanes]
    greet(place)
    tile_over().start()
    for item in order_used:
        loading(item).start()
        passing(item).start()
    combined = set()
    tile_over().wait_recv()
    for i, (p, stage, unit, to) in enumerate(moves):
        item = (p, unit)
        if item not in combined:
            combined.add(item)
            loading(item).wait()
            passing(item).wait_recv()
            for j in inbound[item]:
                sending(j).wait_recv()
            combine(item, False)
            if p == 1:
                tile_combine(item)
        sending(i).start()
        if p == 1:
            tile_sending(i).start()
    images = [
        remote(src, dst, image_sems.at[2 * n], image_sems.at[2 * n + 1], dp, 1 - tp)
        for n, (src, dst) in enumerate(((block_ref, block_out), (grad_ref, grad_out)))
    ]
    for image in images:
        image.start()
    for p in range(len(parts)):
        item = (p, (0, 0, 0))
        loading(item).wait()
        passing(item).wait_recv()
        for j in inbound[item]:
            sending(j).wait_recv()
        combine(item, True)
    slot_count = live_ref.shape[0]
    squares = jnp.zeros((1, lanes), F32)
    for n in range(slot_count):
        block = sum_ref[n * side : (n + 1) * side, :]
        square = jnp.sum(jnp.sum(block * block, axis=0, keepdims=True), axis=1, keepdims=True)
        squares = squares + jnp.where(live_ref[n, 0:1, :] > 0, square, 0.0)
    tile_combine((1, (0, 0, 0)))
    full[tp, dp] = tiles[tp * dp_count + dp]
    full[tp, dp, square_row : square_row + 1, :] = squares
    swap_copy(tp).start()
    swap_copy(1 - tp).wait_recv()
    for k in range(len(hops)):
        hop_copy(k).start()
        hop_arrival(k).wait_recv()
    total = full[0, 0]
    for n in range(1, 2 * dp_count):
        total = total + full[n // dp_count, n % dp_count]
    squares = total[square_row : square_row + 1, :]
    for r in range(vec_ref.shape[0]):
        for i in range(chunks):
            vec_out[r : r + 1, i * lanes : (i + 1) * lanes] = full[r // dp_count, r % dp_count, i : i + 1, :]
    lane = lax.broadcasted_iota(jnp.int32, (1, lanes), 1)
    per_layer = vec_ref.shape[0] // layer_count
    for layer in range(layer_count):
        block = vec_out[layer * per_layer : (layer + 1) * per_layer, :]
        square = jnp.sum(jnp.sum(block * block, axis=0, keepdims=True), axis=1, keepdims=True)
        squares = squares + jnp.where(lane == layer, square, 0.0)
    square_out[...] = jnp.broadcast_to(squares, square_out.shape)
    for item in order_used:
        passing(item).wait_send()
    for i in range(len(moves)):
        sending(i).wait_send()
    tile_over().wait_send()
    for i in riding:
        tile_sending(i).wait_send()
    swap_copy(tp).wait_send()
    for k in range(len(hops)):
        hop_copy(k).wait_send()
    for image in images:
        image.wait()


def reduce_gradients(sizes, layer_count, slot_count, target, vectors, live_tile, block_own, grad_own):
    dp_count = sizes[0] * sizes[1] * sizes[2]
    side = target.shape[-1]
    rows = slot_count * side
    target = target.reshape(2, dp_count * rows, side)
    parts = part_table(sizes, rows)
    plan = gather_plan(sizes, parts)
    hops = 1 + sum(n.bit_length() - 1 for n in sizes)
    riding = sum(1 for p, _, _ in plan if p == 1)
    units = 3 * dp_count
    landing = sum(parts[p][2] for p, _, _ in plan)
    anyspace = pl.BlockSpec(memory_space=pl.ANY)
    vmem = pl.BlockSpec(memory_space=pltpu.VMEM)
    sd = jax.ShapeDtypeStruct
    dma = pltpu.SemaphoreType.DMA
    return pl.pallas_call(
        functools.partial(reduce_kernel, sizes, parts, plan, layer_count),
        in_specs=[anyspace, vmem, vmem, anyspace, anyspace],
        out_specs=[vmem, vmem, vmem, anyspace, anyspace],
        out_shape=[
            sd((rows, side), F32),
            sd(vectors.shape, F32),
            sd(live_tile.shape[1:], F32),
            sd(block_own.shape, F32),
            sd(block_own.shape, F32),
        ],
        scratch_shapes=[
            pltpu.VMEM((dp_count * rows, side), BF16),
            pltpu.VMEM((dp_count * rows, side), BF16),
            pltpu.VMEM((landing, side), BF16),
            pltpu.VMEM((2 * dp_count,) + live_tile.shape[1:], F32),
            pltpu.VMEM((dp_count,) + live_tile.shape[1:], F32),
            pltpu.VMEM((riding,) + live_tile.shape[1:], F32),
            pltpu.VMEM((2, dp_count) + live_tile.shape[1:], F32),
            dma((units,)),
            dma((units,)),
            dma((units,)),
            dma((len(plan),)),
            dma((len(plan),)),
            dma((riding + 1,)),
            dma((riding + 1,)),
            dma((hops,)),
            dma((hops,)),
            dma((4,)),
        ],
        compiler_params=pltpu.CompilerParams(
            collective_id=1, has_side_effects=True, vmem_limit_bytes=VMEM_LIMIT
        ),
        name="reduce_gradients",
    )(target, vectors, live_tile, block_own, grad_own)


def plain_update(gradient, weight, first_state, second_state, step_rate):
    first_new = MOMENT_DECAY * first_state + (1.0 - MOMENT_DECAY) * gradient
    second_new = MOMENT_DECAY * second_state + (1.0 - MOMENT_DECAY) * gradient * gradient
    stepped = first_new / CORRECTION / (jnp.sqrt(second_new / CORRECTION) + ADAM_EPSILON)
    return (weight - step_rate * stepped, first_new, second_new)


def params():
    return pltpu.CompilerParams(vmem_limit_bytes=VMEM_LIMIT, dimension_semantics=("arbitrary",))


def layer_gradients(layer, meta, kept, target, slot_total, side, share_count):
    names = ("a", "dqkv", "mixed", "dhr", "c", "du", "act", "dyr")
    ops = [kept[name].reshape(-1, kept[name].shape[-1]) for name in names]
    tokens, width = ops[0].shape
    ratio = ops[5].shape[1] // width
    pieces = width // side

    def clip(s, low, count):
        return jnp.minimum(jnp.maximum(s - low, 0), count - 1)

    block = (tokens, width)
    maps = [
        lambda s, meta: (0, 0),
        lambda s, meta: (0, clip(s, 0, 3)),
        lambda s, meta: (0, 0),
        lambda s, meta: (0, 0),
        lambda s, meta: (0, 0),
        lambda s, meta: (0, clip(s, 4, ratio)),
        lambda s, meta: (0, clip(s, 4 + ratio, ratio)),
        lambda s, meta: (0, 0),
    ]
    in_specs = [pl.BlockSpec(block, index) for index in maps]
    alias = {}
    if target is not None:
        in_specs.append(pl.BlockSpec(memory_space=pl.ANY))
        ops.append(target)
        alias = {len(ops): 0}
    grid = pltpu.PrefetchScalarGridSpec(
        num_scalar_prefetch=1,
        grid=(4 + 2 * ratio,),
        in_specs=in_specs,
        out_specs=pl.BlockSpec(memory_space=pl.ANY),
        scratch_shapes=[
            pltpu.VMEM((width, tokens), BF16),
            pltpu.VMEM((2, width, width), BF16),
            pltpu.SemaphoreType.DMA((2,)),
        ],
    )
    return pl.pallas_call(
        functools.partial(gradient_kernel, layer, pieces, ratio),
        grid_spec=grid,
        out_shape=jax.ShapeDtypeStruct((share_count, slot_total, side, side), BF16),
        input_output_aliases=alias,
        compiler_params=params(),
        name=f"gradients{layer}",
    )(meta, *ops)


def adam(live, scalars, gradient, weight, left, right, first, second):
    count, _, side, _ = weight.shape
    spec = pl.BlockSpec((1, 1, side, side), lambda i: (i, 0, 0, 0))
    smem = pl.BlockSpec(memory_space=pltpu.SMEM)
    out = jax.ShapeDtypeStruct(weight.shape, F32)
    return pl.pallas_call(
        adam_kernel,
        grid=(count,),
        in_specs=[smem, smem, pl.BlockSpec((1, side, side), lambda i: (i, 0, 0))] + [spec] * 5,
        out_specs=[spec] * 3,
        out_shape=[out] * 3,
        compiler_params=params(),
        name="adam",
    )(live, scalars, gradient, weight, left, right, first, second)


def shards(
    block_input,
    cotangent,
    mask_patches,
    owners,
    master_slots,
    left_bases,
    right_bases,
    first_moment,
    second_moment,
    shared_vectors,
    shared_first,
    shared_second,
    split_vectors,
    split_first,
    split_second,
):
    slot_count = master_slots.shape[0]
    side = master_slots.shape[-1]
    layer_count = shared_vectors.shape[0]
    width = shared_vectors.shape[2]
    half = split_vectors.shape[2]
    ratio = split_vectors.shape[1] - 2
    block_total = owners.shape[0]
    per_layer = block_total // layer_count
    image_total, seq = block_input.shape[:2]
    dp_count = lax.axis_size("dp")
    tp_count = lax.axis_size("tp")
    count = image_total // tp_count
    rows = round_up(seq, 16)
    keys = round_up(seq, 128)
    slot_total = dp_count * slot_count
    dp_rank = lax.axis_index("dp")
    tp_rank = lax.axis_index("tp")
    slot_index = positions(owners, slot_count)
    meta = jnp.concatenate([slot_index, tp_rank[None].astype(jnp.int32)])
    place = block_total

    sizes = line_sizes(dp_count)
    own = master_slots.reshape(slot_count * side, side)
    blocks, split_pair = gather_weights(sizes, own, split_vectors)
    blocks = blocks.reshape(tp_count, slot_total, side, side)
    split_all = jnp.concatenate([split_pair[t] for t in range(tp_count)], axis=2)
    hits = mask_patches[:, None, :]

    kept, output_own, grad_own, vectors = run_layers(
        count, seq, rows, keys, meta, place, block_input, cotangent, hits, shared_vectors, split_all, blocks
    )
    target = None
    for layer in reversed(range(layer_count)):
        target = layer_gradients(layer, meta, kept[layer], target, slot_total, side, tp_count)
    mine_ids = dp_rank * slot_count + jnp.arange(slot_count, dtype=jnp.int32)
    matches = slot_index[None, :] == mine_ids[:, None]
    live = jnp.any(matches, axis=1)
    block_layer = jnp.arange(block_total, dtype=jnp.int32) // per_layer
    owned_layer = jnp.sum(jnp.where(matches, block_layer[None, :], 0), axis=1)
    lanes = lax.broadcasted_iota(jnp.int32, (slot_count, 8, 128), 2)
    live_tile = jnp.where((lanes == owned_layer[:, None, None]) & live[:, None, None], 1.0, 0.0)
    reduced, vector_sum, square_tile, block_far, grad_far = reduce_gradients(
        sizes, layer_count, slot_count, target, vectors.reshape(-1, width), live_tile, output_own, grad_own
    )

    def both(near, far):
        low = jnp.where(tp_rank == 0, near, far)
        high = jnp.where(tp_rank == 0, far, near)
        return jnp.concatenate([low, high], axis=0)

    block_output = both(output_own, block_far)
    input_grad = both(grad_own, grad_far)
    reduced = reduced.reshape(slot_count, side, side)
    vector_sum = vector_sum.reshape(layer_count, -1, width)
    shared_sum = vector_sum[:, :6]
    split_full = vector_sum[:, 6 : 8 + ratio]
    split_sum = lax.dynamic_slice_in_dim(split_full, tp_rank * half, half, axis=2)
    squares = square_tile[0, :layer_count]
    layer_norms = jnp.sqrt(squares)
    global_norm = jnp.sqrt(jnp.sum(squares))
    factor = CLIP_NORM / jnp.maximum(global_norm, CLIP_NORM)
    step_rate = 0.5 / math.sqrt(width)
    scalars = jnp.stack([factor, jnp.asarray(step_rate, F32)])
    new_master, new_first, new_second = adam(
        live.astype(jnp.int32), scalars, reduced, master_slots, left_bases, right_bases,
        first_moment, second_moment,
    )
    new_shared, new_shared_first, new_shared_second = plain_update(
        shared_sum * factor, shared_vectors, shared_first, shared_second, VECTOR_RATE
    )
    new_split, new_split_first, new_split_second = plain_update(
        split_sum * factor, split_vectors, split_first, split_second, VECTOR_RATE
    )
    return (
        block_output,
        input_grad,
        new_master,
        new_first,
        new_second,
        new_shared,
        new_shared_first,
        new_shared_second,
        new_split,
        new_split_first,
        new_split_second,
        layer_norms,
        global_norm,
    )


def solution(mesh):
    sharded = P("dp", None, None)
    slots = P("dp", "tp", None, None)
    split = P(None, None, "tp")
    return jax.shard_map(
        shards,
        mesh=mesh,
        in_specs=(sharded, sharded, P("dp", None), P())
        + (slots,) * 5
        + (P(),) * 3
        + (split,) * 3,
        out_specs=(sharded, sharded) + (slots,) * 3 + (P(),) * 3 + (split,) * 3 + (P(), P()),
        check_vma=False,
    )
```

```python
import functools
import math

import jax
import jax.numpy as jnp
from jax import lax
from jax.experimental import pallas as pl
from jax.experimental.pallas import tpu as pltpu
from jax.sharding import PartitionSpec as P

DH = 64
GROUP = 4
LANES = GROUP * DH
CLIP_NORM = 1.0
MOMENT_DECAY = 0.5
CORRECTION = 0.9375
ADAM_EPSILON = 1e-08
WEIGHT_DECAY = 0.05
LAYER_EPSILON = 1e-06
VECTOR_RATE = 0.2
VMEM_LIMIT = 60 * 1024 * 1024
F32 = jnp.float32
BF16 = jnp.bfloat16


def nn(a, b):
    return lax.dot_general(a, b, (((1,), (0,)), ((), ())), preferred_element_type=F32)


def nt(a, b):
    return lax.dot_general(a, b, (((1,), (1,)), ((), ())), preferred_element_type=F32)


def tn(a, b):
    return lax.dot_general(a, b, (((0,), (0,)), ((), ())), preferred_element_type=F32)


def round_up(number, step):
    return (number + step - 1) // step * step


def positions(owners, slot_count):
    block_ids = jnp.arange(owners.shape[0], dtype=jnp.int32)
    same_owner = owners[None, :] == owners[:, None]
    earlier = block_ids[None, :] < block_ids[:, None]
    ranking = jnp.sum((same_owner & earlier).astype(jnp.int32), axis=1)
    return owners * slot_count + ranking


def normalized(v):
    center = jnp.mean(v, axis=-1, keepdims=True)
    spread = v - center
    second = jnp.mean(spread * spread, axis=-1, keepdims=True)
    inverse = lax.rsqrt(second + LAYER_EPSILON)
    return spread * inverse, inverse


def norm_back(grad, unit, inverse, gain):
    scaled = grad * gain
    first = jnp.mean(scaled, axis=-1, keepdims=True)
    second = jnp.mean(scaled * unit, axis=-1, keepdims=True)
    return inverse * (scaled - first - unit * second)


def gelu_pair(u):
    bell = jnp.exp(u * u * -0.5)
    mass = 0.5 + 0.5 * lax.erf(u * math.sqrt(0.5))
    return u * mass, mass + u * bell * (1.0 / math.sqrt(2.0 * math.pi))


def weight_copies(meta, layer, blocks, wp, wo, wu, wd, sems):
    side = blocks.shape[-1]
    width = wo.shape[0]
    pieces = width // side
    ratio = wd.shape[0] // width
    per_layer = pieces * (4 + 2 * ratio)
    base = layer * per_layer
    jobs = [[], [], [], []]

    def add(kind, target, b, row, col):
        for t in range(blocks.shape[0]):
            r, c = row(t), col(t)
            jobs[kind].append(
                pltpu.make_async_copy(
                    blocks.at[t, meta[base + b]],
                    target.at[pl.ds(r, side), pl.ds(c, side)],
                    sems.at[kind],
                )
            )

    for r in range(pieces):
        for p in range(3):
            add(0, wp, r * 3 + p, lambda t: r * side, lambda t: p * width + t * side)
    for c in range(pieces):
        add(1, wo, 3 * pieces + c, lambda t: t * side, lambda t: c * side)
    for r in range(pieces):
        for j in range(ratio):
            add(
                2, wu, 4 * pieces + r * ratio + j, lambda t: r * side, lambda t: j * width + t * side
            )
    for j in range(ratio):
        for c in range(pieces):
            add(
                3,
                wd,
                (4 + ratio) * pieces + j * pieces + c,
                lambda t: j * width + t * side,
                lambda t: c * side,
            )
    return jobs


def head_masks():
    lane = lax.broadcasted_iota(jnp.int32, (1, LANES), 1)
    return [(lane // DH) == h for h in range(GROUP)]


def spread_heads(masks, value):
    zero = jnp.zeros((), value.dtype)
    return jnp.concatenate([jnp.where(m, value, zero) for m in masks], axis=0)


SAVED = ("a", "mixed", "c", "act", "dyr", "du", "dhr", "dqkv")


def layers_kernel(layer_count, seq, rows, keys, meta, x_ref, dy_ref, hits_ref, shared_ref, split_ref, blocks, *rest):
    outs = rest[: 8 * layer_count]
    y_ref, dx_ref, vec_ref = rest[8 * layer_count : 8 * layer_count + 3]
    rest = rest[8 * layer_count + 3 :]
    saves = rest[: 8 * layer_count]
    rest = rest[8 * layer_count :]
    weights = [rest[4 * n : 4 * n + 4] for n in range(layer_count)]
    rest = rest[4 * layer_count :]
    holds = [rest[7 * n : 7 * n + 7] for n in range(layer_count)]
    save_sems, weight_sems = rest[7 * layer_count :]
    width = x_ref.shape[2]
    ratio = split_ref.shape[1] - 2
    groups = width // LANES
    scale = 1.0 / math.sqrt(DH)
    step = pl.program_id(0)
    zero = jnp.zeros((), BF16)
    masks = head_masks()

    def saving(layer, name, i):
        n = layer * 8 + SAVED.index(name)
        return pltpu.make_async_copy(saves[n], outs[n].at[i], save_sems.at[n])

    def free(names):
        @pl.when(step > 0)
        def _():
            for n in range(layer_count):
                for name in names:
                    saving(n, name, step - 1).wait()

    def send(names):
        for n in range(layer_count):
            for name in names:
                saving(n, name, step).start()

    def buffer(layer, name):
        return saves[layer * 8 + SAVED.index(name)]

    jobs = [
        weight_copies(meta, n, blocks, *weights[n], weight_sems.at[n]) for n in range(layer_count)
    ]

    def start(pairs):
        @pl.when(step == 0)
        def _():
            for n, kind in pairs:
                for job in jobs[n][kind]:
                    job.start()

    def ready(pairs):
        @pl.when(step == 0)
        def _():
            for n, kind in pairs:
                target = weights[n][kind]
                pltpu.make_async_copy(target, target, weight_sems.at[n, kind]).wait()

    start([(0, 0)])

    @pl.when(step == 0)
    def _():
        vec_ref[...] = jnp.zeros_like(vec_ref)
        for hold in holds:
            for ref in (hold[3], hold[4]):
                ref[rows:keys, :] = jnp.zeros((keys - rows, width), BF16)

    free(SAVED[:4])
    holds[0][0][...] = x_ref[0].astype(F32)
    real = lax.broadcasted_iota(jnp.int32, (1, keys), 1) < seq
    for n in range(layer_count):
        xs, hs, qs, ks, vs, ps, ss = holds[n]
        wp, wo, wu, wd = weights[n]
        unit, _ = normalized(xs[...])
        a = (unit * shared_ref[n, 0:1, :] + shared_ref[n, 1:2, :]).astype(BF16)
        buffer(n, "a")[...] = a
        if n == 0:
            ready([(0, 0)])
            start([(0, 1), (0, 2), (0, 3)])
        qs[...] = ((nn(a, wp[:, 0:width]) + split_ref[n, 0:1, :]) * scale).astype(BF16)
        ks[0:rows, :] = nn(a, wp[:, width : 2 * width]).astype(BF16)
        vs[0:rows, :] = (nn(a, wp[:, 2 * width :]) + split_ref[n, 1:2, :]).astype(BF16)
        mixed = buffer(n, "mixed")
        for g in range(groups):
            cols = slice(g * LANES, (g + 1) * LANES)
            scores = nt(spread_heads(masks, qs[:, cols]), ks[:, cols])
            scores = jnp.where(real, scores, -1e30)
            top = jnp.max(scores, axis=-1, keepdims=True)
            power = jnp.exp(scores - top)
            total = jnp.sum(power, axis=-1, keepdims=True)
            probs = (power * (1.0 / total)).astype(BF16)
            ps[g * GROUP * rows : (g + 1) * GROUP * rows, :] = probs
            v4 = vs[:, cols]
            mix = None
            for h in range(GROUP):
                part = nn(probs[h * rows : (h + 1) * rows, :], jnp.where(masks[h], v4, zero))
                mix = part if mix is None else mix + part
            mixed[:, cols] = mix.astype(BF16)
        if n == 0:
            ready([(0, 1), (0, 2), (0, 3)])
            start([(m, kind) for m in range(1, layer_count) for kind in range(4)])
        h = xs[...] + nn(mixed[...], wo[...]) + shared_ref[n, 2:3, :]
        hs[...] = h
        unit, _ = normalized(h)
        c = (unit * shared_ref[n, 3:4, :] + shared_ref[n, 4:5, :]).astype(BF16)
        buffer(n, "c")[...] = c
        y = h + shared_ref[n, 5:6, :]
        active = buffer(n, "act")
        for j in range(ratio):
            cols = slice(j * width, (j + 1) * width)
            u = nn(c, wu[:, cols]) + split_ref[n, 2 + j : 3 + j, :]
            act, slope = gelu_pair(u)
            act = act.astype(BF16)
            active[:, cols] = act
            ss[:, cols] = slope.astype(BF16)
            y = y + nn(act, wd[cols, :])
        if n + 1 < layer_count:
            holds[n + 1][0][...] = y
            ready([(n + 1, kind) for kind in range(4)])
        else:
            y_ref[0] = y[0:seq, :]

    send(SAVED[:4])
    free(SAVED[4:])
    wanted = lax.broadcasted_iota(jnp.int32, (rows, 1), 0)
    hit = jnp.max(jnp.where(hits_ref[0] + 1 == wanted, 1.0, 0.0), axis=-1, keepdims=True)
    dy = dy_ref[0] * hit
    for n in reversed(range(layer_count)):
        xs, hs, qs, ks, vs, ps, ss = holds[n]
        wp, wo, wu, wd = weights[n]

        def collect(row, value):
            vec_ref[n, row : row + 1, :] += jnp.sum(value, axis=0, keepdims=True)

        collect(5, dy)
        dyr = dy.astype(BF16)
        buffer(n, "dyr")[...] = dyr
        hidden = buffer(n, "du")
        dc = None
        for j in range(ratio):
            cols = slice(j * width, (j + 1) * width)
            du = (nt(dyr, wd[cols, :]) * ss[:, cols].astype(F32)).astype(BF16)
            hidden[:, cols] = du
            collect(8 + j, du.astype(F32))
            part = nt(du, wu[:, cols])
            dc = part if dc is None else dc + part
        unit, inverse = normalized(hs[...])
        collect(3, dc * unit)
        collect(4, dc)
        dh = dy + norm_back(dc, unit, inverse, shared_ref[n, 3:4, :])
        collect(2, dh)
        dhr = dh.astype(BF16)
        buffer(n, "dhr")[...] = dhr
        dmixed = nt(dhr, wo[...]).astype(BF16)
        back = buffer(n, "dqkv")
        for g in range(groups):
            cols = slice(g * LANES, (g + 1) * LANES)
            dm = spread_heads(masks, dmixed[:, cols])
            probs = ps[g * GROUP * rows : (g + 1) * GROUP * rows, :]
            k4 = ks[:, cols]
            dprobs = nt(dm, vs[:, cols])
            wide = probs.astype(F32)
            both = wide * dprobs
            ds = (both - wide * jnp.sum(both, axis=-1, keepdims=True)).astype(BF16)
            dv = tn(probs, dm)[0:rows, :].astype(BF16)
            dk = tn(ds, spread_heads(masks, qs[:, cols]))[0:rows, :].astype(BF16)
            dq = None
            for h in range(GROUP):
                part = nn(ds[h * rows : (h + 1) * rows, :], jnp.where(masks[h], k4, zero))
                dq = part if dq is None else dq + part
            back[:, cols] = (dq.astype(BF16).astype(F32) * scale).astype(BF16)
            back[:, width + g * LANES : width + (g + 1) * LANES] = dk
            back[:, 2 * width + g * LANES : 2 * width + (g + 1) * LANES] = dv
        dqkv = back[...]
        collect(6, dqkv[:, 0:width].astype(F32))
        collect(7, dqkv[:, 2 * width :].astype(F32))
        da = nt(dqkv, wp[...])
        unit, inverse = normalized(xs[...])
        collect(0, da * unit)
        collect(1, da)
        dy = dh + norm_back(da, unit, inverse, shared_ref[n, 0:1, :])
    dx_ref[0] = dy[0:seq, :]
    send(SAVED[4:])

    @pl.when(step == pl.num_programs(0) - 1)
    def _():
        for n in range(layer_count):
            for name in SAVED:
                saving(n, name, step).wait()


def run_layers(count, seq, rows, keys, meta, place, stream, seed, hits, shared, split, blocks):
    layer_count, _, width = shared.shape
    ratio = split.shape[1] - 2
    heads = width // DH
    sd = jax.ShapeDtypeStruct
    widths = [width, width, width, ratio * width, width, ratio * width, width, 3 * width] * layer_count
    anyspace = pl.BlockSpec(memory_space=pl.ANY)
    outs = [sd((count, rows, w), BF16) for w in widths]
    outs += [sd((2 * count, seq, width), F32)] * 2 + [sd((layer_count, 16, width), F32)]
    image = pl.BlockSpec((1, seq, width), lambda i, meta: (meta[place] * count + i, 0, 0))

    def shifted(shape):
        return pl.BlockSpec((1,) + tuple(shape[1:]), lambda i, meta: (meta[place] * count + i, 0, 0))

    def whole(shape):
        return pl.BlockSpec(tuple(shape), lambda i, meta: (0,) * len(shape))

    vmem = pltpu.VMEM
    scratch = [vmem((rows, w), BF16) for w in widths]
    scratch += [
        vmem((width, 3 * width), BF16),
        vmem((width, width), BF16),
        vmem((width, ratio * width), BF16),
        vmem((ratio * width, width), BF16),
    ] * layer_count
    scratch += [
        vmem((rows, width), F32),
        vmem((rows, width), F32),
        vmem((rows, width), BF16),
        vmem((keys, width), BF16),
        vmem((keys, width), BF16),
        vmem((heads * rows, keys), BF16),
        vmem((rows, ratio * width), BF16),
    ] * layer_count
    scratch += [
        pltpu.SemaphoreType.DMA((8 * layer_count,)),
        pltpu.SemaphoreType.DMA((layer_count, 4)),
    ]
    grid = pltpu.PrefetchScalarGridSpec(
        num_scalar_prefetch=1,
        grid=(count,),
        in_specs=[
            pl.BlockSpec((1, rows, width), lambda i, meta: (i, 0, 0)),
            pl.BlockSpec((1, rows, width), lambda i, meta: (i, 0, 0)),
            shifted(hits.shape),
            whole(shared.shape),
            whole(split.shape),
            anyspace,
        ],
        out_specs=[anyspace] * len(widths) + [image, image, whole((layer_count, 16, width))],
        scratch_shapes=scratch,
    )
    res = pl.pallas_call(
        functools.partial(layers_kernel, layer_count, seq, rows, keys),
        grid_spec=grid,
        out_shape=outs,
        compiler_params=params(),
        name="layers",
    )(meta, stream, seed, hits, shared, split, blocks)
    kept = [dict(zip(SAVED, res[8 * n : 8 * n + 8])) for n in range(layer_count)]
    return kept, res[8 * layer_count], res[8 * layer_count + 1], res[8 * layer_count + 2]


def gradient_kernel(
    layer, pieces, ratio, meta, a_ref, dqkv_ref, mixed_ref, dhr_ref, c_ref, du_ref, act_ref,
    dyr_ref, *rest,
):
    out_ref, turned, stage, sems = rest[-4:]
    side = out_ref.shape[-1]
    shares = out_ref.shape[0]
    step = pl.program_id(0)
    last = pl.num_programs(0) - 1
    start_up = 4
    start_down = 4 + ratio
    base = layer * pieces * (4 + 2 * ratio)
    slot = step % 2

    def saves(buffer, place):
        out = []
        for i in range(pieces):
            for j in range(pieces):
                block, share = place(i, j)
                out.append(
                    pltpu.make_async_copy(
                        stage.at[buffer, pl.ds(i * side, side), pl.ds(j * side, side)],
                        out_ref.at[share, meta[base + block]],
                        sems.at[buffer],
                    )
                )
        return out

    def drain(buffer):
        pltpu.make_async_copy(stage.at[buffer], stage.at[buffer], sems.at[buffer]).wait()

    @pl.when(step >= 2)
    def _():
        drain(slot)

    def work(lhs_ref, rhs_ref, first, place):
        if first is None:
            lhs = lhs_ref[...].T
        else:

            @pl.when(first)
            def _():
                turned[...] = lhs_ref[...].T

            lhs = turned[...]
        stage[slot] = nn(lhs, rhs_ref[...]).astype(BF16)
        for save in saves(slot, place):
            save.start()

    @pl.when(step < 3)
    def _():
        work(a_ref, dqkv_ref, step == 0, lambda i, j: (i * 3 + step, j))

    @pl.when(step == 3)
    def _():
        work(mixed_ref, dhr_ref, None, lambda i, j: (3 * pieces + j, i))

    @pl.when((step >= start_up) & (step < start_down))
    def _():
        work(
            c_ref, du_ref, step == start_up,
            lambda i, j: (4 * pieces + i * ratio + step - start_up, j),
        )

    @pl.when(step >= start_down)
    def _():
        work(
            act_ref, dyr_ref, None,
            lambda i, j: ((4 + ratio) * pieces + (step - start_down) * pieces + j, i),
        )

    @pl.when(step == last)
    def _():
        drain(1 - slot)
        drain(slot)


def adam_kernel(layer_count, step_rate, live_ref, square_ref, g_ref, w_ref, l_ref, r_ref, m_ref, s_ref, w_out, m_out, s_out):
    lane = lax.broadcasted_iota(jnp.int32, (1, square_ref.shape[1]), 1)
    total = jnp.sum(jnp.where(lane < layer_count, square_ref[0:1, :], 0.0), axis=1, keepdims=True)
    factor = CLIP_NORM / jnp.maximum(jnp.sqrt(total), CLIP_NORM)
    slot = pl.program_id(0)
    alive = live_ref[slot] > 0
    weight = w_ref[0, 0]
    left = l_ref[0, 0].astype(BF16)
    right = r_ref[0, 0].astype(BF16)
    turned = nn(tn(left, g_ref[0].astype(BF16)).astype(BF16), right) * factor
    first = MOMENT_DECAY * m_ref[0, 0] + (1.0 - MOMENT_DECAY) * turned
    second = MOMENT_DECAY * s_ref[0, 0] + (1.0 - MOMENT_DECAY) * turned * turned
    stepped = first / CORRECTION / (jnp.sqrt(second / CORRECTION) + ADAM_EPSILON)
    back = nt(nn(left, stepped.astype(BF16)).astype(BF16), right)
    w_out[0, 0] = jnp.where(alive, weight - step_rate * (back + WEIGHT_DECAY * weight), weight)
    m_out[0, 0] = jnp.where(alive, first, m_ref[0, 0])
    s_out[0, 0] = jnp.where(alive, second, s_ref[0, 0])


def line_sizes(dp_count):
    if dp_count == 16:
        return (4, 2, 2)
    if dp_count == 64:
        return (4, 4, 4)
    return (dp_count, 1, 1)


def part_table(sizes, total_rows):
    step = 16
    if sizes[0] > sizes[1]:
        large = int(total_rows * 0.39) // step * step
        lengths = (total_rows - 2 * large, large, large)
        orders = ((2, 1, 0), (0, 1, 2), (0, 2, 1))
    else:
        small = total_rows // 3 // step * step
        lengths = (total_rows - 2 * small, small, small)
        orders = ((2, 1, 0), (0, 2, 1), (1, 0, 2))
    offsets = (0, lengths[0], lengths[0] + lengths[1])
    return [(orders[i], offsets[i], lengths[i]) for i in range(3)]


def gather_plan(sizes, parts):
    ready, moves, plan = {}, [], []
    free = [0.0] * 3
    for p, (order, _, _) in enumerate(parts):
        n = [sizes[d] for d in order]
        ready[(p, (0, 0, 0))] = 0.0
        for a in range(n[0]):
            if a + 1 < n[0]:
                moves.append((p, 0, (a, 0, 0)))
            for b in range(n[1]):
                if b + 1 < n[1]:
                    moves.append((p, 1, (a, b, 0)))
                for c in range(n[2] - 1):
                    moves.append((p, 2, (a, b, c)))
    while moves:
        choices = []
        for move in moves:
            p, stage, unit = move
            if (p, unit) in ready:
                start = max(ready[(p, unit)], free[parts[p][0][stage]])
                choices.append((start, stage, p, unit))
        start, stage, p, unit = min(choices)
        end = start + parts[p][2]
        free[parts[p][0][stage]] = end
        ready[(p, one_on(unit, stage))] = end + 60.0
        plan.append((p, stage, unit))
        moves.remove((p, stage, unit))
    return plan


def one_on(unit, stage):
    return tuple(v + (1 if i == stage else 0) for i, v in enumerate(unit))


class Place:
    def __init__(self, sizes):
        self.sizes = sizes
        self.dp = lax.axis_index("dp")
        self.tp = lax.axis_index("tp")
        nz, ny, nx = sizes
        self.at = (self.dp // (ny * nx), self.dp // nx % ny, self.dp % nx)

    def shifted(self, offsets):
        nz, ny, nx = self.sizes
        z, y, x = [
            lax.rem(self.at[d] + (offsets[d] + self.sizes[d]) % self.sizes[d], self.sizes[d])
            for d in range(3)
        ]
        return (z * ny + y) * nx + x

    def along(self, dim, step):
        return self.shifted(tuple(step if d == dim else 0 for d in range(3)))

    def behind(self, order, unit, sign):
        offsets = [0, 0, 0]
        for d, v in zip(order, unit):
            offsets[d] = sign * v
        return self.shifted(tuple(offsets))


def greet(place):
    barrier = pltpu.get_barrier_semaphore()
    number = 1
    pl.semaphore_signal(
        barrier, inc=1, device_id=(place.dp, 1 - place.tp), device_id_type=pl.DeviceIdType.MESH
    )
    for d in range(3):
        for step in range(1, place.sizes[d]):
            number += 1
            pl.semaphore_signal(
                barrier,
                inc=1,
                device_id=(place.along(d, step), place.tp),
                device_id_type=pl.DeviceIdType.MESH,
            )
    pl.semaphore_wait(barrier, number)


def remote(src, dst, send, recv, dp, tp):
    return pltpu.make_async_remote_copy(
        src_ref=src,
        dst_ref=dst,
        send_sem=send,
        recv_sem=recv,
        device_id=(dp, tp),
        device_id_type=pl.DeviceIdType.MESH,
    )


def gather_kernel(
    sizes, parts, plan, master_ref, split_ref, x_ref, seed_ref, out_ref, split_out, x_out, seed_out,
    own_ref, x_in, x_wide, seed_in, x_own, seed_own, send, recv, over_send, over_recv, here, stream_sems,
):
    place = Place(sizes)
    dp, tp = place.dp, place.tp
    rows = own_ref.shape[0]
    dims = [n for n in sizes]
    numbers = {}
    for p, (order, _, _) in enumerate(parts):
        for a in range(dims[order[0]]):
            for b in range(dims[order[1]]):
                for c in range(dims[order[2]]):
                    numbers[(p, (a, b, c))] = len(numbers)

    def region(p, unit, share):
        order, start, length = parts[p]
        owner = place.behind(order, unit, -1)
        return out_ref.at[share, pl.ds(pl.multiple_of(owner * rows + start, 16), length)]

    def source(p, unit):
        if unit == (0, 0, 0):
            return own_ref.at[pl.ds(parts[p][1], parts[p][2])]
        return region(p, unit, tp)

    def pass_over(p, unit):
        n = numbers[(p, unit)]
        return remote(
            source(p, unit), region(p, unit, tp), over_send.at[n], over_recv.at[n], dp, 1 - tp
        )

    def taken_over(p, unit):
        n = numbers[(p, unit)]
        piece = region(p, unit, 1 - tp)
        return remote(piece, piece, over_send.at[n], over_recv.at[n], dp, 1 - tp)

    def arriving(p, unit):
        n = numbers[(p, unit)]
        piece = region(p, unit, tp)
        return remote(piece, piece, send.at[n], recv.at[n], dp, 1 - tp)

    def sending(p, stage, unit):
        n = numbers[(p, one_on(unit, stage))]
        target = place.along(parts[p][0][stage], 1)
        return remote(source(p, unit), region(p, unit, tp), send.at[n], recv.at[n], target, tp)

    own_ref[...] = master_ref[...].astype(BF16)
    greet(place)
    started = []
    arrived = set()
    count, padded = x_own.shape[:2]
    images = 2 * count
    seq = x_in.shape[0] // images
    strips, _, lanes = x_wide.shape
    fetch = [pltpu.make_async_copy(x_ref, x_in, stream_sems.at[0])] + [
        pltpu.make_async_copy(
            seed_ref.at[:, pl.ds(n * lanes, lanes)], seed_in.at[n], stream_sems.at[4 + n]
        )
        for n in range(strips)
    ]
    leave = [
        pltpu.make_async_copy(x_own, x_out, stream_sems.at[2]),
        pltpu.make_async_copy(seed_own, seed_out, stream_sems.at[3]),
    ]
    tail = seq // 16 * 16

    def widen():
        fetch[0].wait()
        for n in range(strips):
            x_wide[n] = x_in[:, n * lanes : (n + 1) * lanes].astype(F32)

    def pick(source, target, i):
        def go():
            target[i, tail:padded, :] = jnp.zeros((padded - tail, target.shape[2]), target.dtype)
            for n in range(strips):
                rows_of = source[n, pl.ds(tp * count + i, seq, stride=images), :]
                target[i, 0:seq, n * lanes : (n + 1) * lanes] = rows_of.astype(target.dtype)

        return go

    def leaving(n):
        return lambda: leave[n].start()

    tasks = [lambda: [copy.start() for copy in fetch], widen]
    tasks += [pick(x_wide, x_own, i) for i in range(count)] + [leaving(0), lambda: [copy.wait() for copy in fetch[1:]]]
    tasks += [pick(seed_in, seed_own, i) for i in range(count)] + [leaving(1)]
    spacing = max(1, len(plan) // (len(tasks) + 1))

    def need(p, unit):
        if (p, unit) in arrived:
            return
        arrived.add((p, unit))
        if unit != (0, 0, 0):
            arriving(p, unit).wait_recv()
        late.append((p, unit))

    late = []
    for i, (p, stage, unit) in enumerate(plan):
        if (i + 1) % spacing == 0 and tasks:
            tasks.pop(0)()
        need(p, unit)
        move = sending(p, stage, unit)
        move.start()
        started.append(move)
        while late:
            item = late.pop()
            move = pass_over(*item)
            move.start()
            started.append(move)
    for task in tasks:
        task()
    vector = remote(split_ref, split_out.at[tp], here.at[1], here.at[2], dp, 1 - tp)
    vector.start()
    mine = pltpu.make_async_copy(
        own_ref, out_ref.at[tp, pl.ds(pl.multiple_of(dp * rows, 16), rows)], here.at[0]
    )
    mine.start()
    split_out[tp] = split_ref[...]
    for p, unit in numbers:
        need(p, unit)
        while late:
            item = late.pop()
            move = pass_over(*item)
            move.start()
            started.append(move)
    for p, unit in numbers:
        taken_over(p, unit).wait_recv()
    for move in started:
        move.wait_send()
    for copy in leave:
        copy.wait()
    remote(split_ref, split_out.at[1 - tp], here.at[1], here.at[2], dp, 1 - tp).wait()
    mine.wait()


def gather_weights(sizes, own, split, stream, seed, rows_padded):
    dp_count = sizes[0] * sizes[1] * sizes[2]
    rows, side = own.shape
    parts = part_table(sizes, rows)
    plan = gather_plan(sizes, parts)
    units = 3 * dp_count
    anyspace = pl.BlockSpec(memory_space=pl.ANY)
    vmem = pl.BlockSpec(memory_space=pltpu.VMEM)
    sd = jax.ShapeDtypeStruct
    tokens, images, width = stream.shape
    flat = (tokens * images, width)
    mine = (images // 2, rows_padded, width)
    dma = pltpu.SemaphoreType.DMA
    return pl.pallas_call(
        functools.partial(gather_kernel, sizes, parts, plan),
        in_specs=[vmem, vmem, anyspace, anyspace],
        out_specs=[anyspace, vmem, anyspace, anyspace],
        out_shape=[
            sd((2, dp_count * rows, side), BF16),
            sd((2,) + split.shape, split.dtype),
            sd(mine, BF16),
            sd(mine, F32),
        ],
        scratch_shapes=[
            pltpu.VMEM((rows, side), BF16),
            pltpu.VMEM(flat, BF16),
            pltpu.VMEM((width // 128, tokens * images, 128), F32),
            pltpu.VMEM((width // 128, tokens * images, 128), F32),
            pltpu.VMEM(mine, BF16),
            pltpu.VMEM(mine, F32),
            dma((units,)),
            dma((units,)),
            dma((units,)),
            dma((units,)),
            dma((3,)),
            dma((4 + width // 128,)),
        ],
        compiler_params=pltpu.CompilerParams(
            collective_id=0, has_side_effects=True, vmem_limit_bytes=VMEM_LIMIT
        ),
        name="gather_weights",
    )(own, split, stream.reshape(flat), seed.reshape(flat))


def reduce_kernel(
    sizes, parts, plan, layer_count, target_ref, vec_ref, live_ref, block_ref, grad_ref,
    sum_ref, vec_out, square_out, block_out, grad_out,
    own, other, pieces, tiles, far_tiles, tile_pieces, full,
    load, over_send, over_recv, send, recv, tile_send, tile_recv, hop_send, hop_recv, image_sems,
):
    place = Place(sizes)
    dp, tp = place.dp, place.tp
    rows, side = sum_ref.shape
    moves = [(p, stage, one_on(unit, stage), unit) for p, stage, unit in reversed(plan)]
    order_used = []
    for p, stage, unit, _ in moves:
        if (p, unit) not in order_used:
            order_used.append((p, unit))
    for p in range(len(parts)):
        order_used.append((p, (0, 0, 0)))
    numbers = {item: i for i, item in enumerate(order_used)}
    landing = {}
    offset = 0
    inbound = {item: [] for item in order_used}
    for i, (p, stage, unit, to) in enumerate(moves):
        landing[i] = (offset, parts[p][2])
        offset += parts[p][2]
        inbound[(p, to)].append(i)

    def row_range(p, unit):
        order, start, length = parts[p]
        owner = place.behind(order, unit, 1)
        return pl.ds(pl.multiple_of(owner * rows + start, 16), length)

    def loading(item):
        span = row_range(*item)
        n = numbers[item]
        return pltpu.make_async_copy(target_ref.at[tp, span], own.at[span], load.at[n])

    def passing(item):
        span = row_range(*item)
        n = numbers[item]
        return remote(
            target_ref.at[1 - tp, span], other.at[span], over_send.at[n], over_recv.at[n], dp, 1 - tp
        )

    def sending(i):
        p, stage, unit, _ = moves[i]
        start, length = landing[i]
        return remote(
            own.at[row_range(p, unit)],
            pieces.at[pl.ds(start, length)],
            send.at[i],
            recv.at[i],
            place.along(parts[p][0][stage], 1),
            tp,
        )

    def combine(item, final):
        p, unit = item
        order, start, length = parts[p]
        owner = place.behind(order, unit, 1)
        base = owner * rows + start
        froms = [landing[i][0] for i in inbound[item]]
        step = math.gcd(length, 64)

        def body(k, carry):
            at = pl.ds(pl.multiple_of(base + k * step, 16), step)
            total = own[at, :].astype(F32) + other[at, :].astype(F32)
            for place_from in froms:
                got = pieces[pl.ds(pl.multiple_of(place_from + k * step, 16), step), :]
                total = total + got.astype(F32)
            if final:
                sum_ref[pl.ds(pl.multiple_of(start + k * step, 16), step), :] = total
            else:
                own[at, :] = total.astype(BF16)
            return carry

        lax.fori_loop(0, length // step, body, 0)

    dp_count = sizes[0] * sizes[1] * sizes[2]
    lanes = tiles.shape[2]
    chunks = vec_ref.shape[1] // lanes
    square_row = chunks
    riding = [i for i in range(len(moves)) if moves[i][0] == 1]

    def tile_of(p, unit):
        return tp * dp_count + place.behind(parts[p][0], unit, 1)

    def tile_over():
        return remote(
            tiles.at[pl.ds((1 - tp) * dp_count, dp_count)],
            far_tiles,
            tile_send.at[len(riding)],
            tile_recv.at[len(riding)],
            dp,
            1 - tp,
        )

    def tile_sending(i):
        p, stage, unit, _ = moves[i]
        n = riding.index(i)
        return remote(
            tiles.at[tile_of(p, unit)],
            tile_pieces.at[n],
            tile_send.at[n],
            tile_recv.at[n],
            place.along(parts[p][0][stage], 1),
            tp,
        )

    def tile_combine(item):
        at = tile_of(*item)
        total = tiles[at] + far_tiles[place.behind(parts[1][0], item[1], 1)]
        for j in inbound[item]:
            tile_sending(j).wait_recv()
            total = total + tile_pieces[riding.index(j)]
        tiles[at] = total

    hops = []
    for d in (2, 1, 0):
        reach = 1
        while reach < sizes[d]:
            bit = place.at[d] // reach % 2
            there = place.at[d] + reach * (1 - 2 * bit)
            coords = [there if e == d else place.at[e] for e in range(3)]
            stride = (sizes[1] * sizes[2], sizes[2], 1)[d]
            low = dp // (stride * reach) * (stride * reach)
            hops.append(((coords[0] * sizes[1] + coords[1]) * sizes[2] + coords[2], tp, stride * reach, low))
            reach *= 2

    def hop_copy(k):
        far_dp, far_tp, span, low = hops[k]
        region = full.at[:, pl.ds(low, span)]
        return remote(region, region, hop_send.at[k], hop_recv.at[k], far_dp, far_tp)

    def hop_arrival(k):
        far_dp, far_tp, span, low = hops[k]
        region = full.at[:, pl.ds(far_dp // span * span, span)]
        return remote(region, region, hop_send.at[k], hop_recv.at[k], far_dp, far_tp)

    def swap_copy(share):
        region = full.at[share, dp]
        return remote(region, region, hop_send.at[len(hops)], hop_recv.at[len(hops)], dp, 1 - tp)

    tiles[...] = jnp.zeros_like(tiles)
    for r in range(vec_ref.shape[0]):
        for i in range(chunks):
            tiles[r, i : i + 1, :] = vec_ref[r : r + 1, i * lanes : (i + 1) * lanes]
    greet(place)
    tile_over().start()
    for item in order_used:
        loading(item).start()
        passing(item).start()
    combined = set()
    tile_over().wait_recv()
    for i, (p, stage, unit, to) in enumerate(moves):
        item = (p, unit)
        if item not in combined:
            combined.add(item)
            loading(item).wait()
            passing(item).wait_recv()
            for j in inbound[item]:
                sending(j).wait_recv()
            combine(item, False)
            if p == 1:
                tile_combine(item)
        sending(i).start()
        if p == 1:
            tile_sending(i).start()
    half = block_out.shape[0] // 2

    def image_copy(n, ref, share):
        region = ref.at[pl.ds(share * half, half)]
        return remote(region, region, image_sems.at[2 * n], image_sems.at[2 * n + 1], dp, 1 - tp)

    for n, ref in enumerate((block_out, grad_out)):
        image_copy(n, ref, tp).start()
    for p in range(len(parts)):
        item = (p, (0, 0, 0))
        loading(item).wait()
        passing(item).wait_recv()
        for j in inbound[item]:
            sending(j).wait_recv()
        combine(item, True)
    slot_count = live_ref.shape[0]
    squares = jnp.zeros((1, lanes), F32)
    for n in range(slot_count):
        block = sum_ref[n * side : (n + 1) * side, :]
        square = jnp.sum(jnp.sum(block * block, axis=0, keepdims=True), axis=1, keepdims=True)
        squares = squares + jnp.where(live_ref[n, 0:1, :] > 0, square, 0.0)
    tile_combine((1, (0, 0, 0)))
    full[tp, dp] = tiles[tp * dp_count + dp]
    full[tp, dp, square_row : square_row + 1, :] = squares
    swap_copy(tp).start()
    swap_copy(1 - tp).wait_recv()
    for k in range(len(hops)):
        hop_copy(k).start()
        hop_arrival(k).wait_recv()
    total = full[0, 0]
    for n in range(1, 2 * dp_count):
        total = total + full[n // dp_count, n % dp_count]
    squares = total[square_row : square_row + 1, :]
    for r in range(vec_ref.shape[0]):
        for i in range(chunks):
            vec_out[r : r + 1, i * lanes : (i + 1) * lanes] = full[r // dp_count, r % dp_count, i : i + 1, :]
    lane = lax.broadcasted_iota(jnp.int32, (1, lanes), 1)
    per_layer = vec_ref.shape[0] // layer_count
    for layer in range(layer_count):
        block = vec_out[layer * per_layer : (layer + 1) * per_layer, :]
        square = jnp.sum(jnp.sum(block * block, axis=0, keepdims=True), axis=1, keepdims=True)
        squares = squares + jnp.where(lane == layer, square, 0.0)
    square_out[...] = jnp.broadcast_to(squares, square_out.shape)
    for item in order_used:
        passing(item).wait_send()
    for i in range(len(moves)):
        sending(i).wait_send()
    tile_over().wait_send()
    for i in riding:
        tile_sending(i).wait_send()
    swap_copy(tp).wait_send()
    for k in range(len(hops)):
        hop_copy(k).wait_send()
    for n, ref in enumerate((block_out, grad_out)):
        image_copy(n, ref, tp).wait_send()
        image_copy(n, ref, 1 - tp).wait_recv()


def reduce_gradients(sizes, layer_count, slot_count, target, vectors, live_tile, block_own, grad_own):
    dp_count = sizes[0] * sizes[1] * sizes[2]
    side = target.shape[-1]
    rows = slot_count * side
    target = target.reshape(2, dp_count * rows, side)
    parts = part_table(sizes, rows)
    plan = gather_plan(sizes, parts)
    hops = 1 + sum(n.bit_length() - 1 for n in sizes)
    riding = sum(1 for p, _, _ in plan if p == 1)
    units = 3 * dp_count
    landing = sum(parts[p][2] for p, _, _ in plan)
    anyspace = pl.BlockSpec(memory_space=pl.ANY)
    vmem = pl.BlockSpec(memory_space=pltpu.VMEM)
    sd = jax.ShapeDtypeStruct
    dma = pltpu.SemaphoreType.DMA
    return pl.pallas_call(
        functools.partial(reduce_kernel, sizes, parts, plan, layer_count),
        in_specs=[anyspace, vmem, vmem, anyspace, anyspace],
        out_specs=[vmem, vmem, vmem, anyspace, anyspace],
        out_shape=[
            sd((rows, side), F32),
            sd(vectors.shape, F32),
            sd(live_tile.shape[1:], F32),
            sd(block_own.shape, F32),
            sd(block_own.shape, F32),
        ],
        scratch_shapes=[
            pltpu.VMEM((dp_count * rows, side), BF16),
            pltpu.VMEM((dp_count * rows, side), BF16),
            pltpu.VMEM((landing, side), BF16),
            pltpu.VMEM((2 * dp_count,) + live_tile.shape[1:], F32),
            pltpu.VMEM((dp_count,) + live_tile.shape[1:], F32),
            pltpu.VMEM((riding,) + live_tile.shape[1:], F32),
            pltpu.VMEM((2, dp_count) + live_tile.shape[1:], F32),
            dma((units,)),
            dma((units,)),
            dma((units,)),
            dma((len(plan),)),
            dma((len(plan),)),
            dma((riding + 1,)),
            dma((riding + 1,)),
            dma((hops,)),
            dma((hops,)),
            dma((4,)),
        ],
        input_output_aliases={3: 3, 4: 4},
        compiler_params=pltpu.CompilerParams(
            collective_id=1, has_side_effects=True, vmem_limit_bytes=VMEM_LIMIT
        ),
        name="reduce_gradients",
    )(target, vectors, live_tile, block_own, grad_own)


def plain_update(gradient, weight, first_state, second_state, step_rate):
    first_new = MOMENT_DECAY * first_state + (1.0 - MOMENT_DECAY) * gradient
    second_new = MOMENT_DECAY * second_state + (1.0 - MOMENT_DECAY) * gradient * gradient
    stepped = first_new / CORRECTION / (jnp.sqrt(second_new / CORRECTION) + ADAM_EPSILON)
    return (weight - step_rate * stepped, first_new, second_new)


def params():
    return pltpu.CompilerParams(vmem_limit_bytes=VMEM_LIMIT, dimension_semantics=("arbitrary",))


def layer_gradients(layer, meta, kept, target, slot_total, side, share_count):
    names = ("a", "dqkv", "mixed", "dhr", "c", "du", "act", "dyr")
    ops = [kept[name].reshape(-1, kept[name].shape[-1]) for name in names]
    tokens, width = ops[0].shape
    ratio = ops[5].shape[1] // width
    pieces = width // side

    def clip(s, low, count):
        return jnp.minimum(jnp.maximum(s - low, 0), count - 1)

    block = (tokens, width)
    maps = [
        lambda s, meta: (0, 0),
        lambda s, meta: (0, clip(s, 0, 3)),
        lambda s, meta: (0, 0),
        lambda s, meta: (0, 0),
        lambda s, meta: (0, 0),
        lambda s, meta: (0, clip(s, 4, ratio)),
        lambda s, meta: (0, clip(s, 4 + ratio, ratio)),
        lambda s, meta: (0, 0),
    ]
    in_specs = [pl.BlockSpec(block, index) for index in maps]
    alias = {}
    if target is not None:
        in_specs.append(pl.BlockSpec(memory_space=pl.ANY))
        ops.append(target)
        alias = {len(ops): 0}
    grid = pltpu.PrefetchScalarGridSpec(
        num_scalar_prefetch=1,
        grid=(4 + 2 * ratio,),
        in_specs=in_specs,
        out_specs=pl.BlockSpec(memory_space=pl.ANY),
        scratch_shapes=[
            pltpu.VMEM((width, tokens), BF16),
            pltpu.VMEM((2, width, width), BF16),
            pltpu.SemaphoreType.DMA((2,)),
        ],
    )
    return pl.pallas_call(
        functools.partial(gradient_kernel, layer, pieces, ratio),
        grid_spec=grid,
        out_shape=jax.ShapeDtypeStruct((share_count, slot_total, side, side), BF16),
        input_output_aliases=alias,
        compiler_params=params(),
        name=f"gradients{layer}",
    )(meta, *ops)


def adam(layer_count, step_rate, live, squares, gradient, weight, left, right, first, second):
    count, _, side, _ = weight.shape
    spec = pl.BlockSpec((1, 1, side, side), lambda i: (i, 0, 0, 0))
    smem = pl.BlockSpec(memory_space=pltpu.SMEM)
    out = jax.ShapeDtypeStruct(weight.shape, F32)
    return pl.pallas_call(
        functools.partial(adam_kernel, layer_count, step_rate),
        grid=(count,),
        in_specs=[smem, pl.BlockSpec(squares.shape, lambda i: (0, 0)), pl.BlockSpec((1, side, side), lambda i: (i, 0, 0))] + [spec] * 5,
        out_specs=[spec] * 3,
        out_shape=[out] * 3,
        compiler_params=params(),
        name="adam",
    )(live, squares, gradient, weight, left, right, first, second)


def shards(
    block_input,
    cotangent,
    mask_patches,
    owners,
    master_slots,
    left_bases,
    right_bases,
    first_moment,
    second_moment,
    shared_vectors,
    shared_first,
    shared_second,
    split_vectors,
    split_first,
    split_second,
):
    slot_count = master_slots.shape[0]
    side = master_slots.shape[-1]
    layer_count = shared_vectors.shape[0]
    width = shared_vectors.shape[2]
    half = split_vectors.shape[2]
    ratio = split_vectors.shape[1] - 2
    block_total = owners.shape[0]
    per_layer = block_total // layer_count
    image_total, seq = block_input.shape[:2]
    dp_count = lax.axis_size("dp")
    tp_count = lax.axis_size("tp")
    count = image_total // tp_count
    rows = round_up(seq, 16)
    keys = round_up(seq, 128)
    slot_total = dp_count * slot_count
    dp_rank = lax.axis_index("dp")
    tp_rank = lax.axis_index("tp")
    slot_index = positions(owners, slot_count)
    meta = jnp.concatenate([slot_index, tp_rank[None].astype(jnp.int32)])
    place = block_total

    sizes = line_sizes(dp_count)
    own = master_slots.reshape(slot_count * side, side)
    blocks, split_pair, stream, seed = gather_weights(
        sizes,
        own,
        split_vectors,
        block_input.transpose(1, 0, 2),
        cotangent.transpose(1, 0, 2),
        rows,
    )
    blocks = blocks.reshape(tp_count, slot_total, side, side)
    split_all = jnp.concatenate([split_pair[t] for t in range(tp_count)], axis=2)
    hits = mask_patches[:, None, :]

    kept, output_own, grad_own, vectors = run_layers(
        count, seq, rows, keys, meta, place, stream, seed, hits, shared_vectors, split_all, blocks
    )
    target = None
    for layer in reversed(range(layer_count)):
        target = layer_gradients(layer, meta, kept[layer], target, slot_total, side, tp_count)
    mine_ids = dp_rank * slot_count + jnp.arange(slot_count, dtype=jnp.int32)
    matches = slot_index[None, :] == mine_ids[:, None]
    live = jnp.any(matches, axis=1)
    block_layer = jnp.arange(block_total, dtype=jnp.int32) // per_layer
    owned_layer = jnp.sum(jnp.where(matches, block_layer[None, :], 0), axis=1)
    lanes = lax.broadcasted_iota(jnp.int32, (slot_count, 8, 128), 2)
    live_tile = jnp.where((lanes == owned_layer[:, None, None]) & live[:, None, None], 1.0, 0.0)
    reduced, vector_sum, square_tile, block_output, input_grad = reduce_gradients(
        sizes, layer_count, slot_count, target, vectors.reshape(-1, width), live_tile, output_own, grad_own
    )

    reduced = reduced.reshape(slot_count, side, side)
    vector_sum = vector_sum.reshape(layer_count, -1, width)
    shared_sum = vector_sum[:, :6]
    split_full = vector_sum[:, 6 : 8 + ratio]
    split_sum = lax.dynamic_slice_in_dim(split_full, tp_rank * half, half, axis=2)
    squares = square_tile[0, :layer_count]
    layer_norms = jnp.sqrt(squares)
    global_norm = jnp.sqrt(jnp.sum(squares))
    factor = CLIP_NORM / jnp.maximum(global_norm, CLIP_NORM)
    step_rate = 0.5 / math.sqrt(width)
    new_master, new_first, new_second = adam(
        layer_count, step_rate, live.astype(jnp.int32), square_tile, reduced, master_slots, left_bases, right_bases,
        first_moment, second_moment,
    )
    new_shared, new_shared_first, new_shared_second = plain_update(
        shared_sum * factor, shared_vectors, shared_first, shared_second, VECTOR_RATE
    )
    new_split, new_split_first, new_split_second = plain_update(
        split_sum * factor, split_vectors, split_first, split_second, VECTOR_RATE
    )
    return (
        block_output,
        input_grad,
        new_master,
        new_first,
        new_second,
        new_shared,
        new_shared_first,
        new_shared_second,
        new_split,
        new_split_first,
        new_split_second,
        layer_norms,
        global_norm,
    )


def solution(mesh):
    sharded = P("dp", None, None)
    slots = P("dp", "tp", None, None)
    split = P(None, None, "tp")
    return jax.shard_map(
        shards,
        mesh=mesh,
        in_specs=(sharded, sharded, P("dp", None), P())
        + (slots,) * 5
        + (P(),) * 3
        + (split,) * 3,
        out_specs=(sharded, sharded) + (slots,) * 3 + (P(),) * 3 + (split,) * 3 + (P(), P()),
        check_vma=False,
    )
```

```python
import functools
import math

import jax
import jax.numpy as jnp
from jax import lax
from jax.experimental import pallas as pl
from jax.experimental.pallas import tpu as pltpu
from jax.sharding import PartitionSpec as P

DH = 64
GROUP = 4
LANES = GROUP * DH
CLIP_NORM = 1.0
MOMENT_DECAY = 0.5
CORRECTION = 0.9375
ADAM_EPSILON = 1e-08
WEIGHT_DECAY = 0.05
LAYER_EPSILON = 1e-06
VECTOR_RATE = 0.2
VMEM_LIMIT = 60 * 1024 * 1024
F32 = jnp.float32
BF16 = jnp.bfloat16


def nn(a, b):
    return lax.dot_general(a, b, (((1,), (0,)), ((), ())), preferred_element_type=F32)


def nt(a, b):
    return lax.dot_general(a, b, (((1,), (1,)), ((), ())), preferred_element_type=F32)


def tn(a, b):
    return lax.dot_general(a, b, (((0,), (0,)), ((), ())), preferred_element_type=F32)


def round_up(number, step):
    return (number + step - 1) // step * step


def positions(owners, slot_count):
    block_ids = jnp.arange(owners.shape[0], dtype=jnp.int32)
    same_owner = owners[None, :] == owners[:, None]
    earlier = block_ids[None, :] < block_ids[:, None]
    ranking = jnp.sum((same_owner & earlier).astype(jnp.int32), axis=1)
    return owners * slot_count + ranking


def normalized(v):
    center = jnp.mean(v, axis=-1, keepdims=True)
    spread = v - center
    second = jnp.mean(spread * spread, axis=-1, keepdims=True)
    inverse = lax.rsqrt(second + LAYER_EPSILON)
    return spread * inverse, inverse


def norm_back(grad, unit, inverse, gain):
    scaled = grad * gain
    first = jnp.mean(scaled, axis=-1, keepdims=True)
    second = jnp.mean(scaled * unit, axis=-1, keepdims=True)
    return inverse * (scaled - first - unit * second)


def gelu_pair(u):
    bell = jnp.exp(u * u * -0.5)
    mass = 0.5 + 0.5 * lax.erf(u * math.sqrt(0.5))
    return u * mass, mass + u * bell * (1.0 / math.sqrt(2.0 * math.pi))


def weight_copies(meta, layer, blocks, wp, wo, wu, wd, sems):
    side = blocks.shape[-1]
    width = wo.shape[0]
    pieces = width // side
    ratio = wd.shape[0] // width
    per_layer = pieces * (4 + 2 * ratio)
    base = layer * per_layer
    jobs = [[], [], [], []]

    def add(kind, target, b, row, col):
        for t in range(blocks.shape[0]):
            r, c = row(t), col(t)
            jobs[kind].append(
                pltpu.make_async_copy(
                    blocks.at[t, meta[base + b]],
                    target.at[pl.ds(r, side), pl.ds(c, side)],
                    sems.at[kind],
                )
            )

    for r in range(pieces):
        for p in range(3):
            add(0, wp, r * 3 + p, lambda t: r * side, lambda t: p * width + t * side)
    for c in range(pieces):
        add(1, wo, 3 * pieces + c, lambda t: t * side, lambda t: c * side)
    for r in range(pieces):
        for j in range(ratio):
            add(
                2, wu, 4 * pieces + r * ratio + j, lambda t: r * side, lambda t: j * width + t * side
            )
    for j in range(ratio):
        for c in range(pieces):
            add(
                3,
                wd,
                (4 + ratio) * pieces + j * pieces + c,
                lambda t: j * width + t * side,
                lambda t: c * side,
            )
    return jobs


def head_masks():
    lane = lax.broadcasted_iota(jnp.int32, (1, LANES), 1)
    return [(lane // DH) == h for h in range(GROUP)]


def spread_heads(masks, value):
    zero = jnp.zeros((), value.dtype)
    return jnp.concatenate([jnp.where(m, value, zero) for m in masks], axis=0)


def saved_columns(width, ratio):
    left = (("a", 1), ("mixed", 1), ("c", 1), ("act", ratio))
    right = (("dqkv", 3), ("dhr", 1), ("du", ratio), ("dyr", 1))
    table = {}
    for side, names in enumerate((left, right)):
        start = 0
        for name, size in names:
            table[name] = (side, start * width, size * width)
            start += size
    return table, (3 + ratio) * width, (5 + ratio) * width


def layers_kernel(layer_count, seq, rows, keys, meta, x_ref, dy_ref, hits_ref, shared_ref, split_ref, blocks, *rest):
    outs = rest[:2]
    y_ref, dx_ref, vec_ref = rest[2:5]
    rest = rest[5:]
    saves = rest[: 2 * layer_count]
    rest = rest[2 * layer_count :]
    weights = [rest[4 * n : 4 * n + 4] for n in range(layer_count)]
    rest = rest[4 * layer_count :]
    holds = [rest[7 * n : 7 * n + 7] for n in range(layer_count)]
    save_sems, weight_sems = rest[7 * layer_count :]
    width = x_ref.shape[2]
    ratio = split_ref.shape[1] - 2
    groups = width // LANES
    scale = 1.0 / math.sqrt(DH)
    step = pl.program_id(0)
    zero = jnp.zeros((), BF16)
    masks = head_masks()

    columns, _, _ = saved_columns(width, ratio)

    def saving(layer, side, i):
        n = 2 * layer + side
        return pltpu.make_async_copy(saves[n], outs[side].at[layer, i], save_sems.at[n])

    def free(side):
        @pl.when(step > 0)
        def _():
            for n in range(layer_count):
                saving(n, side, step - 1).wait()

    def send(side):
        for n in range(layer_count):
            saving(n, side, step).start()

    def buffer(layer, name):
        side, start, size = columns[name]
        return saves[2 * layer + side].at[:, pl.ds(start, size)]

    jobs = [
        weight_copies(meta, n, blocks, *weights[n], weight_sems.at[n]) for n in range(layer_count)
    ]

    def start(pairs):
        @pl.when(step == 0)
        def _():
            for n, kind in pairs:
                for job in jobs[n][kind]:
                    job.start()

    def ready(pairs):
        @pl.when(step == 0)
        def _():
            for n, kind in pairs:
                target = weights[n][kind]
                pltpu.make_async_copy(target, target, weight_sems.at[n, kind]).wait()

    start([(0, 0)])

    @pl.when(step == 0)
    def _():
        vec_ref[...] = jnp.zeros_like(vec_ref)
        for hold in holds:
            for ref in (hold[3], hold[4]):
                ref[rows:keys, :] = jnp.zeros((keys - rows, width), BF16)

    free(0)
    holds[0][0][...] = x_ref[0].astype(F32)
    real = lax.broadcasted_iota(jnp.int32, (1, keys), 1) < seq
    for n in range(layer_count):
        xs, hs, qs, ks, vs, ps, ss = holds[n]
        wp, wo, wu, wd = weights[n]
        unit, _ = normalized(xs[...])
        a = (unit * shared_ref[n, 0:1, :] + shared_ref[n, 1:2, :]).astype(BF16)
        buffer(n, "a")[...] = a
        if n == 0:
            ready([(0, 0)])
            start([(0, 1), (0, 2), (0, 3)])
        qs[...] = ((nn(a, wp[:, 0:width]) + split_ref[n, 0:1, :]) * scale).astype(BF16)
        ks[0:rows, :] = nn(a, wp[:, width : 2 * width]).astype(BF16)
        vs[0:rows, :] = (nn(a, wp[:, 2 * width :]) + split_ref[n, 1:2, :]).astype(BF16)
        mixed = buffer(n, "mixed")
        for g in range(groups):
            cols = slice(g * LANES, (g + 1) * LANES)
            scores = nt(spread_heads(masks, qs[:, cols]), ks[:, cols])
            scores = jnp.where(real, scores, -1e30)
            top = jnp.max(scores, axis=-1, keepdims=True)
            power = jnp.exp(scores - top)
            total = jnp.sum(power, axis=-1, keepdims=True)
            probs = (power * (1.0 / total)).astype(BF16)
            ps[g * GROUP * rows : (g + 1) * GROUP * rows, :] = probs
            v4 = vs[:, cols]
            mix = None
            for h in range(GROUP):
                part = nn(probs[h * rows : (h + 1) * rows, :], jnp.where(masks[h], v4, zero))
                mix = part if mix is None else mix + part
            mixed[:, cols] = mix.astype(BF16)
        if n == 0:
            ready([(0, 1), (0, 2), (0, 3)])
            start([(m, kind) for m in range(1, layer_count) for kind in range(4)])
        h = xs[...] + nn(mixed[...], wo[...]) + shared_ref[n, 2:3, :]
        hs[...] = h
        unit, _ = normalized(h)
        c = (unit * shared_ref[n, 3:4, :] + shared_ref[n, 4:5, :]).astype(BF16)
        buffer(n, "c")[...] = c
        y = h + shared_ref[n, 5:6, :]
        active = buffer(n, "act")
        for j in range(ratio):
            cols = slice(j * width, (j + 1) * width)
            u = nn(c, wu[:, cols]) + split_ref[n, 2 + j : 3 + j, :]
            act, slope = gelu_pair(u)
            act = act.astype(BF16)
            active[:, cols] = act
            ss[:, cols] = slope.astype(BF16)
            y = y + nn(act, wd[cols, :])
        if n + 1 < layer_count:
            holds[n + 1][0][...] = y
            ready([(n + 1, kind) for kind in range(4)])
        else:
            y_ref[0] = y[0:seq, :]

    send(0)
    free(1)
    wanted = lax.broadcasted_iota(jnp.int32, (rows, 1), 0)
    hit = jnp.max(jnp.where(hits_ref[0] + 1 == wanted, 1.0, 0.0), axis=-1, keepdims=True)
    dy = dy_ref[0] * hit
    for n in reversed(range(layer_count)):
        xs, hs, qs, ks, vs, ps, ss = holds[n]
        wp, wo, wu, wd = weights[n]

        def collect(row, value):
            vec_ref[n, row : row + 1, :] += jnp.sum(value, axis=0, keepdims=True)

        collect(5, dy)
        dyr = dy.astype(BF16)
        buffer(n, "dyr")[...] = dyr
        hidden = buffer(n, "du")
        dc = None
        for j in range(ratio):
            cols = slice(j * width, (j + 1) * width)
            du = (nt(dyr, wd[cols, :]) * ss[:, cols].astype(F32)).astype(BF16)
            hidden[:, cols] = du
            collect(8 + j, du.astype(F32))
            part = nt(du, wu[:, cols])
            dc = part if dc is None else dc + part
        unit, inverse = normalized(hs[...])
        collect(3, dc * unit)
        collect(4, dc)
        dh = dy + norm_back(dc, unit, inverse, shared_ref[n, 3:4, :])
        collect(2, dh)
        dhr = dh.astype(BF16)
        buffer(n, "dhr")[...] = dhr
        dmixed = nt(dhr, wo[...]).astype(BF16)
        back = buffer(n, "dqkv")
        for g in range(groups):
            cols = slice(g * LANES, (g + 1) * LANES)
            dm = spread_heads(masks, dmixed[:, cols])
            probs = ps[g * GROUP * rows : (g + 1) * GROUP * rows, :]
            k4 = ks[:, cols]
            dprobs = nt(dm, vs[:, cols])
            wide = probs.astype(F32)
            both = wide * dprobs
            ds = (both - wide * jnp.sum(both, axis=-1, keepdims=True)).astype(BF16)
            dv = tn(probs, dm)[0:rows, :].astype(BF16)
            dk = tn(ds, spread_heads(masks, qs[:, cols]))[0:rows, :].astype(BF16)
            dq = None
            for h in range(GROUP):
                part = nn(ds[h * rows : (h + 1) * rows, :], jnp.where(masks[h], k4, zero))
                dq = part if dq is None else dq + part
            back[:, cols] = (dq.astype(BF16).astype(F32) * scale).astype(BF16)
            back[:, width + g * LANES : width + (g + 1) * LANES] = dk
            back[:, 2 * width + g * LANES : 2 * width + (g + 1) * LANES] = dv
        dqkv = back[...]
        collect(6, dqkv[:, 0:width].astype(F32))
        collect(7, dqkv[:, 2 * width :].astype(F32))
        da = nt(dqkv, wp[...])
        unit, inverse = normalized(xs[...])
        collect(0, da * unit)
        collect(1, da)
        dy = dh + norm_back(da, unit, inverse, shared_ref[n, 0:1, :])
    dx_ref[0] = dy[0:seq, :]
    send(1)

    @pl.when(step == pl.num_programs(0) - 1)
    def _():
        for n in range(layer_count):
            for side in range(2):
                saving(n, side, step).wait()


def run_layers(count, seq, rows, keys, meta, place, stream, seed, hits, shared, split, blocks):
    layer_count, _, width = shared.shape
    ratio = split.shape[1] - 2
    heads = width // DH
    sd = jax.ShapeDtypeStruct
    _, *widths = saved_columns(width, ratio)
    anyspace = pl.BlockSpec(memory_space=pl.ANY)
    outs = [sd((layer_count, count, rows, w), BF16) for w in widths]
    outs += [sd((2 * count, seq, width), F32)] * 2 + [sd((layer_count, 16, width), F32)]
    image = pl.BlockSpec((1, seq, width), lambda i, meta: (meta[place] * count + i, 0, 0))

    def shifted(shape):
        return pl.BlockSpec((1,) + tuple(shape[1:]), lambda i, meta: (meta[place] * count + i, 0, 0))

    def whole(shape):
        return pl.BlockSpec(tuple(shape), lambda i, meta: (0,) * len(shape))

    vmem = pltpu.VMEM
    scratch = [vmem((rows, w), BF16) for w in widths] * layer_count
    scratch += [
        vmem((width, 3 * width), BF16),
        vmem((width, width), BF16),
        vmem((width, ratio * width), BF16),
        vmem((ratio * width, width), BF16),
    ] * layer_count
    scratch += [
        vmem((rows, width), F32),
        vmem((rows, width), F32),
        vmem((rows, width), BF16),
        vmem((keys, width), BF16),
        vmem((keys, width), BF16),
        vmem((heads * rows, keys), BF16),
        vmem((rows, ratio * width), BF16),
    ] * layer_count
    scratch += [
        pltpu.SemaphoreType.DMA((2 * layer_count,)),
        pltpu.SemaphoreType.DMA((layer_count, 4)),
    ]
    grid = pltpu.PrefetchScalarGridSpec(
        num_scalar_prefetch=1,
        grid=(count,),
        in_specs=[
            pl.BlockSpec((1, rows, width), lambda i, meta: (i, 0, 0)),
            pl.BlockSpec((1, rows, width), lambda i, meta: (i, 0, 0)),
            shifted(hits.shape),
            whole(shared.shape),
            whole(split.shape),
            anyspace,
        ],
        out_specs=[anyspace] * len(widths) + [image, image, whole((layer_count, 16, width))],
        scratch_shapes=scratch,
    )
    res = pl.pallas_call(
        functools.partial(layers_kernel, layer_count, seq, rows, keys),
        grid_spec=grid,
        out_shape=outs,
        compiler_params=params(),
        name="layers",
    )(meta, stream, seed, hits, shared, split, blocks)
    return res


def gradient_step(s, ratio):
    steps = 4 + 2 * ratio
    q = s % steps
    left = jnp.where(q < 3, 0, jnp.where(q < 4, 1, jnp.where(q < 4 + ratio, 2, q - 1 - ratio)))
    right = jnp.minimum(q, 4 + ratio)
    return s // steps, q, left, right


def gradient_kernel(pieces, ratio, meta, left_ref, right_ref, out_ref, turned, stage, sems):
    side = out_ref.shape[-1]
    step = pl.program_id(0)
    layer, q, _, _ = gradient_step(step, ratio)
    base = layer * pieces * (4 + 2 * ratio)
    slot = step % 2
    by_rows = (q == 3) | (q >= 4 + ratio)

    def block_of(i, j):
        return base + jnp.where(
            q < 3,
            i * 3 + q,
            jnp.where(
                q < 4,
                3 * pieces + j,
                jnp.where(
                    q < 4 + ratio,
                    4 * pieces + i * ratio + q - 4,
                    (4 + ratio) * pieces + (q - 4 - ratio) * pieces + j,
                ),
            ),
        )

    def drain(buffer):
        pltpu.make_async_copy(stage.at[buffer], stage.at[buffer], sems.at[buffer]).wait()

    @pl.when(step >= 2)
    def _():
        drain(slot)

    @pl.when((q == 0) | ((q >= 3) & (q <= 4)) | (q >= 4 + ratio))
    def _():
        turned[...] = left_ref[0].T

    stage[slot] = nn(turned[...], right_ref[0]).astype(BF16)
    for i in range(pieces):
        for j in range(pieces):
            pltpu.make_async_copy(
                stage.at[slot, pl.ds(i * side, side), pl.ds(j * side, side)],
                out_ref.at[jnp.where(by_rows, i, j), meta[block_of(i, j)]],
                sems.at[slot],
            ).start()

    @pl.when(step == pl.num_programs(0) - 1)
    def _():
        drain(1 - slot)
        drain(slot)


def adam_kernel(layer_count, step_rate, live_ref, square_ref, g_ref, w_ref, l_ref, r_ref, m_ref, s_ref, w_out, m_out, s_out):
    lane = lax.broadcasted_iota(jnp.int32, (1, square_ref.shape[1]), 1)
    total = jnp.sum(jnp.where(lane < layer_count, square_ref[0:1, :], 0.0), axis=1, keepdims=True)
    factor = CLIP_NORM / jnp.maximum(jnp.sqrt(total), CLIP_NORM)
    slot = pl.program_id(0)
    alive = live_ref[slot] > 0
    weight = w_ref[0, 0]
    left = l_ref[0, 0].astype(BF16)
    right = r_ref[0, 0].astype(BF16)
    turned = nn(tn(left, g_ref[0].astype(BF16)).astype(BF16), right) * factor
    first = MOMENT_DECAY * m_ref[0, 0] + (1.0 - MOMENT_DECAY) * turned
    second = MOMENT_DECAY * s_ref[0, 0] + (1.0 - MOMENT_DECAY) * turned * turned
    stepped = first / CORRECTION / (jnp.sqrt(second / CORRECTION) + ADAM_EPSILON)
    back = nt(nn(left, stepped.astype(BF16)).astype(BF16), right)
    w_out[0, 0] = jnp.where(alive, weight - step_rate * (back + WEIGHT_DECAY * weight), weight)
    m_out[0, 0] = jnp.where(alive, first, m_ref[0, 0])
    s_out[0, 0] = jnp.where(alive, second, s_ref[0, 0])


def line_sizes(dp_count):
    if dp_count == 16:
        return (4, 2, 2)
    if dp_count == 64:
        return (4, 4, 4)
    return (dp_count, 1, 1)


def part_table(sizes, total_rows):
    step = 16
    if sizes[0] > sizes[1]:
        large = int(total_rows * 0.39) // step * step
        lengths = (total_rows - 2 * large, large, large)
        orders = ((2, 1, 0), (0, 1, 2), (0, 2, 1))
    else:
        small = total_rows // 3 // step * step
        lengths = (total_rows - 2 * small, small, small)
        orders = ((2, 1, 0), (0, 2, 1), (1, 0, 2))
    offsets = (0, lengths[0], lengths[0] + lengths[1])
    return [(orders[i], offsets[i], lengths[i]) for i in range(3)]


def gather_plan(sizes, parts):
    ready, moves, plan = {}, [], []
    free = [0.0] * 3
    for p, (order, _, _) in enumerate(parts):
        n = [sizes[d] for d in order]
        ready[(p, (0, 0, 0))] = 0.0
        for a in range(n[0]):
            if a + 1 < n[0]:
                moves.append((p, 0, (a, 0, 0)))
            for b in range(n[1]):
                if b + 1 < n[1]:
                    moves.append((p, 1, (a, b, 0)))
                for c in range(n[2] - 1):
                    moves.append((p, 2, (a, b, c)))
    while moves:
        choices = []
        for move in moves:
            p, stage, unit = move
            if (p, unit) in ready:
                start = max(ready[(p, unit)], free[parts[p][0][stage]])
                choices.append((start, stage, p, unit))
        start, stage, p, unit = min(choices)
        end = start + parts[p][2]
        free[parts[p][0][stage]] = end
        ready[(p, one_on(unit, stage))] = end + 60.0
        plan.append((p, stage, unit))
        moves.remove((p, stage, unit))
    return plan


def one_on(unit, stage):
    return tuple(v + (1 if i == stage else 0) for i, v in enumerate(unit))


class Place:
    def __init__(self, sizes):
        self.sizes = sizes
        self.dp = lax.axis_index("dp")
        self.tp = lax.axis_index("tp")
        nz, ny, nx = sizes
        self.at = (self.dp // (ny * nx), self.dp // nx % ny, self.dp % nx)

    def shifted(self, offsets):
        nz, ny, nx = self.sizes
        z, y, x = [
            lax.rem(self.at[d] + (offsets[d] + self.sizes[d]) % self.sizes[d], self.sizes[d])
            for d in range(3)
        ]
        return (z * ny + y) * nx + x

    def along(self, dim, step):
        return self.shifted(tuple(step if d == dim else 0 for d in range(3)))

    def behind(self, order, unit, sign):
        offsets = [0, 0, 0]
        for d, v in zip(order, unit):
            offsets[d] = sign * v
        return self.shifted(tuple(offsets))


def greet(place):
    barrier = pltpu.get_barrier_semaphore()
    number = 1
    pl.semaphore_signal(
        barrier, inc=1, device_id=(place.dp, 1 - place.tp), device_id_type=pl.DeviceIdType.MESH
    )
    for d in range(3):
        for step in range(1, place.sizes[d]):
            number += 1
            pl.semaphore_signal(
                barrier,
                inc=1,
                device_id=(place.along(d, step), place.tp),
                device_id_type=pl.DeviceIdType.MESH,
            )
    pl.semaphore_wait(barrier, number)


def remote(src, dst, send, recv, dp, tp):
    return pltpu.make_async_remote_copy(
        src_ref=src,
        dst_ref=dst,
        send_sem=send,
        recv_sem=recv,
        device_id=(dp, tp),
        device_id_type=pl.DeviceIdType.MESH,
    )


def gather_kernel(
    sizes, parts, plan, master_ref, split_ref, x_ref, seed_ref, out_ref, split_out, x_out, seed_out,
    own_ref, x_in, x_wide, seed_in, x_own, seed_own, send, recv, over_send, over_recv, here, stream_sems,
):
    place = Place(sizes)
    dp, tp = place.dp, place.tp
    rows = own_ref.shape[0]
    dims = [n for n in sizes]
    numbers = {}
    for p, (order, _, _) in enumerate(parts):
        for a in range(dims[order[0]]):
            for b in range(dims[order[1]]):
                for c in range(dims[order[2]]):
                    numbers[(p, (a, b, c))] = len(numbers)

    def region(p, unit, share):
        order, start, length = parts[p]
        owner = place.behind(order, unit, -1)
        return out_ref.at[share, pl.ds(pl.multiple_of(owner * rows + start, 16), length)]

    def source(p, unit):
        if unit == (0, 0, 0):
            return own_ref.at[pl.ds(parts[p][1], parts[p][2])]
        return region(p, unit, tp)

    def pass_over(p, unit):
        n = numbers[(p, unit)]
        return remote(
            source(p, unit), region(p, unit, tp), over_send.at[n], over_recv.at[n], dp, 1 - tp
        )

    def taken_over(p, unit):
        n = numbers[(p, unit)]
        piece = region(p, unit, 1 - tp)
        return remote(piece, piece, over_send.at[n], over_recv.at[n], dp, 1 - tp)

    def arriving(p, unit):
        n = numbers[(p, unit)]
        piece = region(p, unit, tp)
        return remote(piece, piece, send.at[n], recv.at[n], dp, 1 - tp)

    def sending(p, stage, unit):
        n = numbers[(p, one_on(unit, stage))]
        target = place.along(parts[p][0][stage], 1)
        return remote(source(p, unit), region(p, unit, tp), send.at[n], recv.at[n], target, tp)

    own_ref[...] = master_ref[...].astype(BF16)
    greet(place)
    started = []
    arrived = set()
    count, padded = x_own.shape[:2]
    images = 2 * count
    seq = x_in.shape[0] // images
    strips, _, lanes = x_wide.shape
    fetch = [pltpu.make_async_copy(x_ref, x_in, stream_sems.at[0])] + [
        pltpu.make_async_copy(
            seed_ref.at[:, pl.ds(n * lanes, lanes)], seed_in.at[n], stream_sems.at[4 + n]
        )
        for n in range(strips)
    ]
    leave = [
        pltpu.make_async_copy(x_own, x_out, stream_sems.at[2]),
        pltpu.make_async_copy(seed_own, seed_out, stream_sems.at[3]),
    ]
    tail = seq // 16 * 16

    def widen():
        fetch[0].wait()
        for n in range(strips):
            x_wide[n] = x_in[:, n * lanes : (n + 1) * lanes].astype(F32)

    def pick(source, target, i):
        def go():
            target[i, tail:padded, :] = jnp.zeros((padded - tail, target.shape[2]), target.dtype)
            for n in range(strips):
                rows_of = source[n, pl.ds(tp * count + i, seq, stride=images), :]
                target[i, 0:seq, n * lanes : (n + 1) * lanes] = rows_of.astype(target.dtype)

        return go

    def leaving(n):
        return lambda: leave[n].start()

    tasks = [lambda: [copy.start() for copy in fetch], widen]
    tasks += [pick(x_wide, x_own, i) for i in range(count)] + [leaving(0), lambda: [copy.wait() for copy in fetch[1:]]]
    tasks += [pick(seed_in, seed_own, i) for i in range(count)] + [leaving(1)]
    spacing = max(1, len(plan) // (len(tasks) + 1))

    def need(p, unit):
        if (p, unit) in arrived:
            return
        arrived.add((p, unit))
        if unit != (0, 0, 0):
            arriving(p, unit).wait_recv()
        late.append((p, unit))

    late = []
    for i, (p, stage, unit) in enumerate(plan):
        if (i + 1) % spacing == 0 and tasks:
            tasks.pop(0)()
        need(p, unit)
        move = sending(p, stage, unit)
        move.start()
        started.append(move)
        while late:
            item = late.pop()
            move = pass_over(*item)
            move.start()
            started.append(move)
    for task in tasks:
        task()
    vector = remote(split_ref, split_out.at[tp], here.at[1], here.at[2], dp, 1 - tp)
    vector.start()
    mine = pltpu.make_async_copy(
        own_ref, out_ref.at[tp, pl.ds(pl.multiple_of(dp * rows, 16), rows)], here.at[0]
    )
    mine.start()
    split_out[tp] = split_ref[...]
    for p, unit in numbers:
        need(p, unit)
        while late:
            item = late.pop()
            move = pass_over(*item)
            move.start()
            started.append(move)
    for p, unit in numbers:
        taken_over(p, unit).wait_recv()
    for move in started:
        move.wait_send()
    for copy in leave:
        copy.wait()
    remote(split_ref, split_out.at[1 - tp], here.at[1], here.at[2], dp, 1 - tp).wait()
    mine.wait()


def gather_weights(sizes, own, split, stream, seed, rows_padded):
    dp_count = sizes[0] * sizes[1] * sizes[2]
    rows, side = own.shape
    parts = part_table(sizes, rows)
    plan = gather_plan(sizes, parts)
    units = 3 * dp_count
    anyspace = pl.BlockSpec(memory_space=pl.ANY)
    vmem = pl.BlockSpec(memory_space=pltpu.VMEM)
    sd = jax.ShapeDtypeStruct
    tokens, images, width = stream.shape
    flat = (tokens * images, width)
    mine = (images // 2, rows_padded, width)
    dma = pltpu.SemaphoreType.DMA
    return pl.pallas_call(
        functools.partial(gather_kernel, sizes, parts, plan),
        in_specs=[vmem, vmem, anyspace, anyspace],
        out_specs=[anyspace, vmem, anyspace, anyspace],
        out_shape=[
            sd((2, dp_count * rows, side), BF16),
            sd((2,) + split.shape, split.dtype),
            sd(mine, BF16),
            sd(mine, F32),
        ],
        scratch_shapes=[
            pltpu.VMEM((rows, side), BF16),
            pltpu.VMEM(flat, BF16),
            pltpu.VMEM((width // 128, tokens * images, 128), F32),
            pltpu.VMEM((width // 128, tokens * images, 128), F32),
            pltpu.VMEM(mine, BF16),
            pltpu.VMEM(mine, F32),
            dma((units,)),
            dma((units,)),
            dma((units,)),
            dma((units,)),
            dma((3,)),
            dma((4 + width // 128,)),
        ],
        compiler_params=pltpu.CompilerParams(
            collective_id=0, has_side_effects=True, vmem_limit_bytes=VMEM_LIMIT
        ),
        name="gather_weights",
    )(own, split, stream.reshape(flat), seed.reshape(flat))


def reduce_kernel(
    sizes, parts, plan, layer_count, target_ref, vec_ref, live_ref, block_ref, grad_ref,
    sum_ref, vec_out, square_out, block_out, grad_out,
    own, other, pieces, tiles, far_tiles, tile_pieces, full,
    load, over_send, over_recv, send, recv, tile_send, tile_recv, hop_send, hop_recv, image_sems,
):
    place = Place(sizes)
    dp, tp = place.dp, place.tp
    rows, side = sum_ref.shape
    moves = [(p, stage, one_on(unit, stage), unit) for p, stage, unit in reversed(plan)]
    order_used = []
    for p, stage, unit, _ in moves:
        if (p, unit) not in order_used:
            order_used.append((p, unit))
    for p in range(len(parts)):
        order_used.append((p, (0, 0, 0)))
    numbers = {item: i for i, item in enumerate(order_used)}
    landing = {}
    offset = 0
    inbound = {item: [] for item in order_used}
    for i, (p, stage, unit, to) in enumerate(moves):
        landing[i] = (offset, parts[p][2])
        offset += parts[p][2]
        inbound[(p, to)].append(i)

    def row_range(p, unit):
        order, start, length = parts[p]
        owner = place.behind(order, unit, 1)
        return pl.ds(pl.multiple_of(owner * rows + start, 16), length)

    def loading(item):
        span = row_range(*item)
        n = numbers[item]
        return pltpu.make_async_copy(target_ref.at[tp, span], own.at[span], load.at[n])

    def passing(item):
        span = row_range(*item)
        n = numbers[item]
        return remote(
            target_ref.at[1 - tp, span], other.at[span], over_send.at[n], over_recv.at[n], dp, 1 - tp
        )

    def sending(i):
        p, stage, unit, _ = moves[i]
        start, length = landing[i]
        return remote(
            own.at[row_range(p, unit)],
            pieces.at[pl.ds(start, length)],
            send.at[i],
            recv.at[i],
            place.along(parts[p][0][stage], 1),
            tp,
        )

    def combine(item, final):
        p, unit = item
        order, start, length = parts[p]
        owner = place.behind(order, unit, 1)
        base = owner * rows + start
        froms = [landing[i][0] for i in inbound[item]]
        step = math.gcd(length, 64)

        def body(k, carry):
            at = pl.ds(pl.multiple_of(base + k * step, 16), step)
            total = own[at, :].astype(F32) + other[at, :].astype(F32)
            for place_from in froms:
                got = pieces[pl.ds(pl.multiple_of(place_from + k * step, 16), step), :]
                total = total + got.astype(F32)
            if final:
                sum_ref[pl.ds(pl.multiple_of(start + k * step, 16), step), :] = total
            else:
                own[at, :] = total.astype(BF16)
            return carry

        lax.fori_loop(0, length // step, body, 0)

    dp_count = sizes[0] * sizes[1] * sizes[2]
    lanes = tiles.shape[2]
    chunks = vec_ref.shape[1] // lanes
    square_row = chunks
    riding = [i for i in range(len(moves)) if moves[i][0] == 1]

    def tile_of(p, unit):
        return tp * dp_count + place.behind(parts[p][0], unit, 1)

    def tile_over():
        return remote(
            tiles.at[pl.ds((1 - tp) * dp_count, dp_count)],
            far_tiles,
            tile_send.at[len(riding)],
            tile_recv.at[len(riding)],
            dp,
            1 - tp,
        )

    def tile_sending(i):
        p, stage, unit, _ = moves[i]
        n = riding.index(i)
        return remote(
            tiles.at[tile_of(p, unit)],
            tile_pieces.at[n],
            tile_send.at[n],
            tile_recv.at[n],
            place.along(parts[p][0][stage], 1),
            tp,
        )

    def tile_combine(item):
        at = tile_of(*item)
        total = tiles[at] + far_tiles[place.behind(parts[1][0], item[1], 1)]
        for j in inbound[item]:
            tile_sending(j).wait_recv()
            total = total + tile_pieces[riding.index(j)]
        tiles[at] = total

    plane = sizes[1] * sizes[2]
    peers = [
        (oy, ox, ot)
        for oy in range(sizes[1])
        for ox in range(sizes[2])
        for ot in range(2)
        if (oy, ox, ot) != (0, 0, 0)
    ]

    def peer(offsets, sign):
        oy, ox, ot = offsets
        return place.shifted((0, sign * oy, sign * ox)), (1 - tp if ot else tp)

    def plane_copy(k, sign):
        far_dp, far_tp = peer(peers[k], sign)
        region = full.at[tp, dp] if sign > 0 else full.at[far_tp, far_dp]
        return remote(region, region, hop_send.at[k], hop_recv.at[k], far_dp, far_tp)

    def line_copy(k, sign):
        n = len(peers) + k - 1
        far_dp = place.along(0, sign * k)
        held = dp if sign > 0 else far_dp
        region = full.at[:, pl.ds(held // plane * plane, plane)]
        return remote(region, region, hop_send.at[n], hop_recv.at[n], far_dp, tp)

    tiles[...] = jnp.zeros_like(tiles)
    for r in range(vec_ref.shape[0]):
        for i in range(chunks):
            tiles[r, i : i + 1, :] = vec_ref[r : r + 1, i * lanes : (i + 1) * lanes]
    barrier = pltpu.get_barrier_semaphore()
    for far_dp, far_tp in [peer(p, 1) for p in peers] + [
        (place.along(0, k), tp) for k in range(1, sizes[0])
    ]:
        pl.semaphore_signal(
            barrier, inc=1, device_id=(far_dp, far_tp), device_id_type=pl.DeviceIdType.MESH
        )
    pl.semaphore_wait(barrier, len(peers) + sizes[0] - 1)
    tile_over().start()
    for item in order_used:
        loading(item).start()
        passing(item).start()
    combined = set()
    tile_over().wait_recv()
    for i, (p, stage, unit, to) in enumerate(moves):
        item = (p, unit)
        if item not in combined:
            combined.add(item)
            loading(item).wait()
            passing(item).wait_recv()
            for j in inbound[item]:
                sending(j).wait_recv()
            combine(item, False)
            if p == 1:
                tile_combine(item)
        sending(i).start()
        if p == 1:
            tile_sending(i).start()
    half = block_out.shape[0] // 2

    def image_copy(n, ref, share):
        region = ref.at[pl.ds(share * half, half)]
        return remote(region, region, image_sems.at[2 * n], image_sems.at[2 * n + 1], dp, 1 - tp)

    for n, ref in enumerate((block_out, grad_out)):
        image_copy(n, ref, tp).start()
    for p in range(len(parts)):
        item = (p, (0, 0, 0))
        loading(item).wait()
        passing(item).wait_recv()
        for j in inbound[item]:
            sending(j).wait_recv()
        combine(item, True)
    slot_count = live_ref.shape[0]
    squares = jnp.zeros((1, lanes), F32)
    for n in range(slot_count):
        block = sum_ref[n * side : (n + 1) * side, :]
        square = jnp.sum(jnp.sum(block * block, axis=0, keepdims=True), axis=1, keepdims=True)
        squares = squares + jnp.where(live_ref[n, 0:1, :] > 0, square, 0.0)
    tile_combine((1, (0, 0, 0)))
    full[tp, dp] = tiles[tp * dp_count + dp]
    full[tp, dp, square_row : square_row + 1, :] = squares
    for k in range(len(peers)):
        plane_copy(k, 1).start()
    for k in range(len(peers)):
        plane_copy(k, -1).wait_recv()
    for k in range(1, sizes[0]):
        line_copy(k, 1).start()
    for k in range(1, sizes[0]):
        line_copy(k, -1).wait_recv()
    total = full[0, 0]
    for n in range(1, 2 * dp_count):
        total = total + full[n // dp_count, n % dp_count]
    squares = total[square_row : square_row + 1, :]
    for r in range(vec_ref.shape[0]):
        for i in range(chunks):
            vec_out[r : r + 1, i * lanes : (i + 1) * lanes] = full[r // dp_count, r % dp_count, i : i + 1, :]
    lane = lax.broadcasted_iota(jnp.int32, (1, lanes), 1)
    per_layer = vec_ref.shape[0] // layer_count
    for layer in range(layer_count):
        block = vec_out[layer * per_layer : (layer + 1) * per_layer, :]
        square = jnp.sum(jnp.sum(block * block, axis=0, keepdims=True), axis=1, keepdims=True)
        squares = squares + jnp.where(lane == layer, square, 0.0)
    square_out[...] = jnp.broadcast_to(squares, square_out.shape)
    for item in order_used:
        passing(item).wait_send()
    for i in range(len(moves)):
        sending(i).wait_send()
    tile_over().wait_send()
    for i in riding:
        tile_sending(i).wait_send()
    for k in range(len(peers)):
        plane_copy(k, 1).wait_send()
    for k in range(1, sizes[0]):
        line_copy(k, 1).wait_send()
    for n, ref in enumerate((block_out, grad_out)):
        image_copy(n, ref, tp).wait_send()
        image_copy(n, ref, 1 - tp).wait_recv()


def reduce_gradients(sizes, layer_count, slot_count, target, vectors, live_tile, block_own, grad_own):
    dp_count = sizes[0] * sizes[1] * sizes[2]
    side = target.shape[-1]
    rows = slot_count * side
    target = target.reshape(2, dp_count * rows, side)
    parts = part_table(sizes, rows)
    plan = gather_plan(sizes, parts)
    hops = 2 * sizes[1] * sizes[2] + sizes[0] - 2
    riding = sum(1 for p, _, _ in plan if p == 1)
    units = 3 * dp_count
    landing = sum(parts[p][2] for p, _, _ in plan)
    anyspace = pl.BlockSpec(memory_space=pl.ANY)
    vmem = pl.BlockSpec(memory_space=pltpu.VMEM)
    sd = jax.ShapeDtypeStruct
    dma = pltpu.SemaphoreType.DMA
    return pl.pallas_call(
        functools.partial(reduce_kernel, sizes, parts, plan, layer_count),
        in_specs=[anyspace, vmem, vmem, anyspace, anyspace],
        out_specs=[vmem, vmem, vmem, anyspace, anyspace],
        out_shape=[
            sd((rows, side), F32),
            sd(vectors.shape, F32),
            sd(live_tile.shape[1:], F32),
            sd(block_own.shape, F32),
            sd(block_own.shape, F32),
        ],
        scratch_shapes=[
            pltpu.VMEM((dp_count * rows, side), BF16),
            pltpu.VMEM((dp_count * rows, side), BF16),
            pltpu.VMEM((landing, side), BF16),
            pltpu.VMEM((2 * dp_count,) + live_tile.shape[1:], F32),
            pltpu.VMEM((dp_count,) + live_tile.shape[1:], F32),
            pltpu.VMEM((riding,) + live_tile.shape[1:], F32),
            pltpu.VMEM((2, dp_count) + live_tile.shape[1:], F32),
            dma((units,)),
            dma((units,)),
            dma((units,)),
            dma((len(plan),)),
            dma((len(plan),)),
            dma((riding + 1,)),
            dma((riding + 1,)),
            dma((hops,)),
            dma((hops,)),
            dma((4,)),
        ],
        input_output_aliases={3: 3, 4: 4},
        compiler_params=pltpu.CompilerParams(
            collective_id=1, has_side_effects=True, vmem_limit_bytes=VMEM_LIMIT
        ),
        name="reduce_gradients",
    )(target, vectors, live_tile, block_own, grad_own)


def plain_update(gradient, weight, first_state, second_state, step_rate):
    first_new = MOMENT_DECAY * first_state + (1.0 - MOMENT_DECAY) * gradient
    second_new = MOMENT_DECAY * second_state + (1.0 - MOMENT_DECAY) * gradient * gradient
    stepped = first_new / CORRECTION / (jnp.sqrt(second_new / CORRECTION) + ADAM_EPSILON)
    return (weight - step_rate * stepped, first_new, second_new)


def params():
    return pltpu.CompilerParams(vmem_limit_bytes=VMEM_LIMIT, dimension_semantics=("arbitrary",))


def weight_gradients(meta, left, right, width, slot_total, side, share_count):
    layer_count, count, rows, _ = left.shape
    tokens = count * rows
    ratio = left.shape[3] // width - 3
    block = (1, tokens, width)

    def left_map(s, meta):
        layer, _, at, _ = gradient_step(s, ratio)
        return (layer, 0, at)

    def right_map(s, meta):
        layer, _, _, at = gradient_step(s, ratio)
        return (layer, 0, at)

    grid = pltpu.PrefetchScalarGridSpec(
        num_scalar_prefetch=1,
        grid=(layer_count * (4 + 2 * ratio),),
        in_specs=[pl.BlockSpec(block, left_map), pl.BlockSpec(block, right_map)],
        out_specs=pl.BlockSpec(memory_space=pl.ANY),
        scratch_shapes=[
            pltpu.VMEM((width, tokens), BF16),
            pltpu.VMEM((2, width, width), BF16),
            pltpu.SemaphoreType.DMA((2,)),
        ],
    )
    return pl.pallas_call(
        functools.partial(gradient_kernel, width // side, ratio),
        grid_spec=grid,
        out_shape=jax.ShapeDtypeStruct((share_count, slot_total, side, side), BF16),
        compiler_params=params(),
        name="gradients",
    )(meta, left.reshape(layer_count, tokens, -1), right.reshape(layer_count, tokens, -1))


def adam(layer_count, step_rate, live, squares, gradient, weight, left, right, first, second):
    count, _, side, _ = weight.shape
    spec = pl.BlockSpec((1, 1, side, side), lambda i: (i, 0, 0, 0))
    smem = pl.BlockSpec(memory_space=pltpu.SMEM)
    out = jax.ShapeDtypeStruct(weight.shape, F32)
    return pl.pallas_call(
        functools.partial(adam_kernel, layer_count, step_rate),
        grid=(count,),
        in_specs=[smem, pl.BlockSpec(squares.shape, lambda i: (0, 0)), pl.BlockSpec((1, side, side), lambda i: (i, 0, 0))] + [spec] * 5,
        out_specs=[spec] * 3,
        out_shape=[out] * 3,
        compiler_params=params(),
        name="adam",
    )(live, squares, gradient, weight, left, right, first, second)


def shards(
    block_input,
    cotangent,
    mask_patches,
    owners,
    master_slots,
    left_bases,
    right_bases,
    first_moment,
    second_moment,
    shared_vectors,
    shared_first,
    shared_second,
    split_vectors,
    split_first,
    split_second,
):
    slot_count = master_slots.shape[0]
    side = master_slots.shape[-1]
    layer_count = shared_vectors.shape[0]
    width = shared_vectors.shape[2]
    half = split_vectors.shape[2]
    ratio = split_vectors.shape[1] - 2
    block_total = owners.shape[0]
    per_layer = block_total // layer_count
    image_total, seq = block_input.shape[:2]
    dp_count = lax.axis_size("dp")
    tp_count = lax.axis_size("tp")
    count = image_total // tp_count
    rows = round_up(seq, 16)
    keys = round_up(seq, 128)
    slot_total = dp_count * slot_count
    dp_rank = lax.axis_index("dp")
    tp_rank = lax.axis_index("tp")
    slot_index = positions(owners, slot_count)
    meta = jnp.concatenate([slot_index, tp_rank[None].astype(jnp.int32)])
    place = block_total

    sizes = line_sizes(dp_count)
    own = master_slots.reshape(slot_count * side, side)
    blocks, split_pair, stream, seed = gather_weights(
        sizes,
        own,
        split_vectors,
        block_input.transpose(1, 0, 2),
        cotangent.transpose(1, 0, 2),
        rows,
    )
    blocks = blocks.reshape(tp_count, slot_total, side, side)
    split_all = jnp.concatenate([split_pair[t] for t in range(tp_count)], axis=2)
    hits = mask_patches[:, None, :]

    left, right, output_own, grad_own, vectors = run_layers(
        count, seq, rows, keys, meta, place, stream, seed, hits, shared_vectors, split_all, blocks
    )
    target = weight_gradients(meta, left, right, width, slot_total, side, tp_count)
    mine_ids = dp_rank * slot_count + jnp.arange(slot_count, dtype=jnp.int32)
    matches = slot_index[None, :] == mine_ids[:, None]
    live = jnp.any(matches, axis=1)
    block_layer = jnp.arange(block_total, dtype=jnp.int32) // per_layer
    owned_layer = jnp.sum(jnp.where(matches, block_layer[None, :], 0), axis=1)
    lanes = lax.broadcasted_iota(jnp.int32, (slot_count, 8, 128), 2)
    live_tile = jnp.where((lanes == owned_layer[:, None, None]) & live[:, None, None], 1.0, 0.0)
    reduced, vector_sum, square_tile, block_output, input_grad = reduce_gradients(
        sizes, layer_count, slot_count, target, vectors.reshape(-1, width), live_tile, output_own, grad_own
    )

    reduced = reduced.reshape(slot_count, side, side)
    vector_sum = vector_sum.reshape(layer_count, -1, width)
    shared_sum = vector_sum[:, :6]
    split_full = vector_sum[:, 6 : 8 + ratio]
    split_sum = lax.dynamic_slice_in_dim(split_full, tp_rank * half, half, axis=2)
    squares = square_tile[0, :layer_count]
    layer_norms = jnp.sqrt(squares)
    global_norm = jnp.sqrt(jnp.sum(squares))
    factor = CLIP_NORM / jnp.maximum(global_norm, CLIP_NORM)
    step_rate = 0.5 / math.sqrt(width)
    new_master, new_first, new_second = adam(
        layer_count, step_rate, live.astype(jnp.int32), square_tile, reduced, master_slots, left_bases, right_bases,
        first_moment, second_moment,
    )
    new_shared, new_shared_first, new_shared_second = plain_update(
        shared_sum * factor, shared_vectors, shared_first, shared_second, VECTOR_RATE
    )
    new_split, new_split_first, new_split_second = plain_update(
        split_sum * factor, split_vectors, split_first, split_second, VECTOR_RATE
    )
    return (
        block_output,
        input_grad,
        new_master,
        new_first,
        new_second,
        new_shared,
        new_shared_first,
        new_shared_second,
        new_split,
        new_split_first,
        new_split_second,
        layer_norms,
        global_norm,
    )


def solution(mesh):
    sharded = P("dp", None, None)
    slots = P("dp", "tp", None, None)
    split = P(None, None, "tp")
    return jax.shard_map(
        shards,
        mesh=mesh,
        in_specs=(sharded, sharded, P("dp", None), P())
        + (slots,) * 5
        + (P(),) * 3
        + (split,) * 3,
        out_specs=(sharded, sharded) + (slots,) * 3 + (P(),) * 3 + (split,) * 3 + (P(), P()),
        check_vma=False,
    )
```

```python
import functools
import math

import jax
import jax.numpy as jnp
from jax import lax
from jax.experimental import pallas as pl
from jax.experimental.pallas import tpu as pltpu
from jax.sharding import PartitionSpec as P

DH = 64
GROUP = 4
LANES = GROUP * DH
CLIP_NORM = 1.0
MOMENT_DECAY = 0.5
CORRECTION = 0.9375
ADAM_EPSILON = 1e-08
WEIGHT_DECAY = 0.05
LAYER_EPSILON = 1e-06
VECTOR_RATE = 0.2
VMEM_LIMIT = 60 * 1024 * 1024
F32 = jnp.float32
BF16 = jnp.bfloat16


def nn(a, b):
    return lax.dot_general(a, b, (((1,), (0,)), ((), ())), preferred_element_type=F32)


def nt(a, b):
    return lax.dot_general(a, b, (((1,), (1,)), ((), ())), preferred_element_type=F32)


def tn(a, b):
    return lax.dot_general(a, b, (((0,), (0,)), ((), ())), preferred_element_type=F32)


def round_up(number, step):
    return (number + step - 1) // step * step


def positions(owners, slot_count):
    block_ids = jnp.arange(owners.shape[0], dtype=jnp.int32)
    same_owner = owners[None, :] == owners[:, None]
    earlier = block_ids[None, :] < block_ids[:, None]
    ranking = jnp.sum((same_owner & earlier).astype(jnp.int32), axis=1)
    return owners * slot_count + ranking


def normalized(v):
    center = jnp.mean(v, axis=-1, keepdims=True)
    spread = v - center
    second = jnp.mean(spread * spread, axis=-1, keepdims=True)
    inverse = lax.rsqrt(second + LAYER_EPSILON)
    return spread * inverse, inverse


def norm_back(grad, unit, inverse, gain):
    scaled = grad * gain
    first = jnp.mean(scaled, axis=-1, keepdims=True)
    second = jnp.mean(scaled * unit, axis=-1, keepdims=True)
    return inverse * (scaled - first - unit * second)


def gelu_pair(u):
    bell = jnp.exp(u * u * -0.5)
    mass = 0.5 + 0.5 * lax.erf(u * math.sqrt(0.5))
    return u * mass, mass + u * bell * (1.0 / math.sqrt(2.0 * math.pi))


def weight_copies(meta, layer, blocks, wp, wo, wu, wd, sems):
    side = blocks.shape[-1]
    width = wo.shape[0]
    pieces = width // side
    ratio = wd.shape[0] // width
    per_layer = pieces * (4 + 2 * ratio)
    base = layer * per_layer
    jobs = [[], [], [], []]

    def add(kind, target, b, row, col):
        for t in range(blocks.shape[0]):
            r, c = row(t), col(t)
            jobs[kind].append(
                pltpu.make_async_copy(
                    blocks.at[t, meta[base + b]],
                    target.at[pl.ds(r, side), pl.ds(c, side)],
                    sems.at[kind],
                )
            )

    for r in range(pieces):
        for p in range(3):
            add(0, wp, r * 3 + p, lambda t: r * side, lambda t: p * width + t * side)
    for c in range(pieces):
        add(1, wo, 3 * pieces + c, lambda t: t * side, lambda t: c * side)
    for r in range(pieces):
        for j in range(ratio):
            add(
                2, wu, 4 * pieces + r * ratio + j, lambda t: r * side, lambda t: j * width + t * side
            )
    for j in range(ratio):
        for c in range(pieces):
            add(
                3,
                wd,
                (4 + ratio) * pieces + j * pieces + c,
                lambda t: j * width + t * side,
                lambda t: c * side,
            )
    return jobs


def head_masks():
    lane = lax.broadcasted_iota(jnp.int32, (1, LANES), 1)
    return [(lane // DH) == h for h in range(GROUP)]


def spread_heads(masks, value):
    zero = jnp.zeros((), value.dtype)
    return jnp.concatenate([jnp.where(m, value, zero) for m in masks], axis=0)


def beside(stack, rows):
    return jnp.concatenate([stack[h * rows : (h + 1) * rows, :] for h in range(GROUP)], axis=1)


def saved_columns(width, ratio):
    left = (("a", 1), ("mixed", 1), ("c", 1), ("act", ratio))
    right = (("dqkv", 3), ("dhr", 1), ("du", ratio), ("dyr", 1))
    table = {}
    for side, names in enumerate((left, right)):
        start = 0
        for name, size in names:
            table[name] = (side, start * width, size * width)
            start += size
    return table, (3 + ratio) * width, (5 + ratio) * width


def layers_kernel(layer_count, seq, rows, keys, meta, x_ref, dy_ref, hits_ref, shared_ref, split_ref, blocks, *rest):
    outs = rest[:2]
    y_ref, dx_ref, vec_ref = rest[2:5]
    rest = rest[5:]
    saves = rest[: 2 * layer_count]
    rest = rest[2 * layer_count :]
    weights = [rest[4 * n : 4 * n + 4] for n in range(layer_count)]
    rest = rest[4 * layer_count :]
    holds = [rest[7 * n : 7 * n + 7] for n in range(layer_count)]
    save_sems, weight_sems = rest[7 * layer_count :]
    width = x_ref.shape[2]
    ratio = split_ref.shape[1] - 2
    groups = width // LANES
    scale = 1.0 / math.sqrt(DH)
    step = pl.program_id(0)
    zero = jnp.zeros((), BF16)
    masks = head_masks()

    columns, _, _ = saved_columns(width, ratio)

    def saving(layer, side, i):
        n = 2 * layer + side
        return pltpu.make_async_copy(saves[n], outs[side].at[layer, i], save_sems.at[n])

    def free(side):
        @pl.when(step > 0)
        def _():
            for n in range(layer_count):
                saving(n, side, step - 1).wait()

    def send(side):
        for n in range(layer_count):
            saving(n, side, step).start()

    def buffer(layer, name):
        side, start, size = columns[name]
        return saves[2 * layer + side].at[:, pl.ds(start, size)]

    jobs = [
        weight_copies(meta, n, blocks, *weights[n], weight_sems.at[n]) for n in range(layer_count)
    ]

    def start(pairs):
        @pl.when(step == 0)
        def _():
            for n, kind in pairs:
                for job in jobs[n][kind]:
                    job.start()

    def ready(pairs):
        @pl.when(step == 0)
        def _():
            for n, kind in pairs:
                target = weights[n][kind]
                pltpu.make_async_copy(target, target, weight_sems.at[n, kind]).wait()

    start([(0, 0)])

    @pl.when(step == 0)
    def _():
        vec_ref[...] = jnp.zeros_like(vec_ref)
        for hold in holds:
            for ref in (hold[3], hold[4]):
                ref[rows:keys, :] = jnp.zeros((keys - rows, width), BF16)

    free(0)
    holds[0][0][...] = x_ref[0].astype(F32)
    real = lax.broadcasted_iota(jnp.int32, (1, keys), 1) < seq
    for n in range(layer_count):
        xs, hs, qs, ks, vs, ps, ss = holds[n]
        wp, wo, wu, wd = weights[n]
        unit, _ = normalized(xs[...])
        a = (unit * shared_ref[n, 0:1, :] + shared_ref[n, 1:2, :]).astype(BF16)
        buffer(n, "a")[...] = a
        if n == 0:
            ready([(0, 0)])
            start([(0, 1), (0, 2), (0, 3)])
        qs[...] = ((nn(a, wp[:, 0:width]) + split_ref[n, 0:1, :]) * scale).astype(BF16)
        ks[0:rows, :] = nn(a, wp[:, width : 2 * width]).astype(BF16)
        vs[0:rows, :] = (nn(a, wp[:, 2 * width :]) + split_ref[n, 1:2, :]).astype(BF16)
        mixed = buffer(n, "mixed")
        for g in range(groups):
            cols = slice(g * LANES, (g + 1) * LANES)
            scores = nt(spread_heads(masks, qs[:, cols]), ks[:, cols])
            scores = jnp.where(real, scores, -1e30)
            top = jnp.max(scores, axis=-1, keepdims=True)
            power = jnp.exp(scores - top)
            total = jnp.sum(power, axis=-1, keepdims=True)
            probs = (power * (1.0 / total)).astype(BF16)
            ps[g * GROUP * rows : (g + 1) * GROUP * rows, :] = probs
            v4 = vs[:, cols]
            mix = nn(beside(probs, rows), spread_heads(masks, v4))
            mixed[:, cols] = mix.astype(BF16)
        if n == 0:
            ready([(0, 1), (0, 2), (0, 3)])
            start([(m, kind) for m in range(1, layer_count) for kind in range(4)])
        h = xs[...] + nn(mixed[...], wo[...]) + shared_ref[n, 2:3, :]
        hs[...] = h
        unit, _ = normalized(h)
        c = (unit * shared_ref[n, 3:4, :] + shared_ref[n, 4:5, :]).astype(BF16)
        buffer(n, "c")[...] = c
        y = h + shared_ref[n, 5:6, :]
        active = buffer(n, "act")
        for j in range(ratio):
            cols = slice(j * width, (j + 1) * width)
            u = nn(c, wu[:, cols]) + split_ref[n, 2 + j : 3 + j, :]
            act, slope = gelu_pair(u)
            act = act.astype(BF16)
            active[:, cols] = act
            ss[:, cols] = slope.astype(BF16)
            y = y + nn(act, wd[cols, :])
        if n + 1 < layer_count:
            holds[n + 1][0][...] = y
            ready([(n + 1, kind) for kind in range(4)])
        else:
            y_ref[0] = y[0:seq, :]

    send(0)
    free(1)
    wanted = lax.broadcasted_iota(jnp.int32, (rows, 1), 0)
    hit = jnp.max(jnp.where(hits_ref[0] + 1 == wanted, 1.0, 0.0), axis=-1, keepdims=True)
    dy = dy_ref[0] * hit
    for n in reversed(range(layer_count)):
        xs, hs, qs, ks, vs, ps, ss = holds[n]
        wp, wo, wu, wd = weights[n]

        def collect(row, value):
            vec_ref[n, row : row + 1, :] += jnp.sum(value, axis=0, keepdims=True)

        collect(5, dy)
        dyr = dy.astype(BF16)
        buffer(n, "dyr")[...] = dyr
        hidden = buffer(n, "du")
        dc = None
        for j in range(ratio):
            cols = slice(j * width, (j + 1) * width)
            du = (nt(dyr, wd[cols, :]) * ss[:, cols].astype(F32)).astype(BF16)
            hidden[:, cols] = du
            collect(8 + j, du.astype(F32))
            part = nt(du, wu[:, cols])
            dc = part if dc is None else dc + part
        unit, inverse = normalized(hs[...])
        collect(3, dc * unit)
        collect(4, dc)
        dh = dy + norm_back(dc, unit, inverse, shared_ref[n, 3:4, :])
        collect(2, dh)
        dhr = dh.astype(BF16)
        buffer(n, "dhr")[...] = dhr
        dmixed = nt(dhr, wo[...]).astype(BF16)
        back = buffer(n, "dqkv")
        for g in range(groups):
            cols = slice(g * LANES, (g + 1) * LANES)
            dm = spread_heads(masks, dmixed[:, cols])
            probs = ps[g * GROUP * rows : (g + 1) * GROUP * rows, :]
            k4 = ks[:, cols]
            dprobs = nt(dm, vs[:, cols])
            wide = probs.astype(F32)
            both = wide * dprobs
            ds = (both - wide * jnp.sum(both, axis=-1, keepdims=True)).astype(BF16)
            dv = tn(probs, dm)[0:rows, :].astype(BF16)
            dk = tn(ds, spread_heads(masks, qs[:, cols]))[0:rows, :].astype(BF16)
            dq = nn(beside(ds, rows), spread_heads(masks, k4))
            back[:, cols] = (dq.astype(BF16).astype(F32) * scale).astype(BF16)
            back[:, width + g * LANES : width + (g + 1) * LANES] = dk
            back[:, 2 * width + g * LANES : 2 * width + (g + 1) * LANES] = dv
        dqkv = back[...]
        collect(6, dqkv[:, 0:width].astype(F32))
        collect(7, dqkv[:, 2 * width :].astype(F32))
        da = nt(dqkv, wp[...])
        unit, inverse = normalized(xs[...])
        collect(0, da * unit)
        collect(1, da)
        dy = dh + norm_back(da, unit, inverse, shared_ref[n, 0:1, :])
    dx_ref[0] = dy[0:seq, :]
    send(1)

    @pl.when(step == pl.num_programs(0) - 1)
    def _():
        for n in range(layer_count):
            for side in range(2):
                saving(n, side, step).wait()


def run_layers(count, seq, rows, keys, meta, place, stream, seed, hits, shared, split, blocks):
    layer_count, _, width = shared.shape
    ratio = split.shape[1] - 2
    heads = width // DH
    sd = jax.ShapeDtypeStruct
    _, *widths = saved_columns(width, ratio)
    anyspace = pl.BlockSpec(memory_space=pl.ANY)
    outs = [sd((layer_count, count, rows, w), BF16) for w in widths]
    outs += [sd((2 * count, seq, width), F32)] * 2 + [sd((layer_count, 16, width), F32)]
    image = pl.BlockSpec((1, seq, width), lambda i, meta: (meta[place] * count + i, 0, 0))

    def shifted(shape):
        return pl.BlockSpec((1,) + tuple(shape[1:]), lambda i, meta: (meta[place] * count + i, 0, 0))

    def whole(shape):
        return pl.BlockSpec(tuple(shape), lambda i, meta: (0,) * len(shape))

    vmem = pltpu.VMEM
    scratch = [vmem((rows, w), BF16) for w in widths] * layer_count
    scratch += [
        vmem((width, 3 * width), BF16),
        vmem((width, width), BF16),
        vmem((width, ratio * width), BF16),
        vmem((ratio * width, width), BF16),
    ] * layer_count
    scratch += [
        vmem((rows, width), F32),
        vmem((rows, width), F32),
        vmem((rows, width), BF16),
        vmem((keys, width), BF16),
        vmem((keys, width), BF16),
        vmem((heads * rows, keys), BF16),
        vmem((rows, ratio * width), BF16),
    ] * layer_count
    scratch += [
        pltpu.SemaphoreType.DMA((2 * layer_count,)),
        pltpu.SemaphoreType.DMA((layer_count, 4)),
    ]
    grid = pltpu.PrefetchScalarGridSpec(
        num_scalar_prefetch=1,
        grid=(count,),
        in_specs=[
            pl.BlockSpec((1, rows, width), lambda i, meta: (i, 0, 0)),
            pl.BlockSpec((1, rows, width), lambda i, meta: (i, 0, 0)),
            shifted(hits.shape),
            whole(shared.shape),
            whole(split.shape),
            anyspace,
        ],
        out_specs=[anyspace] * len(widths) + [image, image, whole((layer_count, 16, width))],
        scratch_shapes=scratch,
    )
    res = pl.pallas_call(
        functools.partial(layers_kernel, layer_count, seq, rows, keys),
        grid_spec=grid,
        out_shape=outs,
        compiler_params=params(),
        name="layers",
    )(meta, stream, seed, hits, shared, split, blocks)
    return res


def gradient_step(s, ratio):
    left = jnp.where(s < 3, 0, jnp.where(s < 4, 1, jnp.where(s < 4 + ratio, 2, s - 1 - ratio)))
    return left, jnp.minimum(s, 4 + ratio)


def gradient_kernel(pieces, ratio, meta, left_ref, right_ref, out_ref, stage, sems):
    side = out_ref.shape[-1]
    step = pl.program_id(0)
    q = step
    layer_count = left_ref.shape[0]
    per_layer = pieces * (4 + 2 * ratio)
    slot = step % 2
    by_rows = (q == 3) | (q >= 4 + ratio)

    def block_of(i, j):
        return jnp.where(
            q < 3,
            i * 3 + q,
            jnp.where(
                q < 4,
                3 * pieces + j,
                jnp.where(
                    q < 4 + ratio,
                    4 * pieces + i * ratio + q - 4,
                    (4 + ratio) * pieces + (q - 4 - ratio) * pieces + j,
                ),
            ),
        )

    def drain(buffer):
        pltpu.make_async_copy(stage.at[buffer], stage.at[buffer], sems.at[buffer]).wait()

    @pl.when(step >= 2)
    def _():
        drain(slot)

    for n in range(layer_count):
        stage[slot, n] = tn(left_ref[n], right_ref[n]).astype(BF16)
    for n in range(layer_count):
        for i in range(pieces):
            for j in range(pieces):
                pltpu.make_async_copy(
                    stage.at[slot, n, pl.ds(i * side, side), pl.ds(j * side, side)],
                    out_ref.at[jnp.where(by_rows, i, j), meta[n * per_layer + block_of(i, j)]],
                    sems.at[slot],
                ).start()

    @pl.when(step == pl.num_programs(0) - 1)
    def _():
        drain(1 - slot)
        drain(slot)


def adam_kernel(layer_count, step_rate, live_ref, square_ref, g_ref, w_ref, l_ref, r_ref, m_ref, s_ref, w_out, m_out, s_out):
    lane = lax.broadcasted_iota(jnp.int32, (1, square_ref.shape[1]), 1)
    total = jnp.sum(jnp.where(lane < layer_count, square_ref[0:1, :], 0.0), axis=1, keepdims=True)
    factor = CLIP_NORM / jnp.maximum(jnp.sqrt(total), CLIP_NORM)
    slot = pl.program_id(0)
    alive = live_ref[slot] > 0
    weight = w_ref[0, 0]
    left = l_ref[0, 0].astype(BF16)
    right = r_ref[0, 0].astype(BF16)
    turned = nn(tn(left, g_ref[0].astype(BF16)).astype(BF16), right) * factor
    first = MOMENT_DECAY * m_ref[0, 0] + (1.0 - MOMENT_DECAY) * turned
    second = MOMENT_DECAY * s_ref[0, 0] + (1.0 - MOMENT_DECAY) * turned * turned
    stepped = first / CORRECTION / (jnp.sqrt(second / CORRECTION) + ADAM_EPSILON)
    back = nt(nn(left, stepped.astype(BF16)).astype(BF16), right)
    w_out[0, 0] = jnp.where(alive, weight - step_rate * (back + WEIGHT_DECAY * weight), weight)
    m_out[0, 0] = jnp.where(alive, first, m_ref[0, 0])
    s_out[0, 0] = jnp.where(alive, second, s_ref[0, 0])


def line_sizes(dp_count):
    if dp_count == 16:
        return (4, 2, 2)
    if dp_count == 64:
        return (4, 4, 4)
    return (dp_count, 1, 1)


def part_table(sizes, total_rows):
    step = 16
    if sizes[0] > sizes[1]:
        large = int(total_rows * 0.39) // step * step
        lengths = (total_rows - 2 * large, large, large)
        orders = ((2, 1, 0), (0, 1, 2), (0, 2, 1))
    else:
        small = total_rows // 3 // step * step
        lengths = (total_rows - 2 * small, small, small)
        orders = ((2, 1, 0), (0, 2, 1), (1, 0, 2))
    offsets = (0, lengths[0], lengths[0] + lengths[1])
    return [(orders[i], offsets[i], lengths[i]) for i in range(3)]


def gather_plan(sizes, parts):
    ready, moves, plan = {}, [], []
    free = [0.0] * 3
    for p, (order, _, _) in enumerate(parts):
        n = [sizes[d] for d in order]
        ready[(p, (0, 0, 0))] = 0.0
        for a in range(n[0]):
            if a + 1 < n[0]:
                moves.append((p, 0, (a, 0, 0)))
            for b in range(n[1]):
                if b + 1 < n[1]:
                    moves.append((p, 1, (a, b, 0)))
                for c in range(n[2] - 1):
                    moves.append((p, 2, (a, b, c)))
    while moves:
        choices = []
        for move in moves:
            p, stage, unit = move
            if (p, unit) in ready:
                start = max(ready[(p, unit)], free[parts[p][0][stage]])
                choices.append((start, stage, p, unit))
        start, stage, p, unit = min(choices)
        end = start + parts[p][2]
        free[parts[p][0][stage]] = end
        ready[(p, one_on(unit, stage))] = end + 60.0
        plan.append((p, stage, unit))
        moves.remove((p, stage, unit))
    return plan


def one_on(unit, stage):
    return tuple(v + (1 if i == stage else 0) for i, v in enumerate(unit))


class Place:
    def __init__(self, sizes):
        self.sizes = sizes
        self.dp = lax.axis_index("dp")
        self.tp = lax.axis_index("tp")
        nz, ny, nx = sizes
        self.at = (self.dp // (ny * nx), self.dp // nx % ny, self.dp % nx)

    def shifted(self, offsets):
        nz, ny, nx = self.sizes
        z, y, x = [
            lax.rem(self.at[d] + (offsets[d] + self.sizes[d]) % self.sizes[d], self.sizes[d])
            for d in range(3)
        ]
        return (z * ny + y) * nx + x

    def along(self, dim, step):
        return self.shifted(tuple(step if d == dim else 0 for d in range(3)))

    def behind(self, order, unit, sign):
        offsets = [0, 0, 0]
        for d, v in zip(order, unit):
            offsets[d] = sign * v
        return self.shifted(tuple(offsets))


def greet(place):
    barrier = pltpu.get_barrier_semaphore()
    number = 1
    pl.semaphore_signal(
        barrier, inc=1, device_id=(place.dp, 1 - place.tp), device_id_type=pl.DeviceIdType.MESH
    )
    for d in range(3):
        for step in range(1, place.sizes[d]):
            number += 1
            pl.semaphore_signal(
                barrier,
                inc=1,
                device_id=(place.along(d, step), place.tp),
                device_id_type=pl.DeviceIdType.MESH,
            )
    pl.semaphore_wait(barrier, number)


def remote(src, dst, send, recv, dp, tp):
    return pltpu.make_async_remote_copy(
        src_ref=src,
        dst_ref=dst,
        send_sem=send,
        recv_sem=recv,
        device_id=(dp, tp),
        device_id_type=pl.DeviceIdType.MESH,
    )


def gather_kernel(
    sizes, parts, plan, master_ref, split_ref, x_ref, seed_ref, out_ref, split_out, x_out, seed_out,
    own_ref, x_in, x_wide, seed_in, x_own, seed_own, send, recv, over_send, over_recv, here, stream_sems,
):
    place = Place(sizes)
    dp, tp = place.dp, place.tp
    rows = own_ref.shape[0]
    dims = [n for n in sizes]
    numbers = {}
    for p, (order, _, _) in enumerate(parts):
        for a in range(dims[order[0]]):
            for b in range(dims[order[1]]):
                for c in range(dims[order[2]]):
                    numbers[(p, (a, b, c))] = len(numbers)

    def region(p, unit, share):
        order, start, length = parts[p]
        owner = place.behind(order, unit, -1)
        return out_ref.at[share, pl.ds(pl.multiple_of(owner * rows + start, 16), length)]

    def source(p, unit):
        if unit == (0, 0, 0):
            return own_ref.at[pl.ds(parts[p][1], parts[p][2])]
        return region(p, unit, tp)

    def pass_over(p, unit):
        n = numbers[(p, unit)]
        return remote(
            source(p, unit), region(p, unit, tp), over_send.at[n], over_recv.at[n], dp, 1 - tp
        )

    def taken_over(p, unit):
        n = numbers[(p, unit)]
        piece = region(p, unit, 1 - tp)
        return remote(piece, piece, over_send.at[n], over_recv.at[n], dp, 1 - tp)

    def arriving(p, unit):
        n = numbers[(p, unit)]
        piece = region(p, unit, tp)
        return remote(piece, piece, send.at[n], recv.at[n], dp, 1 - tp)

    def sending(p, stage, unit):
        n = numbers[(p, one_on(unit, stage))]
        target = place.along(parts[p][0][stage], 1)
        return remote(source(p, unit), region(p, unit, tp), send.at[n], recv.at[n], target, tp)

    own_ref[...] = master_ref[...].astype(BF16)
    greet(place)
    started = []
    arrived = set()
    count, padded = x_own.shape[:2]
    images = 2 * count
    seq = x_in.shape[0] // images
    strips, _, lanes = x_wide.shape
    fetch = [pltpu.make_async_copy(x_ref, x_in, stream_sems.at[0])] + [
        pltpu.make_async_copy(
            seed_ref.at[:, pl.ds(n * lanes, lanes)], seed_in.at[n], stream_sems.at[4 + n]
        )
        for n in range(strips)
    ]
    leave = [
        pltpu.make_async_copy(x_own, x_out, stream_sems.at[2]),
        pltpu.make_async_copy(seed_own, seed_out, stream_sems.at[3]),
    ]
    tail = seq // 16 * 16

    def widen():
        fetch[0].wait()
        for n in range(strips):
            x_wide[n] = x_in[:, n * lanes : (n + 1) * lanes].astype(F32)

    def pick(source, target, i):
        def go():
            target[i, tail:padded, :] = jnp.zeros((padded - tail, target.shape[2]), target.dtype)
            for n in range(strips):
                rows_of = source[n, pl.ds(tp * count + i, seq, stride=images), :]
                target[i, 0:seq, n * lanes : (n + 1) * lanes] = rows_of.astype(target.dtype)

        return go

    def leaving(n):
        return lambda: leave[n].start()

    tasks = [lambda: [copy.start() for copy in fetch], widen]
    tasks += [pick(x_wide, x_own, i) for i in range(count)] + [leaving(0), lambda: [copy.wait() for copy in fetch[1:]]]
    tasks += [pick(seed_in, seed_own, i) for i in range(count)] + [leaving(1)]
    spacing = max(1, len(plan) // (len(tasks) + 1))

    def need(p, unit):
        if (p, unit) in arrived:
            return
        arrived.add((p, unit))
        if unit != (0, 0, 0):
            arriving(p, unit).wait_recv()
        late.append((p, unit))

    late = []
    for i, (p, stage, unit) in enumerate(plan):
        if (i + 1) % spacing == 0 and tasks:
            tasks.pop(0)()
        need(p, unit)
        move = sending(p, stage, unit)
        move.start()
        started.append(move)
        while late:
            item = late.pop()
            move = pass_over(*item)
            move.start()
            started.append(move)
    for task in tasks:
        task()
    vector = remote(split_ref, split_out.at[tp], here.at[1], here.at[2], dp, 1 - tp)
    vector.start()
    mine = pltpu.make_async_copy(
        own_ref, out_ref.at[tp, pl.ds(pl.multiple_of(dp * rows, 16), rows)], here.at[0]
    )
    mine.start()
    split_out[tp] = split_ref[...]
    for p, unit in numbers:
        need(p, unit)
        while late:
            item = late.pop()
            move = pass_over(*item)
            move.start()
            started.append(move)
    for p, unit in numbers:
        taken_over(p, unit).wait_recv()
    for move in started:
        move.wait_send()
    for copy in leave:
        copy.wait()
    remote(split_ref, split_out.at[1 - tp], here.at[1], here.at[2], dp, 1 - tp).wait()
    mine.wait()


def gather_weights(sizes, own, split, stream, seed, rows_padded):
    dp_count = sizes[0] * sizes[1] * sizes[2]
    rows, side = own.shape
    parts = part_table(sizes, rows)
    plan = gather_plan(sizes, parts)
    units = 3 * dp_count
    anyspace = pl.BlockSpec(memory_space=pl.ANY)
    vmem = pl.BlockSpec(memory_space=pltpu.VMEM)
    sd = jax.ShapeDtypeStruct
    tokens, images, width = stream.shape
    flat = (tokens * images, width)
    mine = (images // 2, rows_padded, width)
    dma = pltpu.SemaphoreType.DMA
    return pl.pallas_call(
        functools.partial(gather_kernel, sizes, parts, plan),
        in_specs=[vmem, vmem, anyspace, anyspace],
        out_specs=[anyspace, vmem, anyspace, anyspace],
        out_shape=[
            sd((2, dp_count * rows, side), BF16),
            sd((2,) + split.shape, split.dtype),
            sd(mine, BF16),
            sd(mine, F32),
        ],
        scratch_shapes=[
            pltpu.VMEM((rows, side), BF16),
            pltpu.VMEM(flat, BF16),
            pltpu.VMEM((width // 128, tokens * images, 128), F32),
            pltpu.VMEM((width // 128, tokens * images, 128), F32),
            pltpu.VMEM(mine, BF16),
            pltpu.VMEM(mine, F32),
            dma((units,)),
            dma((units,)),
            dma((units,)),
            dma((units,)),
            dma((3,)),
            dma((4 + width // 128,)),
        ],
        compiler_params=pltpu.CompilerParams(
            collective_id=0, has_side_effects=True, vmem_limit_bytes=VMEM_LIMIT
        ),
        name="gather_weights",
    )(own, split, stream.reshape(flat), seed.reshape(flat))


def reduce_kernel(
    sizes, parts, plan, layer_count, target_ref, vec_ref, live_ref, block_ref, grad_ref,
    sum_ref, vec_out, square_out, block_out, grad_out,
    own, other, pieces, tiles, far_tiles, tile_pieces, full,
    load, over_send, over_recv, send, recv, tile_send, tile_recv, hop_send, hop_recv, image_sems,
):
    place = Place(sizes)
    dp, tp = place.dp, place.tp
    rows, side = sum_ref.shape
    moves = [(p, stage, one_on(unit, stage), unit) for p, stage, unit in reversed(plan)]
    order_used = []
    for p, stage, unit, _ in moves:
        if (p, unit) not in order_used:
            order_used.append((p, unit))
    for p in range(len(parts)):
        order_used.append((p, (0, 0, 0)))
    numbers = {item: i for i, item in enumerate(order_used)}
    landing = {}
    offset = 0
    inbound = {item: [] for item in order_used}
    for i, (p, stage, unit, to) in enumerate(moves):
        landing[i] = (offset, parts[p][2])
        offset += parts[p][2]
        inbound[(p, to)].append(i)

    def row_range(p, unit):
        order, start, length = parts[p]
        owner = place.behind(order, unit, 1)
        return pl.ds(pl.multiple_of(owner * rows + start, 16), length)

    def loading(item):
        span = row_range(*item)
        n = numbers[item]
        return pltpu.make_async_copy(target_ref.at[tp, span], own.at[span], load.at[n])

    def passing(item):
        span = row_range(*item)
        n = numbers[item]
        return remote(
            target_ref.at[1 - tp, span], other.at[span], over_send.at[n], over_recv.at[n], dp, 1 - tp
        )

    def sending(i):
        p, stage, unit, _ = moves[i]
        start, length = landing[i]
        return remote(
            own.at[row_range(p, unit)],
            pieces.at[pl.ds(start, length)],
            send.at[i],
            recv.at[i],
            place.along(parts[p][0][stage], 1),
            tp,
        )

    def combine(item, final):
        p, unit = item
        order, start, length = parts[p]
        owner = place.behind(order, unit, 1)
        base = owner * rows + start
        froms = [landing[i][0] for i in inbound[item]]
        step = math.gcd(length, 64)

        def body(k, carry):
            at = pl.ds(pl.multiple_of(base + k * step, 16), step)
            total = own[at, :].astype(F32) + other[at, :].astype(F32)
            for place_from in froms:
                got = pieces[pl.ds(pl.multiple_of(place_from + k * step, 16), step), :]
                total = total + got.astype(F32)
            if final:
                sum_ref[pl.ds(pl.multiple_of(start + k * step, 16), step), :] = total
            else:
                own[at, :] = total.astype(BF16)
            return carry

        lax.fori_loop(0, length // step, body, 0)

    dp_count = sizes[0] * sizes[1] * sizes[2]
    lanes = tiles.shape[2]
    chunks = vec_ref.shape[1] // lanes
    square_row = chunks
    riding = [i for i in range(len(moves)) if moves[i][0] == 1]

    def tile_of(p, unit):
        return tp * dp_count + place.behind(parts[p][0], unit, 1)

    def tile_over():
        return remote(
            tiles.at[pl.ds((1 - tp) * dp_count, dp_count)],
            far_tiles,
            tile_send.at[len(riding)],
            tile_recv.at[len(riding)],
            dp,
            1 - tp,
        )

    def tile_sending(i):
        p, stage, unit, _ = moves[i]
        n = riding.index(i)
        return remote(
            tiles.at[tile_of(p, unit)],
            tile_pieces.at[n],
            tile_send.at[n],
            tile_recv.at[n],
            place.along(parts[p][0][stage], 1),
            tp,
        )

    def tile_combine(item):
        at = tile_of(*item)
        total = tiles[at] + far_tiles[place.behind(parts[1][0], item[1], 1)]
        for j in inbound[item]:
            tile_sending(j).wait_recv()
            total = total + tile_pieces[riding.index(j)]
        tiles[at] = total

    plane = sizes[1] * sizes[2]
    peers = [
        (oy, ox, ot)
        for oy in range(sizes[1])
        for ox in range(sizes[2])
        for ot in range(2)
        if (oy, ox, ot) != (0, 0, 0)
    ]

    def peer(offsets, sign):
        oy, ox, ot = offsets
        return place.shifted((0, sign * oy, sign * ox)), (1 - tp if ot else tp)

    def plane_copy(k, sign):
        far_dp, far_tp = peer(peers[k], sign)
        region = full.at[tp, dp] if sign > 0 else full.at[far_tp, far_dp]
        return remote(region, region, hop_send.at[k], hop_recv.at[k], far_dp, far_tp)

    def line_copy(k, sign):
        n = len(peers) + k - 1
        far_dp = place.along(0, sign * k)
        held = dp if sign > 0 else far_dp
        region = full.at[:, pl.ds(held // plane * plane, plane)]
        return remote(region, region, hop_send.at[n], hop_recv.at[n], far_dp, tp)

    tiles[...] = jnp.zeros_like(tiles)
    for r in range(vec_ref.shape[0]):
        for i in range(chunks):
            tiles[r, i : i + 1, :] = vec_ref[r : r + 1, i * lanes : (i + 1) * lanes]
    barrier = pltpu.get_barrier_semaphore()
    for far_dp, far_tp in [peer(p, 1) for p in peers] + [
        (place.along(0, k), tp) for k in range(1, sizes[0])
    ]:
        pl.semaphore_signal(
            barrier, inc=1, device_id=(far_dp, far_tp), device_id_type=pl.DeviceIdType.MESH
        )
    pl.semaphore_wait(barrier, len(peers) + sizes[0] - 1)
    tile_over().start()
    for item in order_used:
        loading(item).start()
        passing(item).start()
    combined = set()
    tile_over().wait_recv()
    for i, (p, stage, unit, to) in enumerate(moves):
        item = (p, unit)
        if item not in combined:
            combined.add(item)
            loading(item).wait()
            passing(item).wait_recv()
            for j in inbound[item]:
                sending(j).wait_recv()
            combine(item, False)
            if p == 1:
                tile_combine(item)
        sending(i).start()
        if p == 1:
            tile_sending(i).start()
    half = block_out.shape[0] // 2

    def image_copy(n, ref, share):
        region = ref.at[pl.ds(share * half, half)]
        return remote(region, region, image_sems.at[2 * n], image_sems.at[2 * n + 1], dp, 1 - tp)

    for n, ref in enumerate((block_out, grad_out)):
        image_copy(n, ref, tp).start()
    for p in range(len(parts)):
        item = (p, (0, 0, 0))
        loading(item).wait()
        passing(item).wait_recv()
        for j in inbound[item]:
            sending(j).wait_recv()
        combine(item, True)
    slot_count = live_ref.shape[0]
    squares = jnp.zeros((1, lanes), F32)
    for n in range(slot_count):
        block = sum_ref[n * side : (n + 1) * side, :]
        square = jnp.sum(jnp.sum(block * block, axis=0, keepdims=True), axis=1, keepdims=True)
        squares = squares + jnp.where(live_ref[n, 0:1, :] > 0, square, 0.0)
    tile_combine((1, (0, 0, 0)))
    full[tp, dp] = tiles[tp * dp_count + dp]
    full[tp, dp, square_row : square_row + 1, :] = squares
    for k in range(len(peers)):
        plane_copy(k, 1).start()
    for k in range(len(peers)):
        plane_copy(k, -1).wait_recv()
    for k in range(1, sizes[0]):
        line_copy(k, 1).start()
    for k in range(1, sizes[0]):
        line_copy(k, -1).wait_recv()
    total = full[0, 0]
    for n in range(1, 2 * dp_count):
        total = total + full[n // dp_count, n % dp_count]
    squares = total[square_row : square_row + 1, :]
    for r in range(vec_ref.shape[0]):
        for i in range(chunks):
            vec_out[r : r + 1, i * lanes : (i + 1) * lanes] = full[r // dp_count, r % dp_count, i : i + 1, :]
    lane = lax.broadcasted_iota(jnp.int32, (1, lanes), 1)
    per_layer = vec_ref.shape[0] // layer_count
    for layer in range(layer_count):
        block = vec_out[layer * per_layer : (layer + 1) * per_layer, :]
        square = jnp.sum(jnp.sum(block * block, axis=0, keepdims=True), axis=1, keepdims=True)
        squares = squares + jnp.where(lane == layer, square, 0.0)
    square_out[...] = jnp.broadcast_to(squares, square_out.shape)
    for item in order_used:
        passing(item).wait_send()
    for i in range(len(moves)):
        sending(i).wait_send()
    tile_over().wait_send()
    for i in riding:
        tile_sending(i).wait_send()
    for k in range(len(peers)):
        plane_copy(k, 1).wait_send()
    for k in range(1, sizes[0]):
        line_copy(k, 1).wait_send()
    for n, ref in enumerate((block_out, grad_out)):
        image_copy(n, ref, tp).wait_send()
        image_copy(n, ref, 1 - tp).wait_recv()


def reduce_gradients(sizes, layer_count, slot_count, target, vectors, live_tile, block_own, grad_own):
    dp_count = sizes[0] * sizes[1] * sizes[2]
    side = target.shape[-1]
    rows = slot_count * side
    target = target.reshape(2, dp_count * rows, side)
    parts = part_table(sizes, rows)
    plan = gather_plan(sizes, parts)
    hops = 2 * sizes[1] * sizes[2] + sizes[0] - 2
    riding = sum(1 for p, _, _ in plan if p == 1)
    units = 3 * dp_count
    landing = sum(parts[p][2] for p, _, _ in plan)
    anyspace = pl.BlockSpec(memory_space=pl.ANY)
    vmem = pl.BlockSpec(memory_space=pltpu.VMEM)
    sd = jax.ShapeDtypeStruct
    dma = pltpu.SemaphoreType.DMA
    return pl.pallas_call(
        functools.partial(reduce_kernel, sizes, parts, plan, layer_count),
        in_specs=[anyspace, vmem, vmem, anyspace, anyspace],
        out_specs=[vmem, vmem, vmem, anyspace, anyspace],
        out_shape=[
            sd((rows, side), F32),
            sd(vectors.shape, F32),
            sd(live_tile.shape[1:], F32),
            sd(block_own.shape, F32),
            sd(block_own.shape, F32),
        ],
        scratch_shapes=[
            pltpu.VMEM((dp_count * rows, side), BF16),
            pltpu.VMEM((dp_count * rows, side), BF16),
            pltpu.VMEM((landing, side), BF16),
            pltpu.VMEM((2 * dp_count,) + live_tile.shape[1:], F32),
            pltpu.VMEM((dp_count,) + live_tile.shape[1:], F32),
            pltpu.VMEM((riding,) + live_tile.shape[1:], F32),
            pltpu.VMEM((2, dp_count) + live_tile.shape[1:], F32),
            dma((units,)),
            dma((units,)),
            dma((units,)),
            dma((len(plan),)),
            dma((len(plan),)),
            dma((riding + 1,)),
            dma((riding + 1,)),
            dma((hops,)),
            dma((hops,)),
            dma((4,)),
        ],
        input_output_aliases={3: 3, 4: 4},
        compiler_params=pltpu.CompilerParams(
            collective_id=1, has_side_effects=True, vmem_limit_bytes=VMEM_LIMIT
        ),
        name="reduce_gradients",
    )(target, vectors, live_tile, block_own, grad_own)


def plain_update(gradient, weight, first_state, second_state, step_rate):
    first_new = MOMENT_DECAY * first_state + (1.0 - MOMENT_DECAY) * gradient
    second_new = MOMENT_DECAY * second_state + (1.0 - MOMENT_DECAY) * gradient * gradient
    stepped = first_new / CORRECTION / (jnp.sqrt(second_new / CORRECTION) + ADAM_EPSILON)
    return (weight - step_rate * stepped, first_new, second_new)


def params():
    return pltpu.CompilerParams(vmem_limit_bytes=VMEM_LIMIT, dimension_semantics=("arbitrary",))


def weight_gradients(meta, left, right, width, slot_total, side, share_count):
    layer_count, count, rows, _ = left.shape
    tokens = count * rows
    ratio = left.shape[3] // width - 3
    block = (layer_count, tokens, width)

    def left_map(s, meta):
        return (0, 0, gradient_step(s, ratio)[0])

    def right_map(s, meta):
        return (0, 0, gradient_step(s, ratio)[1])

    grid = pltpu.PrefetchScalarGridSpec(
        num_scalar_prefetch=1,
        grid=(4 + 2 * ratio,),
        in_specs=[pl.BlockSpec(block, left_map), pl.BlockSpec(block, right_map)],
        out_specs=pl.BlockSpec(memory_space=pl.ANY),
        scratch_shapes=[
            pltpu.VMEM((2, layer_count, width, width), BF16),
            pltpu.SemaphoreType.DMA((2,)),
        ],
    )
    return pl.pallas_call(
        functools.partial(gradient_kernel, width // side, ratio),
        grid_spec=grid,
        out_shape=jax.ShapeDtypeStruct((share_count, slot_total, side, side), BF16),
        compiler_params=params(),
        name="gradients",
    )(meta, left.reshape(layer_count, tokens, -1), right.reshape(layer_count, tokens, -1))


def adam(layer_count, step_rate, live, squares, gradient, weight, left, right, first, second):
    count, _, side, _ = weight.shape
    spec = pl.BlockSpec((1, 1, side, side), lambda i: (i, 0, 0, 0))
    smem = pl.BlockSpec(memory_space=pltpu.SMEM)
    out = jax.ShapeDtypeStruct(weight.shape, F32)
    return pl.pallas_call(
        functools.partial(adam_kernel, layer_count, step_rate),
        grid=(count,),
        in_specs=[smem, pl.BlockSpec(squares.shape, lambda i: (0, 0)), pl.BlockSpec((1, side, side), lambda i: (i, 0, 0))] + [spec] * 5,
        out_specs=[spec] * 3,
        out_shape=[out] * 3,
        compiler_params=params(),
        name="adam",
    )(live, squares, gradient, weight, left, right, first, second)


def shards(
    block_input,
    cotangent,
    mask_patches,
    owners,
    master_slots,
    left_bases,
    right_bases,
    first_moment,
    second_moment,
    shared_vectors,
    shared_first,
    shared_second,
    split_vectors,
    split_first,
    split_second,
):
    slot_count = master_slots.shape[0]
    side = master_slots.shape[-1]
    layer_count = shared_vectors.shape[0]
    width = shared_vectors.shape[2]
    half = split_vectors.shape[2]
    ratio = split_vectors.shape[1] - 2
    block_total = owners.shape[0]
    per_layer = block_total // layer_count
    image_total, seq = block_input.shape[:2]
    dp_count = lax.axis_size("dp")
    tp_count = lax.axis_size("tp")
    count = image_total // tp_count
    rows = round_up(seq, 16)
    keys = round_up(seq, 128)
    slot_total = dp_count * slot_count
    dp_rank = lax.axis_index("dp")
    tp_rank = lax.axis_index("tp")
    slot_index = positions(owners, slot_count)
    meta = jnp.concatenate([slot_index, tp_rank[None].astype(jnp.int32)])
    place = block_total

    sizes = line_sizes(dp_count)
    own = master_slots.reshape(slot_count * side, side)
    blocks, split_pair, stream, seed = gather_weights(
        sizes,
        own,
        split_vectors,
        block_input.transpose(1, 0, 2),
        cotangent.transpose(1, 0, 2),
        rows,
    )
    blocks = blocks.reshape(tp_count, slot_total, side, side)
    split_all = jnp.concatenate([split_pair[t] for t in range(tp_count)], axis=2)
    hits = mask_patches[:, None, :]

    left, right, output_own, grad_own, vectors = run_layers(
        count, seq, rows, keys, meta, place, stream, seed, hits, shared_vectors, split_all, blocks
    )
    target = weight_gradients(meta, left, right, width, slot_total, side, tp_count)
    mine_ids = dp_rank * slot_count + jnp.arange(slot_count, dtype=jnp.int32)
    matches = slot_index[None, :] == mine_ids[:, None]
    live = jnp.any(matches, axis=1)
    block_layer = jnp.arange(block_total, dtype=jnp.int32) // per_layer
    owned_layer = jnp.sum(jnp.where(matches, block_layer[None, :], 0), axis=1)
    lanes = lax.broadcasted_iota(jnp.int32, (slot_count, 8, 128), 2)
    live_tile = jnp.where((lanes == owned_layer[:, None, None]) & live[:, None, None], 1.0, 0.0)
    reduced, vector_sum, square_tile, block_output, input_grad = reduce_gradients(
        sizes, layer_count, slot_count, target, vectors.reshape(-1, width), live_tile, output_own, grad_own
    )

    reduced = reduced.reshape(slot_count, side, side)
    vector_sum = vector_sum.reshape(layer_count, -1, width)
    shared_sum = vector_sum[:, :6]
    split_full = vector_sum[:, 6 : 8 + ratio]
    split_sum = lax.dynamic_slice_in_dim(split_full, tp_rank * half, half, axis=2)
    squares = square_tile[0, :layer_count]
    layer_norms = jnp.sqrt(squares)
    global_norm = jnp.sqrt(jnp.sum(squares))
    factor = CLIP_NORM / jnp.maximum(global_norm, CLIP_NORM)
    step_rate = 0.5 / math.sqrt(width)
    new_master, new_first, new_second = adam(
        layer_count, step_rate, live.astype(jnp.int32), square_tile, reduced, master_slots, left_bases, right_bases,
        first_moment, second_moment,
    )
    new_shared, new_shared_first, new_shared_second = plain_update(
        shared_sum * factor, shared_vectors, shared_first, shared_second, VECTOR_RATE
    )
    new_split, new_split_first, new_split_second = plain_update(
        split_sum * factor, split_vectors, split_first, split_second, VECTOR_RATE
    )
    return (
        block_output,
        input_grad,
        new_master,
        new_first,
        new_second,
        new_shared,
        new_shared_first,
        new_shared_second,
        new_split,
        new_split_first,
        new_split_second,
        layer_norms,
        global_norm,
    )


def solution(mesh):
    sharded = P("dp", None, None)
    slots = P("dp", "tp", None, None)
    split = P(None, None, "tp")
    return jax.shard_map(
        shards,
        mesh=mesh,
        in_specs=(sharded, sharded, P("dp", None), P())
        + (slots,) * 5
        + (P(),) * 3
        + (split,) * 3,
        out_specs=(sharded, sharded) + (slots,) * 3 + (P(),) * 3 + (split,) * 3 + (P(), P()),
        check_vma=False,
    )
```
